32 devices in a mesh: groups: 2 (over x), tensor: 16 (over z, y, core).
Axes of the slice: x: 2, y: 2, z: 4, core: 2. Of those that a mesh axis runs over, the one named last changes fastest.
Arguments:
- input_rows: bfloat16 [512, 8192], P(('groups', 'tensor')), parts along dimension 0, may hold values from -6 to 6
- up_weight: bfloat16 [8192, 28672], P(None, 'tensor'), may hold values from -0.0625 to 0.0625
- adapter_down: bfloat16 [32, 64, 8192], P(('groups', 'tensor')), parts along dimension 0, may hold values from -0.0625 to 0.0625
- adapter_up: bfloat16 [32, 64, 28672], P(('groups', 'tensor')), parts along dimension 0, may hold values from -0.75 to 0.75
- ranks: int32 [32], P('groups'), parts along dimension 0, may hold values from 16 to 64, as said below
- adapter_slot: int32 [32], P('groups'), parts along dimension 0, may hold values from 0 to 15, each once
- segment_lengths: int32 [32], P('groups'), parts along dimension 0, may hold values from 1 to 64, 256 in all
- segment_adapter: int32 [32], P('groups'), parts along dimension 0, may hold values from 0 to 15
Outputs:
- up_out: bfloat16 [512, 28672], P('groups', 'tensor'), parts along dimension 0
The draws below stay inside these ranges and needn't reach their ends.
There are 2 independent parts, one for each index of `groups`. The reference program is written for one: setup_inputs(seed, part) draws one part's arguments, and reference() takes and returns one part's arrays. A program takes and returns all parts, laid end to end along the dimension named above; an argument that names none is the same for every part. Nothing has to cross between parts.
Inputs may be any that keep to these rules, and one draw needn't show every extreme that they name: `ranks`: a multiple of 16; the columns j >= the rank of an adapter's 64 are unused. `adapter_slot`: each storage slot holds exactly one adapter. `segment_lengths`: the segments sum to 256.
All inputs are finite; a program needn't handle non-finite values.
Results may differ from the reference program's by a relative error of at most 0.0039.
Values may be sent and summed in bfloat16 or wider, within the bound.
No kernel may reach another device: no remote copies, remote signals or barrier semaphores. Data moves between devices by JAX's collectives and lax.ppermute only.
A program may use at most 128 MiB of HBM per device.

```python
import math
import jax
import jax.numpy as jnp
import numpy as np
from jax import lax

MODEL_WIDTH = 8192
HIDDEN_UNITS = 28672
RANK_BLOCK = 64
ROWS = 256
ADAPTER_COUNT = 16
SEGS = 16
MOST_SEG = 64


def draw_ranks(key, part):
    key = jax.random.fold_in(key, 11)
    first, second, third = jax.random.split(key, 3)
    levels = 16 * jax.random.randint(first, (ADAPTER_COUNT,), 1, 5)
    highest = jax.random.randint(second, (), 0, ADAPTER_COUNT)
    lowest = (highest + 1 + jax.random.randint(third, (), 0, ADAPTER_COUNT - 1)) % ADAPTER_COUNT
    levels = levels.at[highest].set(64).at[lowest].set(16)
    return levels.astype(jnp.int32)


def place_ends(entries, key, least, largest):
    longest = entries.shape.index(max(entries.shape))
    spots = []
    for shift in (0, 1):
        where = [jax.random.randint(jax.random.fold_in(key, axis), (), 0, length) for axis, length in enumerate(entries.shape)]
        where[longest] = (where[longest] + shift) % entries.shape[longest]
        spots.append(tuple(where))
    return entries.at[spots[0]].set(least).at[spots[1]].set(largest)


def block_scale(stream_key, shape, cuts, smallest, high):
    level, own = 1.0, jax.random.fold_in(stream_key, 6)
    for dim, parts in cuts:
        draws = jnp.exp(jax.random.uniform(jax.random.fold_in(own, dim), (parts,), jnp.float32, smallest / len(cuts), high / len(cuts)))
        level = level * jnp.repeat(draws, shape[dim] // parts).reshape([-1 if axis == dim else 1 for axis in range(len(shape))])
    return level


def cumulative_ranks(amount, slope):
    portions = [(1 << 20) // math.isqrt(grade ** slope) + 1 for grade in range(1, amount + 1)]
    width = 1 + sum(portions) // (1 << 30)
    return np.cumsum(np.array([max(1, weight // width) for weight in portions]))


def ranked_ids(own_key, shape, amount, skew):
    grid = cumulative_ranks(amount, skew)
    pick = jax.random.randint(jax.random.fold_in(own_key, 1), shape, 0, int(grid[amount - 1]))
    grade = jnp.searchsorted(jnp.asarray(grid, jnp.int32), pick, side="right")
    return jax.random.permutation(jax.random.fold_in(own_key, 2), amount)[grade].astype(jnp.int32)


def profile(count, total, most, skew):
    loads = [(1 << 20) // math.isqrt(grade ** skew) + 1 for grade in range(2, count + 1)]
    surplus, given = total - most - (count - 1), [1] * (count - 1)
    while surplus > 0:
        free = [i for i in range(count - 1) if given[i] < most]
        mass, remaining = sum([loads[i] for i in free]), surplus
        for i in free:
            addition = min(most - given[i], max(1, remaining * loads[i] // mass), surplus)
            given[i] = given[i] + addition
            surplus = surplus - addition
    return np.array([most] + given)


def uneven_parts(key, amount, total, limit, lean):
    if amount == 2:
        one = jax.random.randint(key, (), max(1, total - limit), min(limit, total - 1) + 1)
        return jnp.stack([one, total - one])
    tallies = jnp.asarray(profile(amount, total, limit, lean), jnp.int32)
    pairs = (amount - 1) // 2
    giver, receiver = tallies[1:1 + 2 * pairs:2], tallies[2:2 + 2 * pairs:2]
    margin = jnp.minimum(giver - 1, limit - receiver)
    passed = jax.random.randint(jax.random.fold_in(key, 1), (pairs,), 0, 1 << 20) % (margin + 1)
    tallies = tallies.at[1:1 + 2 * pairs:2].set(giver - passed).at[2:2 + 2 * pairs:2].set(receiver + passed)
    return tallies[jax.random.permutation(jax.random.fold_in(key, 2), amount)]


def scatter_about(rng, dims, scale, most, pieces=(), kind=jnp.bfloat16):
    values = scale * jax.random.normal(rng, dims, jnp.float32)
    if pieces:
        values = values * block_scale(rng, dims, pieces, -0.22, 0.18)
    return jnp.clip(values, -most, most).astype(kind)


def setup_inputs(seed: int = 0, part: int = 0) -> dict:
    keys = jax.random.split(jax.random.key(seed), 9)
    part_keys = jax.random.split(jax.random.fold_in(keys[8], part), 9)
    input_rows = scatter_about(part_keys[0], (ROWS, MODEL_WIDTH), 1.0, 6.0, ((0, 16),))
    up_weight = scatter_about(keys[1], (MODEL_WIDTH, HIDDEN_UNITS), MODEL_WIDTH ** -0.5, 0.0625, ((1, 16),))
    adapter_down = scatter_about(part_keys[2], (ADAPTER_COUNT, RANK_BLOCK, MODEL_WIDTH), MODEL_WIDTH ** -0.5, 0.0625, ((0, 16),))
    adapter_up = scatter_about(part_keys[3], (ADAPTER_COUNT, RANK_BLOCK, HIDDEN_UNITS), RANK_BLOCK ** -0.5, 0.75, ((0, 16),))
    ranks = draw_ranks(jax.random.fold_in(jax.random.fold_in(keys[8], part), 71), part)
    adapter_slot = jax.random.permutation(part_keys[5], ADAPTER_COUNT).astype(jnp.int32)
    segment_lengths = uneven_parts(part_keys[6], SEGS, ROWS, MOST_SEG, 2).astype(jnp.int32)
    segment_adapter = place_ends(ranked_ids(part_keys[7], (SEGS,), ADAPTER_COUNT, 2), jax.random.fold_in(part_keys[7], 3), 0, ADAPTER_COUNT - 1).astype(jnp.int32)
    return dict(input_rows=input_rows, up_weight=up_weight, adapter_down=adapter_down, adapter_up=adapter_up, ranks=ranks, adapter_slot=adapter_slot, segment_lengths=segment_lengths, segment_adapter=segment_adapter)


ADAPTER_ALPHA = 32.0


def row_tables(row_count, ranks, adapter_slot, segment_lengths, segment_adapter):
    seg_ends = jnp.cumsum(segment_lengths).astype(jnp.int32)
    positions = jnp.arange(row_count, dtype=jnp.int32)
    seg_row = jnp.sum((seg_ends[None, :] <= positions[:, None]).astype(jnp.int32), axis=1)
    seg_pick = (seg_row[:, None] == jnp.arange(segment_lengths.shape[0], dtype=jnp.int32)[None, :]).astype(jnp.int32)
    adapter_row = jnp.sum(seg_pick * segment_adapter[None, :], axis=1)
    pool_pick = (adapter_row[:, None] == jnp.arange(ranks.shape[0], dtype=jnp.int32)[None, :]).astype(jnp.int32)
    slot_row = jnp.sum(pool_pick * adapter_slot[None, :], axis=1)
    row_rank_values = jnp.sum(pool_pick * ranks[None, :], axis=1)
    return slot_row, row_rank_values


def coefficients(shrink, row_rank_values):
    columns = jnp.arange(shrink.shape[1], dtype=jnp.int32)
    row_scale_values = ADAPTER_ALPHA / row_rank_values.astype(jnp.float32)
    inside = columns[None, :] < row_rank_values[:, None]
    return jnp.where(inside, shrink * row_scale_values[:, None], jnp.zeros_like(shrink)).astype(jnp.bfloat16)


def reference(input_rows, up_weight, adapter_down, adapter_up, ranks, adapter_slot, segment_lengths, segment_adapter):
    slot_row, row_rank_values = row_tables(ROWS, ranks, adapter_slot, segment_lengths, segment_adapter)
    base = jnp.dot(input_rows, up_weight, preferred_element_type=jnp.float32)
    flattened_down = adapter_down.reshape(ADAPTER_COUNT * RANK_BLOCK, MODEL_WIDTH)
    wide = jnp.dot(input_rows, flattened_down.T, preferred_element_type=jnp.float32).reshape(ROWS, ADAPTER_COUNT, RANK_BLOCK)
    shrink = jnp.take_along_axis(wide, slot_row[:, None, None], axis=1)[:, 0, :]
    coeff = coefficients(shrink, row_rank_values)
    seg_ends = jnp.cumsum(segment_lengths).astype(jnp.int32)
    seg_starts = (seg_ends - segment_lengths).astype(jnp.int32)
    seg_slots = jnp.sum((segment_adapter[:, None] == jnp.arange(ADAPTER_COUNT, dtype=jnp.int32)[None, :]).astype(jnp.int32) * adapter_slot[None, :], axis=1)
    padded = jnp.concatenate([coeff, jnp.zeros((MOST_SEG, RANK_BLOCK), jnp.bfloat16)], axis=0)
    offsets = jnp.arange(MOST_SEG, dtype=jnp.int32)

    def add_segment(running, item):
        seg_start, seg_length, segment_slot = item
        rows_block = lax.dynamic_slice_in_dim(padded, seg_start, MOST_SEG, 0)
        adapter_factor = lax.dynamic_index_in_dim(adapter_up, segment_slot, 0, keepdims=False)
        term = jnp.dot(rows_block, adapter_factor, preferred_element_type=jnp.float32)
        term = jnp.where((offsets < seg_length)[:, None], term, jnp.zeros_like(term))
        previous = lax.dynamic_slice_in_dim(running, seg_start, MOST_SEG, 0)
        return lax.dynamic_update_slice_in_dim(running, previous + term, seg_start, 0), None

    running = jnp.zeros((ROWS + MOST_SEG, HIDDEN_UNITS), jnp.float32)
    running, unused = lax.scan(add_segment, running, (seg_starts, segment_lengths, seg_slots))
    return (base + running[:ROWS]).astype(jnp.bfloat16)
```

```python
import jax
import jax.numpy as jnp
from jax import lax
from jax.sharding import PartitionSpec as P

ADAPTER_ALPHA = 32.0


def row_tables(row_count, ranks, adapter_slot, segment_lengths, segment_adapter):
    seg_ends = jnp.cumsum(segment_lengths)
    positions = jnp.arange(row_count, dtype=jnp.int32)
    seg_row = jnp.sum((seg_ends[None, :] <= positions[:, None]).astype(jnp.int32), axis=1)
    seg_pick = (
        seg_row[:, None] == jnp.arange(segment_lengths.shape[0], dtype=jnp.int32)[None, :]
    ).astype(jnp.int32)
    adapter_row = jnp.sum(seg_pick * segment_adapter[None, :], axis=1)
    pool_pick = (
        adapter_row[:, None] == jnp.arange(ranks.shape[0], dtype=jnp.int32)[None, :]
    ).astype(jnp.int32)
    slot_row = jnp.sum(pool_pick * adapter_slot[None, :], axis=1)
    row_rank_values = jnp.sum(pool_pick * ranks[None, :], axis=1)
    return (slot_row, row_rank_values)


def on_device(
    input_rows,
    up_weight,
    adapter_down,
    adapter_up,
    ranks,
    adapter_slot,
    segment_lengths,
    segment_adapter,
):
    shards = lax.axis_size("tensor")
    position = lax.axis_index("tensor")
    total_rows = input_rows.shape[0] * shards
    stored, rank_width, hidden = adapter_up.shape
    width = hidden // shards
    outgoing = jnp.stack(
        [adapter_up[:, :, i * width : (i + 1) * width] for i in range(shards)], axis=0
    )
    incoming = lax.all_to_all(outgoing, "tensor", split_axis=0, concat_axis=0, tiled=True)
    rows = lax.all_gather(input_rows, "tensor", axis=0, tiled=True)
    slot_row, row_rank = row_tables(
        total_rows, ranks, adapter_slot, segment_lengths, segment_adapter
    )
    shrink = jnp.einsum("gf,ojf->ogj", rows, adapter_down, preferred_element_type=jnp.float32)
    own = position * stored + jnp.arange(stored, dtype=jnp.int32)
    inside = jnp.arange(rank_width, dtype=jnp.int32)[None, :] < row_rank[:, None]
    keep = (slot_row[None, :] == own[:, None])[:, :, None] & inside[None]
    scale = ADAPTER_ALPHA / row_rank.astype(jnp.float32)
    own_coeff = jnp.where(keep, shrink * scale[None, :, None], 0.0).astype(jnp.bfloat16)
    coeff = lax.all_gather(own_coeff, "tensor", axis=0, tiled=True)
    base = jnp.dot(rows, up_weight, preferred_element_type=jnp.float32)
    placed = coeff.transpose(1, 0, 2).reshape(total_rows, shards * stored * rank_width)
    factors = incoming.reshape(shards * stored * rank_width, width)
    term = jnp.dot(placed, factors, preferred_element_type=jnp.float32)
    return (base + term).astype(jnp.bfloat16)


def solution(mesh):
    placed = (
        P(("groups", "tensor"), None),
        P(None, "tensor"),
        P(("groups", "tensor"), None, None),
        P(("groups", "tensor"), None, None),
        P("groups"),
        P("groups"),
        P("groups"),
        P("groups"),
    )
    return jax.shard_map(
        on_device, mesh=mesh, in_specs=placed, out_specs=P("groups", "tensor"), check_vma=False
    )
```

```python
import jax
import jax.numpy as jnp
from jax import lax
from jax.experimental import pallas as pl
from jax.sharding import PartitionSpec as P

ADAPTER_ALPHA = 32.0


def row_tables(row_count, ranks, adapter_slot, segment_lengths, segment_adapter):
    seg_ends = jnp.cumsum(segment_lengths)
    positions = jnp.arange(row_count, dtype=jnp.int32)
    seg_row = jnp.sum((seg_ends[None, :] <= positions[:, None]).astype(jnp.int32), axis=1)
    seg_pick = (
        seg_row[:, None] == jnp.arange(segment_lengths.shape[0], dtype=jnp.int32)[None, :]
    ).astype(jnp.int32)
    adapter_row = jnp.sum(seg_pick * segment_adapter[None, :], axis=1)
    pool_pick = (
        adapter_row[:, None] == jnp.arange(ranks.shape[0], dtype=jnp.int32)[None, :]
    ).astype(jnp.int32)
    slot_row = jnp.sum(pool_pick * adapter_slot[None, :], axis=1)
    row_rank_values = jnp.sum(pool_pick * ranks[None, :], axis=1)
    return (slot_row, row_rank_values)


def block_copy(source, target):
    target[0] = source[...]


def split_columns(array, shards):
    stored, rank_width, hidden = array.shape
    width = hidden // shards
    if width % 128:
        return jnp.stack([array[:, :, i * width : (i + 1) * width] for i in range(shards)], axis=0)
    return pl.pallas_call(
        block_copy,
        grid=(shards,),
        in_specs=[pl.BlockSpec((stored, rank_width, width), lambda i: (0, 0, i))],
        out_specs=pl.BlockSpec((1, stored, rank_width, width), lambda i: (i, 0, 0, 0)),
        out_shape=jax.ShapeDtypeStruct((shards, stored, rank_width, width), array.dtype),
        cost_estimate=pl.CostEstimate(
            flops=0, bytes_accessed=4 * stored * rank_width * hidden, transcendentals=0
        ),
    )(array)


def on_device(
    input_rows,
    up_weight,
    adapter_down,
    adapter_up,
    ranks,
    adapter_slot,
    segment_lengths,
    segment_adapter,
):
    shards = lax.axis_size("tensor")
    position = lax.axis_index("tensor")
    total_rows = input_rows.shape[0] * shards
    stored, rank_width, hidden = adapter_up.shape
    width = hidden // shards
    outgoing = split_columns(adapter_up, shards)
    incoming = lax.all_to_all(outgoing, "tensor", split_axis=0, concat_axis=0, tiled=True)
    rows = lax.all_gather(input_rows, "tensor", axis=0, tiled=True)
    slot_row, row_rank = row_tables(
        total_rows, ranks, adapter_slot, segment_lengths, segment_adapter
    )
    shrink = jnp.einsum("gf,ojf->ogj", rows, adapter_down, preferred_element_type=jnp.float32)
    own = position * stored + jnp.arange(stored, dtype=jnp.int32)
    inside = jnp.arange(rank_width, dtype=jnp.int32)[None, :] < row_rank[:, None]
    keep = (slot_row[None, :] == own[:, None])[:, :, None] & inside[None]
    scale = ADAPTER_ALPHA / row_rank.astype(jnp.float32)
    own_coeff = jnp.where(keep, shrink * scale[None, :, None], 0.0).astype(jnp.bfloat16)
    base = jnp.dot(rows, up_weight, preferred_element_type=jnp.float32)
    own_coeff, base = lax.optimization_barrier((own_coeff, base))
    coeff = lax.all_gather(own_coeff, "tensor", axis=0, tiled=True)
    placed = coeff.transpose(1, 0, 2).reshape(total_rows, shards * stored * rank_width)
    factors = incoming.reshape(shards * stored * rank_width, width)
    term = jnp.dot(placed, factors, preferred_element_type=jnp.float32)
    return (base + term).astype(jnp.bfloat16)


def solution(mesh):
    placed = (
        P(("groups", "tensor"), None),
        P(None, "tensor"),
        P(("groups", "tensor"), None, None),
        P(("groups", "tensor"), None, None),
        P("groups"),
        P("groups"),
        P("groups"),
        P("groups"),
    )
    return jax.shard_map(
        on_device, mesh=mesh, in_specs=placed, out_specs=P("groups", "tensor"), check_vma=False
    )
```

```python
import jax
import jax.numpy as jnp
from jax import lax
from jax.experimental import pallas as pl
from jax.experimental.pallas import tpu as pltpu
from jax.sharding import PartitionSpec as P

ADAPTER_ALPHA = 32.0
RING_CHIPS = 8


def row_tables(row_count, ranks, adapter_slot, segment_lengths, segment_adapter):
    seg_ends = jnp.cumsum(segment_lengths)
    positions = jnp.arange(row_count, dtype=jnp.int32)
    seg_row = jnp.sum((seg_ends[None, :] <= positions[:, None]).astype(jnp.int32), axis=1)
    seg_pick = (
        seg_row[:, None] == jnp.arange(segment_lengths.shape[0], dtype=jnp.int32)[None, :]
    ).astype(jnp.int32)
    adapter_row = jnp.sum(seg_pick * segment_adapter[None, :], axis=1)
    pool_pick = (
        adapter_row[:, None] == jnp.arange(ranks.shape[0], dtype=jnp.int32)[None, :]
    ).astype(jnp.int32)
    slot_row = jnp.sum(pool_pick * adapter_slot[None, :], axis=1)
    row_rank_values = jnp.sum(pool_pick * ranks[None, :], axis=1)
    return (slot_row, row_rank_values)


def split_columns(array, shards):
    stored, rank_width, hidden = array.shape
    width = hidden // shards
    if width % 128:
        return jnp.stack([array[:, :, i * width : (i + 1) * width] for i in range(shards)], axis=0)

    def kernel(source, target, sems):
        copies = [
            pltpu.make_async_copy(
                source.at[:, :, pl.ds(i * width, width)], target.at[i], sems.at[i]
            )
            for i in range(shards)
        ]
        for copy in copies:
            copy.start()
        for copy in copies:
            copy.wait()

    return pl.pallas_call(
        kernel,
        in_specs=[pl.BlockSpec(memory_space=pl.ANY)],
        out_specs=pl.BlockSpec(memory_space=pl.ANY),
        out_shape=jax.ShapeDtypeStruct((shards, stored, rank_width, width), array.dtype),
        scratch_shapes=[pltpu.SemaphoreType.DMA((shards,))],
        cost_estimate=pl.CostEstimate(
            flops=0, bytes_accessed=4 * stored * rank_width * hidden, transcendentals=0
        ),
    )(array)


def place_blocks(blocks, places):
    count = len(blocks)
    height, width = blocks[0].shape

    def kernel(places_ref, *refs):
        sources, target, sems = refs[:count], refs[count], refs[count + 1]
        copies = [
            pltpu.make_async_copy(
                sources[i],
                target.at[pl.ds(pl.multiple_of(places_ref[i] * height, height), height)],
                sems.at[i],
            )
            for i in range(count)
        ]
        for copy in copies:
            copy.start()
        for copy in copies:
            copy.wait()

    return pl.pallas_call(
        kernel,
        in_specs=[pl.BlockSpec(memory_space=pltpu.SMEM)]
        + [pl.BlockSpec(memory_space=pl.ANY)] * count,
        out_specs=pl.BlockSpec(memory_space=pl.ANY),
        out_shape=jax.ShapeDtypeStruct((count * height, width), blocks[0].dtype),
        scratch_shapes=[pltpu.SemaphoreType.DMA((count,))],
        cost_estimate=pl.CostEstimate(
            flops=0, bytes_accessed=4 * count * height * width, transcendentals=0
        ),
    )(places, *blocks)


def ring_gather(block, shards):
    chips = shards // 2
    depth = chips // 2
    cycle = list(range(0, chips, 2)) + list(range(chips - 1, 0, -2))
    ahead = [
        (2 * cycle[p] + c, 2 * cycle[(p + 1) % chips] + c) for p in range(chips) for c in range(2)
    ]
    back = [(b, a) for a, b in ahead]
    sibling = [(t, t ^ 1) for t in range(shards)]
    position = lax.axis_index("tensor")
    spot = jnp.zeros((), jnp.int32)
    for p in range(chips):
        spot = jnp.where(position // 2 == cycle[p], p, spot)
    held = {0: block}
    for step in range(1, depth + 1):
        held[-step] = lax.ppermute(held[1 - step], "tensor", ahead)
        if step < chips - depth:
            held[step] = lax.ppermute(held[step - 1], "tensor", back)
    table = jnp.asarray(cycle, jnp.int32)
    blocks, places = [], []
    for offset, piece in held.items():
        chip = table[(spot + offset) % chips]
        blocks += [piece, lax.ppermute(piece, "tensor", sibling)]
        places += [2 * chip + position % 2, 2 * chip + 1 - position % 2]
    return place_blocks(blocks, jnp.stack(places).astype(jnp.int32))


def gather_rows(block, shards):
    if shards == 2 * RING_CHIPS:
        return ring_gather(block, shards)
    return lax.all_gather(block, "tensor", axis=0, tiled=True)


def butterfly_sum(value, shards):
    if shards & (shards - 1):
        return lax.psum(value, "tensor")
    bit = 1
    while bit < shards:
        value = value + lax.ppermute(value, "tensor", [(t, t ^ bit) for t in range(shards)])
        bit *= 2
    return value


def on_device(
    input_rows,
    up_weight,
    adapter_down,
    adapter_up,
    ranks,
    adapter_slot,
    segment_lengths,
    segment_adapter,
):
    shards = lax.axis_size("tensor")
    position = lax.axis_index("tensor")
    total_rows = input_rows.shape[0] * shards
    stored, rank_width, hidden = adapter_up.shape
    width = hidden // shards
    slots = shards * stored
    outgoing = split_columns(adapter_up, shards)
    incoming = lax.all_to_all(outgoing, "tensor", split_axis=0, concat_axis=0, tiled=True)
    rows = gather_rows(input_rows, shards)
    slot_row, row_rank = row_tables(
        total_rows, ranks, adapter_slot, segment_lengths, segment_adapter
    )
    inside = jnp.arange(rank_width, dtype=jnp.int32)[None, :] < row_rank[:, None]
    scale = ADAPTER_ALPHA / row_rank.astype(jnp.float32)
    own_coeff = jnp.zeros((total_rows, rank_width), jnp.bfloat16)
    for i in range(stored):
        shrink = jnp.einsum(
            "gf,jf->gj", rows, adapter_down[i], preferred_element_type=jnp.float32
        )
        keep = (slot_row == position * stored + i)[:, None] & inside
        own_coeff += jnp.where(keep, shrink * scale[:, None], 0.0).astype(jnp.bfloat16)
    coeff = butterfly_sum(own_coeff, shards)
    base = jnp.dot(rows, up_weight, preferred_element_type=jnp.float32)
    picked = slot_row[:, None] == jnp.arange(slots, dtype=jnp.int32)[None, :]
    placed = jnp.where(picked[:, :, None], coeff[:, None, :], 0).astype(jnp.bfloat16)
    placed = placed.reshape(total_rows, slots * rank_width)
    factors = incoming.reshape(slots * rank_width, width)
    term = jnp.dot(placed, factors, preferred_element_type=jnp.float32)
    return (base + term).astype(jnp.bfloat16)


def solution(mesh):
    placed = (
        P(("groups", "tensor"), None),
        P(None, "tensor"),
        P(("groups", "tensor"), None, None),
        P(("groups", "tensor"), None, None),
        P("groups"),
        P("groups"),
        P("groups"),
        P("groups"),
    )
    return jax.shard_map(
        on_device, mesh=mesh, in_specs=placed, out_specs=P("groups", "tensor"), check_vma=False
    )
```

```python
import jax
import jax.numpy as jnp
import numpy as np
from jax import lax
from jax.experimental import pallas as pl
from jax.experimental.pallas import tpu as pltpu
from jax.sharding import PartitionSpec as P

ADAPTER_ALPHA = 32.0
POOLED_SHARDS = 16
STEP = 16


def row_tables(row_count, ranks, adapter_slot, segment_lengths, segment_adapter):
    seg_ends = jnp.cumsum(segment_lengths)
    positions = jnp.arange(row_count, dtype=jnp.int32)
    seg_row = jnp.sum((seg_ends[None, :] <= positions[:, None]).astype(jnp.int32), axis=1)
    seg_pick = (
        seg_row[:, None] == jnp.arange(segment_lengths.shape[0], dtype=jnp.int32)[None, :]
    ).astype(jnp.int32)
    adapter_row = jnp.sum(seg_pick * segment_adapter[None, :], axis=1)
    pool_pick = (
        adapter_row[:, None] == jnp.arange(ranks.shape[0], dtype=jnp.int32)[None, :]
    ).astype(jnp.int32)
    slot_row = jnp.sum(pool_pick * adapter_slot[None, :], axis=1)
    row_rank_values = jnp.sum(pool_pick * ranks[None, :], axis=1)
    return (slot_row, row_rank_values)


def vmem(buffers):
    return pltpu.CompilerParams(vmem_limit_bytes=buffers + (8 << 20))


def split_for_pair(up_factor, core, chips):
    rank_width, hidden = up_factor.shape
    width = hidden // (2 * chips)

    def kernel(core_ref, source, mine, other, sems):
        copies = []
        for q in range(chips):
            for target, half in ((mine, core_ref[0]), (other, 1 - core_ref[0])):
                start = pl.multiple_of((2 * q + half) * width, width)
                copies.append(
                    pltpu.make_async_copy(
                        source.at[:, pl.ds(start, width)], target.at[q], sems.at[len(copies)]
                    )
                )
        for copy in copies:
            copy.start()
        for copy in copies:
            copy.wait()

    block = jax.ShapeDtypeStruct((chips, rank_width, width), up_factor.dtype)
    return pl.pallas_call(
        kernel,
        in_specs=[pl.BlockSpec(memory_space=pltpu.SMEM), pl.BlockSpec(memory_space=pl.ANY)],
        out_specs=[pl.BlockSpec(memory_space=pltpu.VMEM)] * 2,
        out_shape=[block, block],
        scratch_shapes=[pltpu.SemaphoreType.DMA((2 * chips,))],
        compiler_params=vmem(2 * rank_width * hidden),
        cost_estimate=pl.CostEstimate(
            flops=0, bytes_accessed=4 * rank_width * hidden, transcendentals=0
        ),
    )(core, up_factor)


def collect_rows(blocks, places, down_pair, gain):
    count = len(blocks)
    height, features = blocks[0].shape
    rank_width = down_pair[0].shape[0]
    chunk = 1024 if features % 1024 == 0 else features

    def kernel(places_ref, gain_ref, *refs):
        sources, down_refs = refs[:count], refs[count : count + 2]
        rows_ref, coeff_ref, downs, sems = refs[count + 2 :]
        copies = [
            pltpu.make_async_copy(
                sources[i],
                rows_ref.at[pl.ds(pl.multiple_of(places_ref[i] * height, height), height)],
                sems.at[i],
            )
            for i in range(count)
        ]
        copies += [
            pltpu.make_async_copy(
                down_refs[i], downs.at[pl.ds(i * rank_width, rank_width)], sems.at[count + i]
            )
            for i in range(2)
        ]
        for copy in copies:
            copy.start()
        for copy in copies:
            copy.wait()

        def add(k, total):
            columns = pl.ds(pl.multiple_of(k * chunk, chunk), chunk)
            return total + lax.dot_general(
                rows_ref[:, columns],
                downs[:, columns],
                (((1,), (1,)), ((), ())),
                preferred_element_type=jnp.float32,
            )

        shrink = lax.fori_loop(0, features // chunk, add, jnp.zeros(gain_ref.shape, jnp.float32))
        coeff_ref[...] = (shrink * gain_ref[...]).astype(jnp.bfloat16)

    rows = count * height
    return pl.pallas_call(
        kernel,
        in_specs=[pl.BlockSpec(memory_space=pltpu.SMEM), pl.BlockSpec(memory_space=pltpu.VMEM)]
        + [pl.BlockSpec(memory_space=pl.ANY)] * (count + 2),
        out_specs=[pl.BlockSpec(memory_space=pltpu.VMEM)] * 2,
        out_shape=[
            jax.ShapeDtypeStruct((rows, features), blocks[0].dtype),
            jax.ShapeDtypeStruct((rows, 2 * rank_width), jnp.bfloat16),
        ],
        scratch_shapes=[
            pltpu.VMEM((2 * rank_width, features), down_pair[0].dtype),
            pltpu.SemaphoreType.DMA((count + 2,)),
        ],
        compiler_params=vmem(4 * rows * features),
        cost_estimate=pl.CostEstimate(
            flops=4 * rows * features * rank_width,
            bytes_accessed=4 * rows * features,
            transcendentals=0,
        ),
    )(places, gain, *blocks, *down_pair)


def build_payload(choose, fixed, coeff, mine, other):
    chips, rank_width, width = mine.shape
    count = choose.shape[0]

    def kernel(choose_ref, fixed_ref, coeff_ref, mine_ref, other_ref, out_ref, factors, sems):
        copies = []
        for q in range(chips):
            for half, source in enumerate((mine_ref, other_ref)):
                copies.append(
                    pltpu.make_async_copy(
                        source.at[q],
                        factors.at[q, pl.ds(half * rank_width, rank_width)],
                        sems.at[q, half],
                    )
                )
        for copy in copies:
            copy.start()
        select = jnp.dot(choose_ref[...], coeff_ref[...], preferred_element_type=jnp.float32)
        select = (select + fixed_ref[...].astype(jnp.float32)).astype(jnp.bfloat16)
        for q in range(chips):
            copies[2 * q].wait()
            copies[2 * q + 1].wait()
            out_ref[q] = jnp.dot(
                select, factors[q], preferred_element_type=jnp.float32
            ).astype(out_ref.dtype)

    return pl.pallas_call(
        kernel,
        in_specs=[pl.BlockSpec(memory_space=pltpu.VMEM)] * 3
        + [pl.BlockSpec(memory_space=pl.ANY)] * 2,
        out_specs=pl.BlockSpec(memory_space=pltpu.VMEM),
        out_shape=jax.ShapeDtypeStruct((chips, count, width), mine.dtype),
        scratch_shapes=[
            pltpu.VMEM((chips, 2 * rank_width, width), mine.dtype),
            pltpu.SemaphoreType.DMA((chips, 2)),
        ],
        compiler_params=vmem(4 * chips * width * (2 * rank_width + count)),
        cost_estimate=pl.CostEstimate(
            flops=4 * chips * count * rank_width * width,
            bytes_accessed=2 * chips * width * (2 * rank_width + count),
            transcendentals=0,
        ),
    )(choose, fixed, coeff, mine, other)


def ring_gather(block, shards):
    chips = shards // 2
    depth = chips // 2
    cycle = list(range(0, chips, 2)) + list(range(chips - 1, 0, -2))
    ahead = [
        (2 * cycle[p] + c, 2 * cycle[(p + 1) % chips] + c) for p in range(chips) for c in range(2)
    ]
    back = [(b, a) for a, b in ahead]
    sibling = [(t, t ^ 1) for t in range(shards)]
    held = {0: block}
    for step in range(1, depth + 1):
        held[-step] = lax.ppermute(held[1 - step], "tensor", ahead)
        if step < chips - depth:
            held[step] = lax.ppermute(held[step - 1], "tensor", back)
    blocks = []
    for piece in held.values():
        blocks += [piece, lax.ppermute(piece, "tensor", sibling)]
    table = np.zeros((shards, shards), np.int32)
    for t in range(shards):
        for i, offset in enumerate(held):
            chip = cycle[(cycle.index(t // 2) + offset) % chips]
            table[t, 2 * i], table[t, 2 * i + 1] = 2 * chip + t % 2, 2 * chip + 1 - t % 2
    places = lax.dynamic_index_in_dim(table, lax.axis_index("tensor"), keepdims=False)
    return blocks, places, held[-1]


def largest_over_groups(value):
    groups = lax.axis_size("groups")
    for shift in range(1, groups):
        other = lax.ppermute(value, "groups", [(g, (g + shift) % groups) for g in range(groups)])
        value = jnp.maximum(value, other)
    return value


def pooled(input_rows, up_weight, adapter_down, adapter_up, slot_row, row_rank, slot_rank):
    shards = lax.axis_size("tensor")
    position = lax.axis_index("tensor")
    chips, core = shards // 2, position & 1
    total_rows = input_rows.shape[0] * shards
    rank_width, hidden = adapter_up.shape[1:]
    width = hidden // shards
    sibling = [(t, t ^ 1) for t in range(shards)]
    count = jnp.arange

    blocks, places, first = ring_gather(input_rows, shards)
    adapter_up, adapter_down, first = lax.optimization_barrier((adapter_up, adapter_down, first))
    mine, other = split_for_pair(adapter_up[0], core[None].astype(jnp.int32), chips)
    other = lax.ppermute(other, "tensor", sibling)
    down_pair = (adapter_down[0], lax.ppermute(adapter_down[0], "tensor", sibling))

    owner = slot_row[:, None] == count(shards, dtype=jnp.int32)[None, :]
    rows_of = jnp.sum(owner.astype(jnp.int32), axis=0)
    by_factor = slot_rank < rows_of
    used = jnp.minimum(slot_rank, rows_of)
    begin = jnp.where(count(shards) & 1 == 1, jnp.roll(used, 1), 0)
    fullest = largest_over_groups(jnp.max(jnp.sum(used.reshape(chips, 2), axis=1))[None])[0]
    earlier = (count(total_rows)[:, None] > count(total_rows)[None, :]).astype(jnp.bfloat16)
    before = jnp.dot(earlier, owner.astype(jnp.bfloat16), preferred_element_type=jnp.float32)
    spot_row = jnp.sum(jnp.where(owner, before.astype(jnp.int32) + begin[None, :], 0), axis=1)
    factor_row = jnp.any(owner & by_factor[None, :], axis=1)
    chip_row = slot_row >> 1

    scale = ADAPTER_ALPHA / row_rank.astype(jnp.float32)
    inside = count(rank_width, dtype=jnp.int32)[None, :] < row_rank[:, None]
    pair = jnp.stack([position, position ^ 1])
    here = slot_row[:, None] == pair[None, :]
    gain = jnp.where(here[:, :, None] & inside[:, None, :], scale[:, None, None], 0.0)
    gain = gain.reshape(total_rows, 2 * rank_width)
    limit = 2 * rank_width
    choose = (
        (count(limit)[:, None] == spot_row[None, :])
        & (~factor_row & (chip_row == position >> 1))[None, :]
    ).astype(jnp.bfloat16)
    pair_begin, pair_used, pair_kind = begin[pair], used[pair], by_factor[pair]
    column = count(rank_width)[None, None, :]
    fixed = (
        pair_kind[None, :, None]
        & (column < pair_used[None, :, None])
        & (count(limit)[:, None, None] == column + pair_begin[None, :, None])
    )
    fixed = fixed.astype(jnp.bfloat16).reshape(limit, 2 * rank_width)

    rows, coeff = collect_rows(blocks, places, down_pair, gain)

    def finish(payload_rows):
        def run(rows, coeff, choose, fixed, mine, other, up_weight):
            own = coeff[:, :rank_width] + coeff[:, rank_width:]
            every = own
            for shift in range(1, chips):
                hop = [(t, (t + 2 * shift) % shards) for t in range(shards)]
                every = every + lax.ppermute(own, "tensor", hop)
            payload = build_payload(
                choose[:payload_rows], fixed[:payload_rows], coeff, mine, other
            )
            incoming = lax.all_to_all(
                payload,
                "tensor",
                split_axis=0,
                concat_axis=0,
                axis_index_groups=[list(range(c, shards, 2)) for c in range(2)],
                tiled=True,
            )
            base = jnp.dot(rows, up_weight, preferred_element_type=jnp.float32)
            line = count(payload_rows)
            terms = (
                (~factor_row[:, None] & (chip_row[:, None] == count(chips)[None, :]))[:, :, None]
                & (line[None, None, :] == spot_row[:, None, None])
            ).reshape(total_rows, chips * payload_rows)
            wide = jnp.where((owner & by_factor[None, :])[:, :, None], every[:, None, :], 0)
            wide = wide.astype(jnp.bfloat16).reshape(total_rows, shards * rank_width)
            shift_to = (
                (count(shards)[:, None] >> 1 == count(chips)[None, :])[:, None, :, None]
                & (
                    (begin[:, None] + count(rank_width)[None, :])[:, :, None, None]
                    == line[None, None, None, :]
                )
            ).astype(jnp.bfloat16)
            shift_to = shift_to.reshape(shards * rank_width, chips * payload_rows)
            weights = jnp.dot(wide, shift_to, preferred_element_type=jnp.float32)
            weights = jnp.where(terms, 1.0, weights).astype(jnp.bfloat16)
            flat = incoming.reshape(chips * payload_rows, width)
            term = jnp.dot(weights, flat, preferred_element_type=jnp.float32)
            return (base + term).astype(jnp.bfloat16)

        return run

    sizes = list(range(min(2 * STEP, limit), limit + 1, STEP))
    which = jnp.sum((fullest > jnp.asarray(sizes[:-1], jnp.int32)).astype(jnp.int32))
    return lax.switch(
        which,
        [finish(size) for size in sizes],
        *(rows, coeff, choose, fixed, mine, other, up_weight),
    )


def gathered(input_rows, up_weight, adapter_down, adapter_up, slot_row, row_rank):
    shards = lax.axis_size("tensor")
    position = lax.axis_index("tensor")
    total_rows = input_rows.shape[0] * shards
    stored, rank_width, hidden = adapter_up.shape
    width = hidden // shards
    slots = shards * stored
    outgoing = jnp.stack(
        [adapter_up[:, :, i * width : (i + 1) * width] for i in range(shards)], axis=0
    )
    incoming = lax.all_to_all(outgoing, "tensor", split_axis=0, concat_axis=0, tiled=True)
    rows = lax.all_gather(input_rows, "tensor", axis=0, tiled=True)
    shrink = jnp.einsum("gf,ojf->ogj", rows, adapter_down, preferred_element_type=jnp.float32)
    own = position * stored + jnp.arange(stored, dtype=jnp.int32)
    inside = jnp.arange(rank_width, dtype=jnp.int32)[None, :] < row_rank[:, None]
    keep = (slot_row[None, :] == own[:, None])[:, :, None] & inside[None]
    scale = ADAPTER_ALPHA / row_rank.astype(jnp.float32)
    own_coeff = jnp.where(keep, shrink * scale[None, :, None], 0.0).astype(jnp.bfloat16)
    base = jnp.dot(rows, up_weight, preferred_element_type=jnp.float32)
    own_coeff, base = lax.optimization_barrier((own_coeff, base))
    coeff = lax.all_gather(own_coeff, "tensor", axis=0, tiled=True)
    placed = coeff.transpose(1, 0, 2).reshape(total_rows, slots * rank_width)
    factors = incoming.reshape(slots * rank_width, width)
    term = jnp.dot(placed, factors, preferred_element_type=jnp.float32)
    return (base + term).astype(jnp.bfloat16)


def on_device(
    input_rows,
    up_weight,
    adapter_down,
    adapter_up,
    ranks,
    adapter_slot,
    segment_lengths,
    segment_adapter,
):
    shards = lax.axis_size("tensor")
    slot_row, row_rank = row_tables(
        input_rows.shape[0] * shards, ranks, adapter_slot, segment_lengths, segment_adapter
    )
    tiled = up_weight.shape[1] % 128 == 0 and input_rows.shape[0] % 16 == 0
    if shards != POOLED_SHARDS or adapter_up.shape[0] != 1 or not tiled:
        return gathered(input_rows, up_weight, adapter_down, adapter_up, slot_row, row_rank)
    slots = jnp.arange(shards, dtype=jnp.int32)
    slot_rank = jnp.sum(jnp.where(slots[:, None] == adapter_slot[None, :], ranks[None, :], 0), 1)
    return pooled(
        input_rows, up_weight, adapter_down, adapter_up, slot_row, row_rank, slot_rank
    )


def solution(mesh):
    placed = (
        P(("groups", "tensor"), None),
        P(None, "tensor"),
        P(("groups", "tensor"), None, None),
        P(("groups", "tensor"), None, None),
        P("groups"),
        P("groups"),
        P("groups"),
        P("groups"),
    )
    return jax.shard_map(
        on_device, mesh=mesh, in_specs=placed, out_specs=P("groups", "tensor"), check_vma=False
    )
```

```python
import functools

import jax
import jax.numpy as jnp
import numpy as np
from jax import lax
from jax.experimental import pallas as pl
from jax.experimental.pallas import tpu as pltpu
from jax.sharding import PartitionSpec as P

ADAPTER_ALPHA = 32.0
POOLED_SHARDS = 16
FIRST_ROWS = 80


def row_tables(row_count, ranks, adapter_slot, segment_lengths, segment_adapter):
    seg_ends = jnp.cumsum(segment_lengths)
    positions = jnp.arange(row_count, dtype=jnp.int32)
    seg_row = jnp.sum((seg_ends[None, :] <= positions[:, None]).astype(jnp.int32), axis=1)
    seg_pick = (
        seg_row[:, None] == jnp.arange(segment_lengths.shape[0], dtype=jnp.int32)[None, :]
    ).astype(jnp.int32)
    adapter_row = jnp.sum(seg_pick * segment_adapter[None, :], axis=1)
    pool_pick = (
        adapter_row[:, None] == jnp.arange(ranks.shape[0], dtype=jnp.int32)[None, :]
    ).astype(jnp.int32)
    slot_row = jnp.sum(pool_pick * adapter_slot[None, :], axis=1)
    row_rank_values = jnp.sum(pool_pick * ranks[None, :], axis=1)
    return (slot_row, row_rank_values)


def vmem(buffers):
    return pltpu.CompilerParams(vmem_limit_bytes=buffers + (8 << 20))


def split_for_pair(up_factor, core, chips):
    rank_width, hidden = up_factor.shape
    width = hidden // (2 * chips)

    def kernel(core_ref, source, mine, other, sems):
        copies = []
        for q in range(chips):
            for target, half in ((mine, core_ref[0]), (other, 1 - core_ref[0])):
                start = pl.multiple_of((2 * q + half) * width, width)
                copies.append(
                    pltpu.make_async_copy(
                        source.at[:, pl.ds(start, width)], target.at[q], sems.at[len(copies)]
                    )
                )
        for copy in copies:
            copy.start()
        for copy in copies:
            copy.wait()

    block = jax.ShapeDtypeStruct((chips, rank_width, width), up_factor.dtype)
    return pl.pallas_call(
        kernel,
        in_specs=[pl.BlockSpec(memory_space=pltpu.SMEM), pl.BlockSpec(memory_space=pl.ANY)],
        out_specs=[pl.BlockSpec(memory_space=pltpu.VMEM)] * 2,
        out_shape=[block, block],
        scratch_shapes=[pltpu.SemaphoreType.DMA((2 * chips,))],
        compiler_params=vmem(2 * rank_width * hidden),
        cost_estimate=pl.CostEstimate(
            flops=0, bytes_accessed=4 * rank_width * hidden, transcendentals=0
        ),
    )(core, up_factor)


def describe(ranks, adapter_slot, segment_lengths, segment_adapter, position, total_rows, limit):
    slots, segments = ranks.shape[0], segment_lengths.shape[0]
    rank_width = limit // 2
    shift = rank_width.bit_length() - 1

    def kernel(
        ranks_ref, home_ref, length_ref, adapter_ref, position_ref,
        gain_ref, choose_ref, fixed_ref, code_ref, begin_ref, full_ref,
        rank_of, rows_of, used, factor, order,
    ):
        for a in range(slots):
            rows_of[a] = 0
            rank_of[home_ref[a]] = ranks_ref[a]
        starts, start = [], jnp.int32(0)
        for i in range(segments):
            slot = home_ref[adapter_ref[i]]
            starts.append((start, start + length_ref[i], slot))
            order[i] = rows_of[slot] - start
            rows_of[slot] = rows_of[slot] + length_ref[i]
            start = start + length_ref[i]
        full = jnp.int32(0)
        for s in range(slots):
            used[s] = jnp.minimum(rows_of[s], rank_of[s])
            factor[s] = (rank_of[s] < rows_of[s]).astype(jnp.int32)
            begin_ref[s] = used[s - 1] if s % 2 else jnp.int32(0)
            if s % 2:
                full = jnp.maximum(full, used[s - 1] + used[s])
        full_ref[0] = full

        def tables(row):
            spot, code = jnp.zeros_like(row), jnp.zeros_like(row)
            for i, (low, high, slot) in enumerate(starts):
                hit = (row >= low) & (row < high)
                spot = jnp.where(hit, row + (order[i] + begin_ref[slot]), spot)
                code = jnp.where(hit, slot + 32 * factor[slot] + 64 * rank_of[slot], code)
            return spot, code & 31, (code >> 5) & 1, code >> 6

        here = position_ref[0]
        spot, slot, by_factor, rank = tables(
            lax.broadcasted_iota(jnp.int32, (total_rows, limit), 0)
        )
        code_ref[...] = slot + 32 * by_factor + 64 * spot
        lane = lax.broadcasted_iota(jnp.int32, (total_rows, limit), 1)
        half, column = lane >> shift, lane & (rank_width - 1)
        scale = ADAPTER_ALPHA / rank.astype(jnp.float32)
        gain_ref[...] = jnp.where((slot == (here ^ half)) & (column < rank), scale, 0.0)

        spot, slot, by_factor, _ = tables(lax.broadcasted_iota(jnp.int32, (8, total_rows), 1))
        mine = ((slot >> 1) == (here >> 1)) & (by_factor == 0)
        spot = jnp.broadcast_to(jnp.where(mine, spot, -1)[:1], (limit, total_rows))
        line = lax.broadcasted_iota(jnp.int32, (limit, total_rows), 0)
        choose_ref[...] = jnp.where(line == spot, 1.0, 0.0).astype(jnp.bfloat16)

        line = lax.broadcasted_iota(jnp.int32, (limit, limit), 0)
        lane = lax.broadcasted_iota(jnp.int32, (limit, limit), 1)
        half, column = lane >> shift, lane & (rank_width - 1)
        other = here ^ 1
        begin = jnp.where(half == 0, begin_ref[here], begin_ref[other])
        bound = jnp.where(
            half == 0, used[here] * factor[here], used[other] * factor[other]
        )
        held = (line == begin + column) & (column < bound)
        fixed_ref[...] = jnp.where(held, 1.0, 0.0).astype(jnp.bfloat16)

    smem, whole = pl.BlockSpec(memory_space=pltpu.SMEM), pl.BlockSpec(memory_space=pltpu.VMEM)
    return pl.pallas_call(
        kernel,
        in_specs=[smem] * 5,
        out_specs=[whole] * 4 + [smem] * 2,
        out_shape=[
            jax.ShapeDtypeStruct((total_rows, limit), jnp.float32),
            jax.ShapeDtypeStruct((limit, total_rows), jnp.bfloat16),
            jax.ShapeDtypeStruct((limit, limit), jnp.bfloat16),
            jax.ShapeDtypeStruct((total_rows, limit), jnp.int32),
            jax.ShapeDtypeStruct((slots,), jnp.int32),
            jax.ShapeDtypeStruct((1,), jnp.int32),
        ],
        scratch_shapes=[pltpu.SMEM((slots,), jnp.int32)] * 4 + [pltpu.SMEM((segments,), jnp.int32)],
        compiler_params=vmem(16 * total_rows * limit),
        cost_estimate=pl.CostEstimate(
            flops=200 * total_rows * limit, bytes_accessed=16 * total_rows * limit, transcendentals=0
        ),
    )(ranks, adapter_slot, segment_lengths, segment_adapter, position)


def collect_rows(blocks, places, down_pair, gain):
    count = len(blocks)
    height, features = blocks[0].shape
    rank_width = down_pair[0].shape[0]
    chunk = 2048 if features % 2048 == 0 else features
    chunks = features // chunk

    def kernel(places_ref, gain_ref, *refs):
        sources, down_refs = refs[:count], refs[count : count + 2]
        rows_ref, coeff_ref, downs, sems = refs[count + 2 :]
        copies = []
        for k in range(chunks):
            columns = pl.ds(k * chunk, chunk)
            for i in range(2):
                copies.append(
                    pltpu.make_async_copy(
                        down_refs[i].at[:, columns],
                        downs.at[pl.ds(i * rank_width, rank_width), columns],
                        sems.at[k, count + i],
                    )
                )
            for i in range(count):
                start = pl.multiple_of(places_ref[i] * height, height)
                copies.append(
                    pltpu.make_async_copy(
                        sources[i].at[:, columns],
                        rows_ref.at[pl.ds(start, height), columns],
                        sems.at[k, i],
                    )
                )
        for copy in copies:
            copy.start()
        shrink = jnp.zeros(gain_ref.shape, jnp.float32)
        for k in range(chunks):
            for copy in copies[k * (count + 2) : (k + 1) * (count + 2)]:
                copy.wait()
            columns = pl.ds(k * chunk, chunk)
            shrink = shrink + lax.dot_general(
                rows_ref[:, columns],
                downs[:, columns],
                (((1,), (1,)), ((), ())),
                preferred_element_type=jnp.float32,
            )
        coeff_ref[...] = (shrink * gain_ref[...]).astype(jnp.bfloat16)

    rows = count * height
    return pl.pallas_call(
        kernel,
        in_specs=[pl.BlockSpec(memory_space=pltpu.SMEM), pl.BlockSpec(memory_space=pltpu.VMEM)]
        + [pl.BlockSpec(memory_space=pl.ANY)] * (count + 2),
        out_specs=[pl.BlockSpec(memory_space=pltpu.VMEM)] * 2,
        out_shape=[
            jax.ShapeDtypeStruct((rows, features), blocks[0].dtype),
            jax.ShapeDtypeStruct((rows, 2 * rank_width), jnp.bfloat16),
        ],
        scratch_shapes=[
            pltpu.VMEM((2 * rank_width, features), down_pair[0].dtype),
            pltpu.SemaphoreType.DMA((chunks, count + 2)),
        ],
        compiler_params=vmem(4 * rows * features),
        cost_estimate=pl.CostEstimate(
            flops=4 * rows * features * rank_width,
            bytes_accessed=4 * rows * features,
            transcendentals=0,
        ),
    )(places, gain, *blocks, *down_pair)


def build_payload(choose, fixed, coeff, mine, other, first, count):
    chips, rank_width, width = mine.shape

    def kernel(choose_ref, fixed_ref, coeff_ref, mine_ref, other_ref, out_ref):
        lines = pl.ds(first, count)
        select = jnp.dot(choose_ref[lines], coeff_ref[...], preferred_element_type=jnp.float32)
        select = (select + fixed_ref[lines].astype(jnp.float32)).astype(jnp.bfloat16)

        @pl.loop(0, chips)
        def _(q):
            out_ref[q] = jnp.dot(
                select,
                jnp.concatenate([mine_ref[q], other_ref[q]], axis=0),
                preferred_element_type=jnp.float32,
            ).astype(out_ref.dtype)

    return pl.pallas_call(
        kernel,
        in_specs=[pl.BlockSpec(memory_space=pltpu.VMEM)] * 5,
        out_specs=pl.BlockSpec(memory_space=pltpu.VMEM),
        out_shape=jax.ShapeDtypeStruct((chips, count, width), mine.dtype),
        compiler_params=vmem(4 * chips * width * (2 * rank_width + count)),
        cost_estimate=pl.CostEstimate(
            flops=4 * chips * count * rank_width * width,
            bytes_accessed=2 * chips * width * (2 * rank_width + count),
            transcendentals=0,
        ),
    )(choose, fixed, coeff, mine, other)


def combine(base, code, begin, more, coeffs, incoming, extra):
    total_rows, width = base.shape
    chips, first, _ = incoming.shape
    second = extra.shape[1]
    limit = first + second
    rank_width = limit // 2
    shift = rank_width.bit_length() - 1
    tile = 256 if width % 256 == 0 else 128

    def kernel(begin_ref, more_ref, base_ref, code_ref, *refs):
        coeff_refs, incoming_ref = refs[: len(coeffs)], refs[len(coeffs)]
        extra_ref, out_ref, late, sem = refs[len(coeffs) + 1 :]
        fetch = pltpu.make_async_copy(extra_ref, late, sem)
        half = functools.reduce(jnp.add, [ref[...].astype(jnp.float32) for ref in coeff_refs])
        both = jnp.concatenate([half, half], axis=1)
        code_value = code_ref[...]
        slot, by_factor, spot = code_value & 31, (code_value >> 5) & 1, code_value >> 6
        lane = lax.broadcasted_iota(jnp.int32, (total_rows, limit), 1)
        owned = jnp.where(by_factor == 1, slot, -1) - (lane >> shift)
        finished = jnp.where(by_factor == 0, spot, -1)[:, :1]
        finished_chip = (slot >> 1)[:, :1]

        def weights(low, count):
            target = finished - low
            target = jnp.where((target >= 0) & (target < count), finished_chip * count + target, -1)
            wide = lax.broadcasted_iota(jnp.int32, (total_rows, chips * count), 1)
            total = jnp.where(wide == target, 1.0, 0.0)
            line = lax.broadcasted_iota(jnp.int32, (limit, chips * count), 0)
            place = lax.broadcasted_iota(jnp.int32, (limit, chips * count), 1)
            for q in range(chips):
                goal = jnp.where(
                    line < rank_width, line, line - rank_width + begin_ref[2 * q + 1]
                ) - low
                moved = (goal >= 0) & (goal < count) & (place == q * count + goal)
                moved = jnp.where(moved, 1.0, 0.0).astype(jnp.bfloat16)
                part = jnp.where(owned == 2 * q, both, 0.0).astype(jnp.bfloat16)
                total = total + jnp.dot(part, moved, preferred_element_type=jnp.float32)
            return total.astype(jnp.bfloat16)

        near = weights(0, first)

        def write(far):
            @pl.loop(0, width // tile)
            def _(i):
                columns = pl.ds(pl.multiple_of(i * tile, tile), tile)
                block = incoming_ref[:, :, columns].reshape(chips * first, tile)
                total = jnp.dot(near, block, preferred_element_type=jnp.float32)
                total += base_ref[:, columns]
                if far is not None:
                    block = late[:, :, columns].reshape(chips * second, tile)
                    total += jnp.dot(far, block, preferred_element_type=jnp.float32)
                out_ref[:, columns] = total.astype(out_ref.dtype)

        @pl.when(more_ref[0] > first)
        def _():
            fetch.start()
            far = weights(first, second)
            fetch.wait()
            write(far)

        @pl.when(more_ref[0] <= first)
        def _():
            write(None)

    smem, whole = pl.BlockSpec(memory_space=pltpu.SMEM), pl.BlockSpec(memory_space=pltpu.VMEM)
    return pl.pallas_call(
        kernel,
        in_specs=[smem] * 2
        + [whole] * (len(coeffs) + 3)
        + [pl.BlockSpec(memory_space=pl.ANY)],
        out_specs=whole,
        out_shape=jax.ShapeDtypeStruct((total_rows, width), jnp.bfloat16),
        scratch_shapes=[pltpu.VMEM(extra.shape, extra.dtype), pltpu.SemaphoreType.DMA(())],
        compiler_params=vmem(8 * total_rows * width + 2 * chips * limit * width),
        cost_estimate=pl.CostEstimate(
            flops=4 * total_rows * chips * limit * width,
            bytes_accessed=6 * total_rows * width + 2 * chips * limit * width,
            transcendentals=0,
        ),
    )(begin, more, base, code, *coeffs, incoming, extra)


def ring_gather(block, shards):
    chips = shards // 2
    depth = chips // 2
    cycle = list(range(0, chips, 2)) + list(range(chips - 1, 0, -2))
    ahead = [
        (2 * cycle[p] + c, 2 * cycle[(p + 1) % chips] + c) for p in range(chips) for c in range(2)
    ]
    back = [(b, a) for a, b in ahead]
    sibling = [(t, t ^ 1) for t in range(shards)]
    held = {0: block}
    for step in range(1, depth + 1):
        held[-step] = lax.ppermute(held[1 - step], "tensor", ahead)
        if step < chips - depth:
            held[step] = lax.ppermute(held[step - 1], "tensor", back)
    blocks = []
    for piece in held.values():
        blocks += [piece, lax.ppermute(piece, "tensor", sibling)]
    table = np.zeros((shards, shards), np.int32)
    for t in range(shards):
        for i, offset in enumerate(held):
            chip = cycle[(cycle.index(t // 2) + offset) % chips]
            table[t, 2 * i], table[t, 2 * i + 1] = 2 * chip + t % 2, 2 * chip + 1 - t % 2
    places = lax.dynamic_index_in_dim(table, lax.axis_index("tensor"), keepdims=False)
    return blocks, places, held[-1]


def largest_over_groups(value):
    groups = lax.axis_size("groups")
    for shift in range(1, groups):
        other = lax.ppermute(value, "groups", [(g, (g + shift) % groups) for g in range(groups)])
        value = jnp.maximum(value, other)
    return value


def pooled(
    input_rows,
    up_weight,
    adapter_down,
    adapter_up,
    ranks,
    adapter_slot,
    segment_lengths,
    segment_adapter,
):
    shards = lax.axis_size("tensor")
    position = lax.axis_index("tensor").astype(jnp.int32)
    chips = shards // 2
    total_rows = input_rows.shape[0] * shards
    rank_width = adapter_up.shape[1]
    limit = 2 * rank_width
    sibling = [(t, t ^ 1) for t in range(shards)]
    same_core = [list(range(c, shards, 2)) for c in range(2)]

    blocks, places, first = ring_gather(input_rows, shards)
    adapter_up, adapter_down, first = lax.optimization_barrier((adapter_up, adapter_down, first))
    mine, other = split_for_pair(adapter_up[0], (position & 1)[None], chips)
    other = lax.ppermute(other, "tensor", sibling)
    down_pair = (adapter_down[0], lax.ppermute(adapter_down[0], "tensor", sibling))
    gain, choose, fixed, code, begin, full = describe(
        ranks, adapter_slot, segment_lengths, segment_adapter, position[None], total_rows, limit
    )
    fullest = largest_over_groups(full)
    rows, coeff = collect_rows(blocks, places, down_pair, gain)

    def exchange(low, count):
        payload = build_payload(choose, fixed, coeff, mine, other, low, count)
        return lax.all_to_all(
            payload,
            "tensor",
            split_axis=0,
            concat_axis=0,
            axis_index_groups=same_core,
            tiled=True,
        )

    incoming = exchange(0, FIRST_ROWS)
    base = jnp.dot(rows, up_weight, preferred_element_type=jnp.float32)
    coeff, fullest, base = lax.optimization_barrier((coeff, fullest, base))
    own = coeff[:, :rank_width] + coeff[:, rank_width:]
    coeffs = [own]
    for step in range(1, chips):
        hop = [(t, (t + 2 * step) % shards) for t in range(shards)]
        coeffs.append(lax.ppermute(own, "tensor", hop))
    rest = limit - FIRST_ROWS
    extra = lax.cond(
        fullest[0] > FIRST_ROWS,
        lambda: exchange(FIRST_ROWS, rest),
        lambda: jnp.zeros((chips, rest, up_weight.shape[1]), adapter_up.dtype),
    )
    return combine(base, code, begin, fullest, coeffs, incoming, extra)


def gathered(input_rows, up_weight, adapter_down, adapter_up, slot_row, row_rank):
    shards = lax.axis_size("tensor")
    position = lax.axis_index("tensor")
    total_rows = input_rows.shape[0] * shards
    stored, rank_width, hidden = adapter_up.shape
    width = hidden // shards
    slots = shards * stored
    outgoing = jnp.stack(
        [adapter_up[:, :, i * width : (i + 1) * width] for i in range(shards)], axis=0
    )
    incoming = lax.all_to_all(outgoing, "tensor", split_axis=0, concat_axis=0, tiled=True)
    rows = lax.all_gather(input_rows, "tensor", axis=0, tiled=True)
    shrink = jnp.einsum("gf,ojf->ogj", rows, adapter_down, preferred_element_type=jnp.float32)
    own = position * stored + jnp.arange(stored, dtype=jnp.int32)
    inside = jnp.arange(rank_width, dtype=jnp.int32)[None, :] < row_rank[:, None]
    keep = (slot_row[None, :] == own[:, None])[:, :, None] & inside[None]
    scale = ADAPTER_ALPHA / row_rank.astype(jnp.float32)
    own_coeff = jnp.where(keep, shrink * scale[None, :, None], 0.0).astype(jnp.bfloat16)
    base = jnp.dot(rows, up_weight, preferred_element_type=jnp.float32)
    own_coeff, base = lax.optimization_barrier((own_coeff, base))
    coeff = lax.all_gather(own_coeff, "tensor", axis=0, tiled=True)
    placed = coeff.transpose(1, 0, 2).reshape(total_rows, slots * rank_width)
    factors = incoming.reshape(slots * rank_width, width)
    term = jnp.dot(placed, factors, preferred_element_type=jnp.float32)
    return (base + term).astype(jnp.bfloat16)


def on_device(
    input_rows,
    up_weight,
    adapter_down,
    adapter_up,
    ranks,
    adapter_slot,
    segment_lengths,
    segment_adapter,
):
    shards = lax.axis_size("tensor")
    stored, rank_width, _ = adapter_up.shape
    tiled = up_weight.shape[1] % 128 == 0 and input_rows.shape[0] % 16 == 0 and rank_width == 64
    if shards == POOLED_SHARDS and stored == 1 and tiled:
        return pooled(
            input_rows,
            up_weight,
            adapter_down,
            adapter_up,
            ranks,
            adapter_slot,
            segment_lengths,
            segment_adapter,
        )
    slot_row, row_rank = row_tables(
        input_rows.shape[0] * shards, ranks, adapter_slot, segment_lengths, segment_adapter
    )
    return gathered(input_rows, up_weight, adapter_down, adapter_up, slot_row, row_rank)


def solution(mesh):
    placed = (
        P(("groups", "tensor"), None),
        P(None, "tensor"),
        P(("groups", "tensor"), None, None),
        P(("groups", "tensor"), None, None),
        P("groups"),
        P("groups"),
        P("groups"),
        P("groups"),
    )
    return jax.shard_map(
        on_device, mesh=mesh, in_specs=placed, out_specs=P("groups", "tensor"), check_vma=False
    )
```

```python
import jax
import jax.numpy as jnp
import numpy as np
from jax import lax
from jax.experimental import pallas as pl
from jax.experimental.pallas import tpu as pltpu
from jax.sharding import PartitionSpec as P

ADAPTER_ALPHA = 32.0
POOLED_SHARDS = 16
FIRST_ROWS = 80


def row_tables(row_count, ranks, adapter_slot, segment_lengths, segment_adapter):
    seg_ends = jnp.cumsum(segment_lengths)
    positions = jnp.arange(row_count, dtype=jnp.int32)
    seg_row = jnp.sum((seg_ends[None, :] <= positions[:, None]).astype(jnp.int32), axis=1)
    seg_pick = (
        seg_row[:, None] == jnp.arange(segment_lengths.shape[0], dtype=jnp.int32)[None, :]
    ).astype(jnp.int32)
    adapter_row = jnp.sum(seg_pick * segment_adapter[None, :], axis=1)
    pool_pick = (
        adapter_row[:, None] == jnp.arange(ranks.shape[0], dtype=jnp.int32)[None, :]
    ).astype(jnp.int32)
    slot_row = jnp.sum(pool_pick * adapter_slot[None, :], axis=1)
    row_rank_values = jnp.sum(pool_pick * ranks[None, :], axis=1)
    return (slot_row, row_rank_values)


def vmem(buffers):
    return pltpu.CompilerParams(vmem_limit_bytes=buffers + (8 << 20))


def split_for_pair(up_factor, core, chips):
    rank_width, hidden = up_factor.shape
    width = hidden // (2 * chips)

    def kernel(core_ref, source, mine, other, sems):
        copies = []
        for q in range(chips):
            for target, half in ((mine, core_ref[0]), (other, 1 - core_ref[0])):
                start = pl.multiple_of((2 * q + half) * width, width)
                copies.append(
                    pltpu.make_async_copy(
                        source.at[:, pl.ds(start, width)], target.at[q], sems.at[len(copies)]
                    )
                )
        for copy in copies:
            copy.start()
        for copy in copies:
            copy.wait()

    block = jax.ShapeDtypeStruct((chips, rank_width, width), up_factor.dtype)
    return pl.pallas_call(
        kernel,
        in_specs=[pl.BlockSpec(memory_space=pltpu.SMEM), pl.BlockSpec(memory_space=pl.ANY)],
        out_specs=[pl.BlockSpec(memory_space=pltpu.VMEM)] * 2,
        out_shape=[block, block],
        scratch_shapes=[pltpu.SemaphoreType.DMA((2 * chips,))],
        compiler_params=vmem(2 * rank_width * hidden),
        cost_estimate=pl.CostEstimate(
            flops=0, bytes_accessed=4 * rank_width * hidden, transcendentals=0
        ),
    )(core, up_factor)


def describe(ranks, adapter_slot, segment_lengths, segment_adapter, position, total_rows, limit):
    slots, segments = ranks.shape[0], segment_lengths.shape[0]
    rank_width = limit // 2
    shift = rank_width.bit_length() - 1

    def kernel(
        ranks_ref, home_ref, length_ref, adapter_ref, position_ref,
        gain_ref, own_ref, choose_ref, live_ref, fixed_ref, code_ref, begin_ref, full_ref,
        rank_of, rows_of, used, factor, order,
    ):
        for a in range(slots):
            rows_of[a] = 0
            rank_of[home_ref[a]] = ranks_ref[a]
        starts, start = [], jnp.int32(0)
        for i in range(segments):
            slot = home_ref[adapter_ref[i]]
            starts.append((start, start + length_ref[i], slot))
            order[i] = rows_of[slot] - start
            rows_of[slot] = rows_of[slot] + length_ref[i]
            start = start + length_ref[i]
        full = jnp.int32(0)
        for s in range(slots):
            used[s] = jnp.minimum(rows_of[s], rank_of[s])
            factor[s] = (rank_of[s] < rows_of[s]).astype(jnp.int32)
            begin_ref[s] = used[s - 1] if s % 2 else jnp.int32(0)
            if s % 2:
                full = jnp.maximum(full, used[s - 1] + used[s])
        full_ref[0] = full

        def tables(row):
            spot, code = jnp.zeros_like(row), jnp.zeros_like(row)
            for i, (low, high, slot) in enumerate(starts):
                hit = (row >= low) & (row < high)
                spot = jnp.where(hit, row + (order[i] + begin_ref[slot]), spot)
                code = jnp.where(hit, slot + 32 * factor[slot] + 64 * rank_of[slot], code)
            return spot, code & 31, (code >> 5) & 1, code >> 6

        here = position_ref[0]
        spot, slot, by_factor, _ = tables(lax.broadcasted_iota(jnp.int32, (total_rows, limit), 0))
        code_ref[...] = slot + 32 * by_factor + 64 * spot

        lane = lax.broadcasted_iota(jnp.int32, (total_rows // 2, limit), 1)
        row = lax.broadcasted_iota(jnp.int32, (total_rows // 2, limit), 0)
        _, slot, _, rank = tables(row + (lane >> shift) * (total_rows // 2))
        own_ref[...] = jnp.where(slot == here, 1.0, 0.0)
        scale = ADAPTER_ALPHA / rank.astype(jnp.float32)
        inside = ((slot >> 1) == (here >> 1)) & ((lane & (rank_width - 1)) < rank)
        gain_ref[...] = jnp.where(inside, scale, 0.0)

        spot, slot, by_factor, _ = tables(lax.broadcasted_iota(jnp.int32, (8, total_rows), 1))
        mine = ((slot >> 1) == (here >> 1)) & (by_factor == 0)
        spot = jnp.broadcast_to(jnp.where(mine, spot, -1)[:1], (limit, total_rows))
        line = lax.broadcasted_iota(jnp.int32, (limit, total_rows), 0)
        choose_ref[...] = jnp.where(line == spot, 1.0, 0.0).astype(jnp.bfloat16)

        line = lax.broadcasted_iota(jnp.int32, (limit, limit), 0)
        lane = lax.broadcasted_iota(jnp.int32, (limit, limit), 1)
        half, column = lane >> shift, lane & (rank_width - 1)
        other = here ^ 1
        begin = jnp.where(half == 0, begin_ref[here], begin_ref[other])
        many = jnp.where(half == 0, used[here], used[other])
        kind = jnp.where(half == 0, factor[here], factor[other])
        held = (line == begin + column) & (column < many) & (kind == 1)
        fixed_ref[...] = jnp.where(held, 1.0, 0.0).astype(jnp.bfloat16)
        live = (line >= begin) & (line < begin + many) & (kind == 0)
        live_ref[...] = jnp.where(live, 1.0, 0.0)

    smem, whole = pl.BlockSpec(memory_space=pltpu.SMEM), pl.BlockSpec(memory_space=pltpu.VMEM)
    return pl.pallas_call(
        kernel,
        in_specs=[smem] * 5,
        out_specs=[whole] * 6 + [smem] * 2,
        out_shape=[
            jax.ShapeDtypeStruct((total_rows // 2, limit), jnp.float32),
            jax.ShapeDtypeStruct((total_rows // 2, limit), jnp.float32),
            jax.ShapeDtypeStruct((limit, total_rows), jnp.bfloat16),
            jax.ShapeDtypeStruct((limit, limit), jnp.float32),
            jax.ShapeDtypeStruct((limit, limit), jnp.bfloat16),
            jax.ShapeDtypeStruct((total_rows, limit), jnp.int32),
            jax.ShapeDtypeStruct((slots,), jnp.int32),
            jax.ShapeDtypeStruct((1,), jnp.int32),
        ],
        scratch_shapes=[pltpu.SMEM((slots,), jnp.int32)] * 4 + [pltpu.SMEM((segments,), jnp.int32)],
        compiler_params=vmem(16 * total_rows * limit),
        cost_estimate=pl.CostEstimate(
            flops=200 * total_rows * limit, bytes_accessed=16 * total_rows * limit, transcendentals=0
        ),
    )(ranks, adapter_slot, segment_lengths, segment_adapter, position)


def collect_rows(blocks, places, core, own_down, other_down, own):
    count = len(blocks)
    height, features = blocks[0].shape
    height = height // 2
    rank_width = other_down.shape[0]
    half_rows = own.shape[0]
    chunk = 1024 if features % 1024 == 0 else features
    chunks = features // chunk

    def kernel(places_ref, core_ref, own_ref, *refs):
        sources, own_down_ref, other_down_ref = refs[:count], refs[count], refs[count + 1]
        rows_ref, shrink_ref, downs, sems = refs[count + 2 :]
        groups = []
        for k in range(chunks):
            columns = pl.ds(k * chunk, chunk)
            offset = pl.multiple_of(core_ref[0] * features + k * chunk, chunk)
            copies = [
                pltpu.make_async_copy(
                    own_down_ref.at[:, pl.ds(offset, chunk)],
                    downs.at[pl.ds(0, rank_width), columns],
                    sems.at[k, 2 * count],
                ),
                pltpu.make_async_copy(
                    other_down_ref.at[:, columns],
                    downs.at[pl.ds(rank_width, rank_width), columns],
                    sems.at[k, 2 * count + 1],
                ),
            ]
            for i in range(2 * count):
                start = pl.multiple_of(places_ref[i] * height, height)
                copies.append(
                    pltpu.make_async_copy(
                        sources[i // 2].at[pl.ds(i % 2 * height, height), columns],
                        rows_ref.at[pl.ds(start, height), columns],
                        sems.at[k, i],
                    )
                )
            groups.append(copies)
            for copy in copies:
                copy.start()
        shrink = jnp.zeros((2 * half_rows, 2 * rank_width), jnp.float32)
        for k in range(chunks):
            for copy in groups[k]:
                copy.wait()
            columns = pl.ds(k * chunk, chunk)
            shrink = shrink + lax.dot_general(
                rows_ref[:, columns],
                downs[:, columns],
                (((1,), (1,)), ((), ())),
                preferred_element_type=jnp.float32,
            )
        top, bottom = shrink[:half_rows], shrink[half_rows:]
        first = jnp.concatenate([top[:, :rank_width], bottom[:, :rank_width]], axis=1)
        second = jnp.concatenate([top[:, rank_width:], bottom[:, rank_width:]], axis=1)
        shrink_ref[...] = jnp.where(own_ref[...] > 0.5, first, second)

    smem, whole = pl.BlockSpec(memory_space=pltpu.SMEM), pl.BlockSpec(memory_space=pltpu.VMEM)
    rows = 2 * count * height
    return pl.pallas_call(
        kernel,
        in_specs=[smem, smem, whole] + [pl.BlockSpec(memory_space=pl.ANY)] * (count + 2),
        out_specs=[whole] * 2,
        out_shape=[
            jax.ShapeDtypeStruct((rows, features), blocks[0].dtype),
            jax.ShapeDtypeStruct(own.shape, jnp.float32),
        ],
        scratch_shapes=[
            pltpu.VMEM((2 * rank_width, features), own_down.dtype),
            pltpu.SemaphoreType.DMA((chunks, 2 * count + 2)),
        ],
        compiler_params=vmem(4 * rows * features),
        cost_estimate=pl.CostEstimate(
            flops=4 * rows * features * rank_width,
            bytes_accessed=4 * rows * features,
            transcendentals=0,
        ),
    )(places, core, own, *blocks, own_down, other_down)


def build_payload(choose, live, fixed, coeff, mine, other, first, count):
    chips, rank_width, width = mine.shape

    half_rows = coeff.shape[0]

    def kernel(choose_ref, live_ref, fixed_ref, coeff_ref, mine_ref, other_ref, out_ref):
        lines = pl.ds(first, count)
        folded = coeff_ref[...]
        top = jnp.dot(choose_ref[lines, :half_rows], folded, preferred_element_type=jnp.float32)
        low = jnp.dot(choose_ref[lines, half_rows:], folded, preferred_element_type=jnp.float32)
        chosen = top[:, :rank_width] + low[:, rank_width:]
        select = jnp.concatenate([chosen, chosen], axis=1) * live_ref[lines]
        select = (select + fixed_ref[lines].astype(jnp.float32)).astype(jnp.bfloat16)

        @pl.loop(0, chips)
        def _(q):
            out_ref[q] = jnp.dot(
                select,
                jnp.concatenate([mine_ref[q], other_ref[q]], axis=0),
                preferred_element_type=jnp.float32,
            ).astype(out_ref.dtype)

    return pl.pallas_call(
        kernel,
        in_specs=[pl.BlockSpec(memory_space=pltpu.VMEM)] * 6,
        out_specs=pl.BlockSpec(memory_space=pltpu.VMEM),
        out_shape=jax.ShapeDtypeStruct((chips, count, width), mine.dtype),
        compiler_params=vmem(4 * chips * width * (2 * rank_width + count)),
        cost_estimate=pl.CostEstimate(
            flops=4 * chips * count * rank_width * width,
            bytes_accessed=2 * chips * width * (2 * rank_width + count),
            transcendentals=0,
        ),
    )(choose, live, fixed, coeff, mine, other)


def combine(base, code, begin, more, coeff, incoming, extra):
    total_rows, width = base.shape
    chips, first, _ = incoming.shape
    second = extra.shape[1]
    limit = first + second
    rank_width = limit // 2
    shift = rank_width.bit_length() - 1
    tile = 256 if width % 256 == 0 else 128

    def kernel(
        begin_ref, more_ref, base_ref, code_ref, coeff_ref, incoming_ref, extra_ref,
        out_ref, late, sem,
    ):
        fetch = pltpu.make_async_copy(extra_ref, late, sem)
        folded = coeff_ref[...].astype(jnp.float32)
        both = jnp.concatenate(
            [
                jnp.concatenate([part, part], axis=1)
                for part in (folded[:, :rank_width], folded[:, rank_width:])
            ],
            axis=0,
        )
        code_value = code_ref[...]
        slot, by_factor, spot = code_value & 31, (code_value >> 5) & 1, code_value >> 6
        lane = lax.broadcasted_iota(jnp.int32, (total_rows, limit), 1)
        owned = jnp.where(by_factor == 1, slot, -1) - (lane >> shift)
        finished = jnp.where(by_factor == 0, spot, -1)[:, :1]
        finished_chip = (slot >> 1)[:, :1]

        def weights(low, count):
            target = finished - low
            target = jnp.where((target >= 0) & (target < count), finished_chip * count + target, -1)
            wide = lax.broadcasted_iota(jnp.int32, (total_rows, chips * count), 1)
            total = jnp.where(wide == target, 1.0, 0.0)
            line = lax.broadcasted_iota(jnp.int32, (limit, chips * count), 0)
            place = lax.broadcasted_iota(jnp.int32, (limit, chips * count), 1)
            for q in range(chips):
                goal = jnp.where(
                    line < rank_width, line, line - rank_width + begin_ref[2 * q + 1]
                ) - low
                moved = (goal >= 0) & (goal < count) & (place == q * count + goal)
                moved = jnp.where(moved, 1.0, 0.0).astype(jnp.bfloat16)
                part = jnp.where(owned == 2 * q, both, 0.0).astype(jnp.bfloat16)
                total = total + jnp.dot(part, moved, preferred_element_type=jnp.float32)
            return total.astype(jnp.bfloat16)

        near = weights(0, first)

        def write(far):
            @pl.loop(0, width // tile)
            def _(i):
                columns = pl.ds(pl.multiple_of(i * tile, tile), tile)
                block = incoming_ref[:, :, columns].reshape(chips * first, tile)
                total = jnp.dot(near, block, preferred_element_type=jnp.float32)
                total += base_ref[:, columns]
                if far is not None:
                    block = late[:, :, columns].reshape(chips * second, tile)
                    total += jnp.dot(far, block, preferred_element_type=jnp.float32)
                out_ref[:, columns] = total.astype(out_ref.dtype)

        @pl.when(more_ref[0] > first)
        def _():
            fetch.start()
            far = weights(first, second)
            fetch.wait()
            write(far)

        @pl.when(more_ref[0] <= first)
        def _():
            write(None)

    smem, whole = pl.BlockSpec(memory_space=pltpu.SMEM), pl.BlockSpec(memory_space=pltpu.VMEM)
    return pl.pallas_call(
        kernel,
        in_specs=[smem] * 2
        + [whole] * 4
        + [pl.BlockSpec(memory_space=pl.ANY)],
        out_specs=whole,
        out_shape=jax.ShapeDtypeStruct((total_rows, width), jnp.bfloat16),
        scratch_shapes=[pltpu.VMEM(extra.shape, extra.dtype), pltpu.SemaphoreType.DMA(())],
        compiler_params=vmem(8 * total_rows * width + 2 * chips * limit * width),
        cost_estimate=pl.CostEstimate(
            flops=4 * total_rows * chips * limit * width,
            bytes_accessed=6 * total_rows * width + 2 * chips * limit * width,
            transcendentals=0,
        ),
    )(begin, more, base, code, coeff, incoming, extra)


def ring_gather(block, shards, halfway):
    chips = shards // 2
    depth = chips // 2
    cycle = list(range(0, chips, 2)) + list(range(chips - 1, 0, -2))
    ahead = [
        (2 * cycle[p] + c, 2 * cycle[(p + 1) % chips] + c) for p in range(chips) for c in range(2)
    ]
    back = [(b, a) for a, b in ahead]
    held = {0: block}
    for step in range(1, depth + 1):
        held[-step] = lax.ppermute(held[1 - step], "tensor", ahead)
        if step < chips - depth:
            held[step] = lax.ppermute(held[step - 1], "tensor", back)
        held[-step] = halfway(step, held[-step])
    table = np.zeros((shards, shards), np.int32)
    for t in range(shards):
        for i, offset in enumerate(held):
            chip = cycle[(cycle.index(t // 2) + offset) % chips]
            table[t, 2 * i], table[t, 2 * i + 1] = 2 * chip + t % 2, 2 * chip + 1 - t % 2
    places = lax.dynamic_index_in_dim(table, lax.axis_index("tensor"), keepdims=False)
    return list(held.values()), places


def largest_over_groups(value):
    groups = lax.axis_size("groups")
    for shift in range(1, groups):
        other = lax.ppermute(value, "groups", [(g, (g + shift) % groups) for g in range(groups)])
        value = jnp.maximum(value, other)
    return value


def pooled(
    input_rows,
    up_weight,
    adapter_down,
    adapter_up,
    ranks,
    adapter_slot,
    segment_lengths,
    segment_adapter,
):
    shards = lax.axis_size("tensor")
    position = lax.axis_index("tensor").astype(jnp.int32)
    chips = shards // 2
    total_rows = input_rows.shape[0] * shards
    rank_width = adapter_up.shape[1]
    limit = 2 * rank_width
    sibling = [(t, t ^ 1) for t in range(shards)]
    same_core = [list(range(c, shards, 2)) for c in range(2)]

    core = position & 1
    features = input_rows.shape[1] // 2

    def swap(value):
        keep = lax.dynamic_slice_in_dim(value, core * features, features, 1)
        send = lax.dynamic_slice_in_dim(value, (1 - core) * features, features, 1)
        return keep, lax.ppermute(send, "tensor", sibling)

    block = jnp.concatenate(swap(input_rows), axis=0)
    side = {}

    def halfway(step, piece):
        if step == 1:
            up, down, piece = lax.optimization_barrier((adapter_up[0], adapter_down[0], piece))
            side["up"] = split_for_pair(up, core[None], chips)
            side["down"] = swap(down)[1]
            side["tables"] = describe(
                ranks, adapter_slot, segment_lengths, segment_adapter, position[None],
                total_rows, limit,
            )
        if step == 2:
            piece, side["up"], side["tables"] = lax.optimization_barrier(
                (piece, side["up"], side["tables"])
            )
        return piece

    blocks, places = ring_gather(block, shards, halfway)
    mine, other = side["up"]
    other = lax.ppermute(other, "tensor", sibling)
    gain, own, choose, live, fixed, code, begin, full = side["tables"]
    fullest = largest_over_groups(full)
    rows, shrink = collect_rows(
        blocks, places, core[None], adapter_down[0], side["down"], own
    )
    shrink = shrink + lax.ppermute(shrink, "tensor", sibling)
    rows_other = lax.ppermute(rows, "tensor", sibling)
    coeff = (shrink * gain).astype(jnp.bfloat16)
    every, bit = coeff, 2
    while bit < shards:
        every = every + lax.ppermute(every, "tensor", [(t, t ^ bit) for t in range(shards)])
        bit *= 2

    def payload(low, count):
        return build_payload(choose, live, fixed, coeff, mine, other, low, count)

    def exchange(value):
        return lax.all_to_all(
            value,
            "tensor",
            split_axis=0,
            concat_axis=0,
            axis_index_groups=same_core,
            tiled=True,
        )

    near = payload(0, FIRST_ROWS)
    near, every, rows, rows_other = lax.optimization_barrier((near, every, rows, rows_other))
    incoming = exchange(near)
    halves = [jnp.where(core == c, rows, rows_other) for c in range(2)]
    base = jnp.dot(
        jnp.concatenate(halves, axis=1), up_weight, preferred_element_type=jnp.float32
    )
    fullest, base = lax.optimization_barrier((fullest, base))
    rest = limit - FIRST_ROWS
    extra = lax.cond(
        fullest[0] > FIRST_ROWS,
        lambda: exchange(payload(FIRST_ROWS, rest)),
        lambda: jnp.zeros((chips, rest, up_weight.shape[1]), adapter_up.dtype),
    )
    return combine(base, code, begin, fullest, every, incoming, extra)


def gathered(input_rows, up_weight, adapter_down, adapter_up, slot_row, row_rank):
    shards = lax.axis_size("tensor")
    position = lax.axis_index("tensor")
    total_rows = input_rows.shape[0] * shards
    stored, rank_width, hidden = adapter_up.shape
    width = hidden // shards
    slots = shards * stored
    outgoing = jnp.stack(
        [adapter_up[:, :, i * width : (i + 1) * width] for i in range(shards)], axis=0
    )
    incoming = lax.all_to_all(outgoing, "tensor", split_axis=0, concat_axis=0, tiled=True)
    rows = lax.all_gather(input_rows, "tensor", axis=0, tiled=True)
    shrink = jnp.einsum("gf,ojf->ogj", rows, adapter_down, preferred_element_type=jnp.float32)
    own = position * stored + jnp.arange(stored, dtype=jnp.int32)
    inside = jnp.arange(rank_width, dtype=jnp.int32)[None, :] < row_rank[:, None]
    keep = (slot_row[None, :] == own[:, None])[:, :, None] & inside[None]
    scale = ADAPTER_ALPHA / row_rank.astype(jnp.float32)
    own_coeff = jnp.where(keep, shrink * scale[None, :, None], 0.0).astype(jnp.bfloat16)
    base = jnp.dot(rows, up_weight, preferred_element_type=jnp.float32)
    own_coeff, base = lax.optimization_barrier((own_coeff, base))
    coeff = lax.all_gather(own_coeff, "tensor", axis=0, tiled=True)
    placed = coeff.transpose(1, 0, 2).reshape(total_rows, slots * rank_width)
    factors = incoming.reshape(slots * rank_width, width)
    term = jnp.dot(placed, factors, preferred_element_type=jnp.float32)
    return (base + term).astype(jnp.bfloat16)


def on_device(
    input_rows,
    up_weight,
    adapter_down,
    adapter_up,
    ranks,
    adapter_slot,
    segment_lengths,
    segment_adapter,
):
    shards = lax.axis_size("tensor")
    stored, rank_width, _ = adapter_up.shape
    tiled = up_weight.shape[1] % 128 == 0 and input_rows.shape[0] % 16 == 0 and rank_width == 64
    tiled = tiled and input_rows.shape[1] % 256 == 0 and input_rows.shape[0] * shards <= 256
    if shards == POOLED_SHARDS and stored == 1 and tiled:
        return pooled(
            input_rows,
            up_weight,
            adapter_down,
            adapter_up,
            ranks,
            adapter_slot,
            segment_lengths,
            segment_adapter,
        )
    slot_row, row_rank = row_tables(
        input_rows.shape[0] * shards, ranks, adapter_slot, segment_lengths, segment_adapter
    )
    return gathered(input_rows, up_weight, adapter_down, adapter_up, slot_row, row_rank)


def solution(mesh):
    placed = (
        P(("groups", "tensor"), None),
        P(None, "tensor"),
        P(("groups", "tensor"), None, None),
        P(("groups", "tensor"), None, None),
        P("groups"),
        P("groups"),
        P("groups"),
        P("groups"),
    )
    return jax.shard_map(
        on_device, mesh=mesh, in_specs=placed, out_specs=P("groups", "tensor"), check_vma=False
    )
```

```python
import jax
import jax.numpy as jnp
import numpy as np
from jax import lax
from jax.experimental import pallas as pl
from jax.experimental.pallas import tpu as pltpu
from jax.sharding import PartitionSpec as P

ADAPTER_ALPHA = 32.0
POOLED_SHARDS = 16
FIRST_ROWS = 80


def row_tables(row_count, ranks, adapter_slot, segment_lengths, segment_adapter):
    seg_ends = jnp.cumsum(segment_lengths)
    positions = jnp.arange(row_count, dtype=jnp.int32)
    seg_row = jnp.sum((seg_ends[None, :] <= positions[:, None]).astype(jnp.int32), axis=1)
    seg_pick = (
        seg_row[:, None] == jnp.arange(segment_lengths.shape[0], dtype=jnp.int32)[None, :]
    ).astype(jnp.int32)
    adapter_row = jnp.sum(seg_pick * segment_adapter[None, :], axis=1)
    pool_pick = (
        adapter_row[:, None] == jnp.arange(ranks.shape[0], dtype=jnp.int32)[None, :]
    ).astype(jnp.int32)
    slot_row = jnp.sum(pool_pick * adapter_slot[None, :], axis=1)
    row_rank_values = jnp.sum(pool_pick * ranks[None, :], axis=1)
    return (slot_row, row_rank_values)


def vmem(buffers):
    return pltpu.CompilerParams(vmem_limit_bytes=buffers + (8 << 20))


def split_for_pair(up_factor, down_factor, core, chips):
    rank_width, hidden = up_factor.shape
    width = hidden // (2 * chips)
    features = down_factor.shape[1] // 2

    def kernel(core_ref, source, down, mine, other, half_down, sems):
        core = core_ref[0]
        start = pl.multiple_of((1 - core) * features, features)
        copies = [
            pltpu.make_async_copy(
                down.at[:, pl.ds(start, features)], half_down, sems.at[2 * chips]
            )
        ]
        for q in range(chips):
            for i, (target, half) in enumerate(((other, 1 - core), (mine, core))):
                start = pl.multiple_of((2 * q + half) * width, width)
                copies.append(
                    pltpu.make_async_copy(
                        source.at[:, pl.ds(start, width)], target.at[q], sems.at[2 * q + i]
                    )
                )
        for copy in copies:
            copy.start()
        for copy in copies:
            copy.wait()

    block = jax.ShapeDtypeStruct((chips, rank_width, width), up_factor.dtype)
    return pl.pallas_call(
        kernel,
        in_specs=[pl.BlockSpec(memory_space=pltpu.SMEM)]
        + [pl.BlockSpec(memory_space=pltpu.HBM)] * 2,
        out_specs=[pl.BlockSpec(memory_space=pltpu.VMEM)] * 3,
        out_shape=[
            block, block, jax.ShapeDtypeStruct((rank_width, features), down_factor.dtype)
        ],
        scratch_shapes=[pltpu.SemaphoreType.DMA((2 * chips + 1,))],
        compiler_params=vmem(2 * rank_width * (hidden + features)),
        cost_estimate=pl.CostEstimate(
            flops=0, bytes_accessed=4 * rank_width * hidden, transcendentals=0
        ),
    )(core, up_factor, down_factor)


def describe(ranks, adapter_slot, segment_lengths, segment_adapter, position, total_rows, limit):
    slots, segments = ranks.shape[0], segment_lengths.shape[0]
    rank_width = limit // 2
    shift = rank_width.bit_length() - 1

    def kernel(
        ranks_in, home_in, length_in, adapter_in, position_ref,
        gain_ref, own_ref, choose_ref, live_ref, fixed_ref, code_ref, begin_ref, full_ref,
        rank_of, rows_of, used, factor, order, ranks_ref, home_ref, length_ref, adapter_ref, sems,
    ):
        pairs = zip(
            (ranks_in, home_in, length_in, adapter_in),
            (ranks_ref, home_ref, length_ref, adapter_ref),
        )
        copies = [
            pltpu.make_async_copy(source, target, sems.at[i])
            for i, (source, target) in enumerate(pairs)
        ]
        for copy in copies:
            copy.start()
        for copy in copies:
            copy.wait()
        for a in range(slots):
            rows_of[a] = 0
            rank_of[home_ref[a]] = ranks_ref[a]
        starts, start = [], jnp.int32(0)
        for i in range(segments):
            slot = home_ref[adapter_ref[i]]
            starts.append((start, start + length_ref[i], slot))
            order[i] = rows_of[slot] - start
            rows_of[slot] = rows_of[slot] + length_ref[i]
            start = start + length_ref[i]
        full = jnp.int32(0)
        for s in range(slots):
            used[s] = jnp.minimum(rows_of[s], rank_of[s])
            factor[s] = (rank_of[s] < rows_of[s]).astype(jnp.int32)
            begin_ref[s] = used[s - 1] if s % 2 else jnp.int32(0)
            if s % 2:
                full = jnp.maximum(full, used[s - 1] + used[s])
        full_ref[0] = full

        def tables(row):
            spot, code = jnp.zeros_like(row), jnp.zeros_like(row)
            for i, (low, high, slot) in enumerate(starts):
                hit = (row >= low) & (row < high)
                spot = jnp.where(hit, row + (order[i] + begin_ref[slot]), spot)
                code = jnp.where(hit, slot + 32 * factor[slot] + 64 * rank_of[slot], code)
            return spot, code & 31, (code >> 5) & 1, code >> 6

        here = position_ref[0]
        spot, slot, by_factor, _ = tables(lax.broadcasted_iota(jnp.int32, (total_rows, limit), 0))
        code_ref[...] = slot + 32 * by_factor + 64 * spot

        lane = lax.broadcasted_iota(jnp.int32, (total_rows // 2, limit), 1)
        row = lax.broadcasted_iota(jnp.int32, (total_rows // 2, limit), 0)
        _, slot, _, rank = tables(row + (lane >> shift) * (total_rows // 2))
        own_ref[...] = jnp.where(slot == here, 1.0, 0.0)
        scale = ADAPTER_ALPHA / rank.astype(jnp.float32)
        inside = ((slot >> 1) == (here >> 1)) & ((lane & (rank_width - 1)) < rank)
        gain_ref[...] = jnp.where(inside, scale, 0.0)

        spot, slot, by_factor, _ = tables(lax.broadcasted_iota(jnp.int32, (8, total_rows), 1))
        mine = ((slot >> 1) == (here >> 1)) & (by_factor == 0)
        spot = jnp.broadcast_to(jnp.where(mine, spot, -1)[:1], (limit, total_rows))
        line = lax.broadcasted_iota(jnp.int32, (limit, total_rows), 0)
        choose_ref[...] = jnp.where(line == spot, 1.0, 0.0).astype(jnp.bfloat16)

        line = lax.broadcasted_iota(jnp.int32, (limit, limit), 0)
        lane = lax.broadcasted_iota(jnp.int32, (limit, limit), 1)
        half, column = lane >> shift, lane & (rank_width - 1)
        other = here ^ 1
        begin = jnp.where(half == 0, begin_ref[here], begin_ref[other])
        many = jnp.where(half == 0, used[here], used[other])
        kind = jnp.where(half == 0, factor[here], factor[other])
        held = (line == begin + column) & (column < many) & (kind == 1)
        fixed_ref[...] = jnp.where(held, 1.0, 0.0).astype(jnp.bfloat16)
        live = (line >= begin) & (line < begin + many) & (kind == 0)
        live_ref[...] = jnp.where(live, 1.0, 0.0)

    smem, whole = pl.BlockSpec(memory_space=pltpu.SMEM), pl.BlockSpec(memory_space=pltpu.VMEM)
    return pl.pallas_call(
        kernel,
        in_specs=[pl.BlockSpec(memory_space=pltpu.HBM)] * 4 + [smem],
        out_specs=[whole] * 6 + [smem] * 2,
        out_shape=[
            jax.ShapeDtypeStruct((total_rows // 2, limit), jnp.float32),
            jax.ShapeDtypeStruct((total_rows // 2, limit), jnp.float32),
            jax.ShapeDtypeStruct((limit, total_rows), jnp.bfloat16),
            jax.ShapeDtypeStruct((limit, limit), jnp.float32),
            jax.ShapeDtypeStruct((limit, limit), jnp.bfloat16),
            jax.ShapeDtypeStruct((total_rows, limit), jnp.int32),
            jax.ShapeDtypeStruct((slots,), jnp.int32),
            jax.ShapeDtypeStruct((1,), jnp.int32),
        ],
        scratch_shapes=[pltpu.SMEM((slots,), jnp.int32)] * 4
        + [pltpu.SMEM((segments,), jnp.int32)]
        + [pltpu.SMEM((slots,), jnp.int32)] * 2
        + [pltpu.SMEM((segments,), jnp.int32)] * 2
        + [pltpu.SemaphoreType.DMA((4,))],
        compiler_params=vmem(16 * total_rows * limit),
        cost_estimate=pl.CostEstimate(
            flops=200 * total_rows * limit, bytes_accessed=16 * total_rows * limit, transcendentals=0
        ),
    )(ranks, adapter_slot, segment_lengths, segment_adapter, position)


def collect_rows(blocks, places, core, own_down, other_down, own):
    count = len(blocks)
    height, features = blocks[0].shape
    height = height // 2
    rank_width = other_down.shape[0]
    half_rows = own.shape[0]
    chunk = 1024 if features % 1024 == 0 else features
    chunks = features // chunk

    def kernel(places_ref, core_ref, own_ref, *refs):
        sources, own_down_ref, other_down_ref = refs[:count], refs[count], refs[count + 1]
        rows_ref, shrink_ref, downs, sems = refs[count + 2 :]
        groups = []
        for k in range(chunks):
            columns = pl.ds(k * chunk, chunk)
            offset = pl.multiple_of(core_ref[0] * features + k * chunk, chunk)
            copies = [
                pltpu.make_async_copy(
                    own_down_ref.at[:, pl.ds(offset, chunk)],
                    downs.at[pl.ds(0, rank_width), columns],
                    sems.at[k, 2 * count],
                ),
                pltpu.make_async_copy(
                    other_down_ref.at[:, columns],
                    downs.at[pl.ds(rank_width, rank_width), columns],
                    sems.at[k, 2 * count + 1],
                ),
            ]
            for i in range(2 * count):
                start = pl.multiple_of(places_ref[i] * height, height)
                copies.append(
                    pltpu.make_async_copy(
                        sources[i // 2].at[pl.ds(i % 2 * height, height), columns],
                        rows_ref.at[pl.ds(start, height), columns],
                        sems.at[k, i],
                    )
                )
            groups.append(copies)
            for copy in copies:
                copy.start()
        shrink = jnp.zeros((2 * half_rows, 2 * rank_width), jnp.float32)
        for k in range(chunks):
            for copy in groups[k]:
                copy.wait()
            columns = pl.ds(k * chunk, chunk)
            shrink = shrink + lax.dot_general(
                rows_ref[:, columns],
                downs[:, columns],
                (((1,), (1,)), ((), ())),
                preferred_element_type=jnp.float32,
            )
        top, bottom = shrink[:half_rows], shrink[half_rows:]
        first = jnp.concatenate([top[:, :rank_width], bottom[:, :rank_width]], axis=1)
        second = jnp.concatenate([top[:, rank_width:], bottom[:, rank_width:]], axis=1)
        shrink_ref[...] = jnp.where(own_ref[...] > 0.5, first, second)

    smem, whole = pl.BlockSpec(memory_space=pltpu.SMEM), pl.BlockSpec(memory_space=pltpu.VMEM)
    rows = 2 * count * height
    return pl.pallas_call(
        kernel,
        in_specs=[smem, smem, whole] + [pl.BlockSpec(memory_space=pl.ANY)] * (count + 2),
        out_specs=[whole] * 2,
        out_shape=[
            jax.ShapeDtypeStruct((rows, features), blocks[0].dtype),
            jax.ShapeDtypeStruct(own.shape, jnp.float32),
        ],
        scratch_shapes=[
            pltpu.VMEM((2 * rank_width, features), own_down.dtype),
            pltpu.SemaphoreType.DMA((chunks, 2 * count + 2)),
        ],
        compiler_params=vmem(4 * rows * features),
        cost_estimate=pl.CostEstimate(
            flops=4 * rows * features * rank_width,
            bytes_accessed=4 * rows * features,
            transcendentals=0,
        ),
    )(places, core, own, *blocks, own_down, other_down)


def build_payload(choose, live, fixed, coeff, mine, other, first, count):
    chips, rank_width, width = mine.shape

    half_rows = coeff.shape[0]

    def kernel(choose_ref, live_ref, fixed_ref, coeff_ref, mine_ref, other_ref, out_ref):
        lines = pl.ds(first, count)
        folded = coeff_ref[...]
        top = jnp.dot(choose_ref[lines, :half_rows], folded, preferred_element_type=jnp.float32)
        low = jnp.dot(choose_ref[lines, half_rows:], folded, preferred_element_type=jnp.float32)
        chosen = top[:, :rank_width] + low[:, rank_width:]
        select = jnp.concatenate([chosen, chosen], axis=1) * live_ref[lines]
        select = (select + fixed_ref[lines].astype(jnp.float32)).astype(jnp.bfloat16)

        @pl.loop(0, chips)
        def _(q):
            out_ref[q] = jnp.dot(
                select,
                jnp.concatenate([mine_ref[q], other_ref[q]], axis=0),
                preferred_element_type=jnp.float32,
            ).astype(out_ref.dtype)

    return pl.pallas_call(
        kernel,
        in_specs=[pl.BlockSpec(memory_space=pltpu.VMEM)] * 6,
        out_specs=pl.BlockSpec(memory_space=pltpu.VMEM),
        out_shape=jax.ShapeDtypeStruct((chips, count, width), mine.dtype),
        compiler_params=vmem(4 * chips * width * (2 * rank_width + count)),
        cost_estimate=pl.CostEstimate(
            flops=4 * chips * count * rank_width * width,
            bytes_accessed=2 * chips * width * (2 * rank_width + count),
            transcendentals=0,
        ),
    )(choose, live, fixed, coeff, mine, other)


def combine(base, code, begin, more, coeff, incoming, extra):
    total_rows, width = base.shape
    chips, first, _ = incoming.shape
    second = extra.shape[1]
    limit = first + second
    rank_width = limit // 2
    shift = rank_width.bit_length() - 1
    tile = 256 if width % 256 == 0 else 128

    def kernel(
        begin_ref, more_ref, base_ref, code_ref, coeff_ref, incoming_ref, extra_ref,
        out_ref, late, sem,
    ):
        fetch = pltpu.make_async_copy(extra_ref, late, sem)
        folded = coeff_ref[...].astype(jnp.float32)
        both = jnp.concatenate(
            [
                jnp.concatenate([part, part], axis=1)
                for part in (folded[:, :rank_width], folded[:, rank_width:])
            ],
            axis=0,
        )
        code_value = code_ref[...]
        slot, by_factor, spot = code_value & 31, (code_value >> 5) & 1, code_value >> 6
        lane = lax.broadcasted_iota(jnp.int32, (total_rows, limit), 1)
        owned = jnp.where(by_factor == 1, slot, -1) - (lane >> shift)
        finished = jnp.where(by_factor == 0, spot, -1)[:, :1]
        finished_chip = (slot >> 1)[:, :1]

        def weights(low, count):
            target = finished - low
            target = jnp.where((target >= 0) & (target < count), finished_chip * count + target, -1)
            wide = lax.broadcasted_iota(jnp.int32, (total_rows, chips * count), 1)
            total = jnp.where(wide == target, 1.0, 0.0)
            line = lax.broadcasted_iota(jnp.int32, (limit, chips * count), 0)
            place = lax.broadcasted_iota(jnp.int32, (limit, chips * count), 1)
            for q in range(chips):
                goal = jnp.where(
                    line < rank_width, line, line - rank_width + begin_ref[2 * q + 1]
                ) - low
                moved = (goal >= 0) & (goal < count) & (place == q * count + goal)
                moved = jnp.where(moved, 1.0, 0.0).astype(jnp.bfloat16)
                part = jnp.where(owned == 2 * q, both, 0.0).astype(jnp.bfloat16)
                total = total + jnp.dot(part, moved, preferred_element_type=jnp.float32)
            return total.astype(jnp.bfloat16)

        near = weights(0, first)

        def write(far):
            @pl.loop(0, width // tile)
            def _(i):
                columns = pl.ds(pl.multiple_of(i * tile, tile), tile)
                block = incoming_ref[:, :, columns].reshape(chips * first, tile)
                total = jnp.dot(near, block, preferred_element_type=jnp.float32)
                total += base_ref[:, columns]
                if far is not None:
                    block = late[:, :, columns].reshape(chips * second, tile)
                    total += jnp.dot(far, block, preferred_element_type=jnp.float32)
                out_ref[:, columns] = total.astype(out_ref.dtype)

        @pl.when(more_ref[0] > first)
        def _():
            fetch.start()
            far = weights(first, second)
            fetch.wait()
            write(far)

        @pl.when(more_ref[0] <= first)
        def _():
            write(None)

    smem, whole = pl.BlockSpec(memory_space=pltpu.SMEM), pl.BlockSpec(memory_space=pltpu.VMEM)
    return pl.pallas_call(
        kernel,
        in_specs=[smem] * 2
        + [whole] * 4
        + [pl.BlockSpec(memory_space=pl.ANY)],
        out_specs=whole,
        out_shape=jax.ShapeDtypeStruct((total_rows, width), jnp.bfloat16),
        scratch_shapes=[pltpu.VMEM(extra.shape, extra.dtype), pltpu.SemaphoreType.DMA(())],
        compiler_params=vmem(8 * total_rows * width + 2 * chips * limit * width),
        cost_estimate=pl.CostEstimate(
            flops=4 * total_rows * chips * limit * width,
            bytes_accessed=6 * total_rows * width + 2 * chips * limit * width,
            transcendentals=0,
        ),
    )(begin, more, base, code, coeff, incoming, extra)


def ring_gather(block, shards, halfway):
    chips = shards // 2
    depth = chips // 2
    cycle = list(range(0, chips, 2)) + list(range(chips - 1, 0, -2))
    ahead = [
        (2 * cycle[p] + c, 2 * cycle[(p + 1) % chips] + c) for p in range(chips) for c in range(2)
    ]
    back = [(b, a) for a, b in ahead]
    held = {0: block}
    for step in range(1, depth + 1):
        held[-step] = lax.ppermute(held[1 - step], "tensor", ahead)
        if step < chips - depth:
            held[step] = lax.ppermute(held[step - 1], "tensor", back)
        held[-step] = halfway(step, held[-step])
    table = np.zeros((shards, shards), np.int32)
    for t in range(shards):
        for i, offset in enumerate(held):
            chip = cycle[(cycle.index(t // 2) + offset) % chips]
            table[t, 2 * i], table[t, 2 * i + 1] = 2 * chip + t % 2, 2 * chip + 1 - t % 2
    places = lax.dynamic_index_in_dim(table, lax.axis_index("tensor"), keepdims=False)
    return list(held.values()), places


def largest_over_groups(value):
    groups = lax.axis_size("groups")
    for shift in range(1, groups):
        other = lax.ppermute(value, "groups", [(g, (g + shift) % groups) for g in range(groups)])
        value = jnp.maximum(value, other)
    return value


def pooled(
    input_rows,
    up_weight,
    adapter_down,
    adapter_up,
    ranks,
    adapter_slot,
    segment_lengths,
    segment_adapter,
):
    shards = lax.axis_size("tensor")
    position = lax.axis_index("tensor").astype(jnp.int32)
    chips = shards // 2
    total_rows = input_rows.shape[0] * shards
    rank_width = adapter_up.shape[1]
    limit = 2 * rank_width
    sibling = [(t, t ^ 1) for t in range(shards)]
    same_core = [list(range(c, shards, 2)) for c in range(2)]

    core = position & 1
    features = input_rows.shape[1] // 2

    def swap(value):
        keep = lax.dynamic_slice_in_dim(value, core * features, features, 1)
        send = lax.dynamic_slice_in_dim(value, (1 - core) * features, features, 1)
        return keep, lax.ppermute(send, "tensor", sibling)

    mine, other, down_half = split_for_pair(adapter_up[0], adapter_down[0], core[None], chips)
    block = jnp.concatenate(swap(input_rows), axis=0)
    block, mine, other, down_half = lax.optimization_barrier((block, mine, other, down_half))
    other = lax.ppermute(other, "tensor", sibling)
    down_half = lax.ppermute(down_half, "tensor", sibling)
    gain, own, choose, live, fixed, code, begin, full = describe(
        ranks, adapter_slot, segment_lengths, segment_adapter, position[None], total_rows, limit
    )
    fullest = largest_over_groups(full)
    pending = [(own, choose), (fullest, other, down_half)]

    def halfway(step, piece):
        nonlocal pending
        if step <= len(pending):
            piece, pending[step - 1] = lax.optimization_barrier((piece, pending[step - 1]))
        return piece

    blocks, places = ring_gather(block, shards, halfway)
    (own, choose), (fullest, other, down_half) = pending
    rows, shrink = collect_rows(blocks, places, core[None], adapter_down[0], down_half, own)
    shrink = shrink + lax.ppermute(shrink, "tensor", sibling)
    coeff = (shrink * gain).astype(jnp.bfloat16)
    coeff, rows = lax.optimization_barrier((coeff, rows))

    def payload(low, count):
        return build_payload(choose, live, fixed, coeff, mine, other, low, count)

    def exchange(value):
        return lax.all_to_all(
            value,
            "tensor",
            split_axis=0,
            concat_axis=0,
            axis_index_groups=same_core,
            tiled=True,
        )

    near = payload(0, FIRST_ROWS)
    rows_other = lax.ppermute(rows, "tensor", sibling)
    every, bit = coeff, 2
    while bit < shards:
        every = every + lax.ppermute(every, "tensor", [(t, t ^ bit) for t in range(shards)])
        if bit == 2:
            every, near = lax.optimization_barrier((every, near))
        bit *= 2
    near, every, rows, rows_other = lax.optimization_barrier((near, every, rows, rows_other))
    incoming = exchange(near)
    halves = [jnp.where(core == c, rows, rows_other) for c in range(2)]
    base = jnp.dot(
        jnp.concatenate(halves, axis=1), up_weight, preferred_element_type=jnp.float32
    )
    fullest, base, incoming = lax.optimization_barrier((fullest, base, incoming))
    rest = limit - FIRST_ROWS
    extra = lax.cond(
        fullest[0] > FIRST_ROWS,
        lambda: exchange(payload(FIRST_ROWS, rest)),
        lambda: jnp.zeros((chips, rest, up_weight.shape[1]), adapter_up.dtype),
    )
    return combine(base, code, begin, fullest, every, incoming, extra)


def gathered(input_rows, up_weight, adapter_down, adapter_up, slot_row, row_rank):
    shards = lax.axis_size("tensor")
    position = lax.axis_index("tensor")
    total_rows = input_rows.shape[0] * shards
    stored, rank_width, hidden = adapter_up.shape
    width = hidden // shards
    slots = shards * stored
    outgoing = jnp.stack(
        [adapter_up[:, :, i * width : (i + 1) * width] for i in range(shards)], axis=0
    )
    incoming = lax.all_to_all(outgoing, "tensor", split_axis=0, concat_axis=0, tiled=True)
    rows = lax.all_gather(input_rows, "tensor", axis=0, tiled=True)
    shrink = jnp.einsum("gf,ojf->ogj", rows, adapter_down, preferred_element_type=jnp.float32)
    own = position * stored + jnp.arange(stored, dtype=jnp.int32)
    inside = jnp.arange(rank_width, dtype=jnp.int32)[None, :] < row_rank[:, None]
    keep = (slot_row[None, :] == own[:, None])[:, :, None] & inside[None]
    scale = ADAPTER_ALPHA / row_rank.astype(jnp.float32)
    own_coeff = jnp.where(keep, shrink * scale[None, :, None], 0.0).astype(jnp.bfloat16)
    base = jnp.dot(rows, up_weight, preferred_element_type=jnp.float32)
    own_coeff, base = lax.optimization_barrier((own_coeff, base))
    coeff = lax.all_gather(own_coeff, "tensor", axis=0, tiled=True)
    placed = coeff.transpose(1, 0, 2).reshape(total_rows, slots * rank_width)
    factors = incoming.reshape(slots * rank_width, width)
    term = jnp.dot(placed, factors, preferred_element_type=jnp.float32)
    return (base + term).astype(jnp.bfloat16)


def on_device(
    input_rows,
    up_weight,
    adapter_down,
    adapter_up,
    ranks,
    adapter_slot,
    segment_lengths,
    segment_adapter,
):
    shards = lax.axis_size("tensor")
    stored, rank_width, _ = adapter_up.shape
    tiled = up_weight.shape[1] % 128 == 0 and input_rows.shape[0] % 16 == 0 and rank_width == 64
    tiled = tiled and input_rows.shape[1] % 256 == 0 and input_rows.shape[0] * shards <= 256
    if shards == POOLED_SHARDS and stored == 1 and tiled:
        return pooled(
            input_rows,
            up_weight,
            adapter_down,
            adapter_up,
            ranks,
            adapter_slot,
            segment_lengths,
            segment_adapter,
        )
    slot_row, row_rank = row_tables(
        input_rows.shape[0] * shards, ranks, adapter_slot, segment_lengths, segment_adapter
    )
    return gathered(input_rows, up_weight, adapter_down, adapter_up, slot_row, row_rank)


def solution(mesh):
    placed = (
        P(("groups", "tensor"), None),
        P(None, "tensor"),
        P(("groups", "tensor"), None, None),
        P(("groups", "tensor"), None, None),
        P("groups"),
        P("groups"),
        P("groups"),
        P("groups"),
    )
    return jax.shard_map(
        on_device, mesh=mesh, in_specs=placed, out_specs=P("groups", "tensor"), check_vma=False
    )
```

```python
import jax
import jax.numpy as jnp
import numpy as np
from jax import lax
from jax.experimental import pallas as pl
from jax.experimental.pallas import tpu as pltpu
from jax.sharding import PartitionSpec as P

ADAPTER_ALPHA = 32.0
POOLED_SHARDS = 16
FIRST_ROWS = 64
MORE_ROWS = (16, 32)


def row_tables(row_count, ranks, adapter_slot, segment_lengths, segment_adapter):
    seg_ends = jnp.cumsum(segment_lengths)
    positions = jnp.arange(row_count, dtype=jnp.int32)
    seg_row = jnp.sum((seg_ends[None, :] <= positions[:, None]).astype(jnp.int32), axis=1)
    seg_pick = (
        seg_row[:, None] == jnp.arange(segment_lengths.shape[0], dtype=jnp.int32)[None, :]
    ).astype(jnp.int32)
    adapter_row = jnp.sum(seg_pick * segment_adapter[None, :], axis=1)
    pool_pick = (
        adapter_row[:, None] == jnp.arange(ranks.shape[0], dtype=jnp.int32)[None, :]
    ).astype(jnp.int32)
    slot_row = jnp.sum(pool_pick * adapter_slot[None, :], axis=1)
    row_rank_values = jnp.sum(pool_pick * ranks[None, :], axis=1)
    return (slot_row, row_rank_values)


def vmem(buffers):
    return pltpu.CompilerParams(vmem_limit_bytes=buffers + (8 << 20))


def split_for_pair(up_factor, down_factor, core, chips):
    rank_width, hidden = up_factor.shape
    width = hidden // (2 * chips)
    features = down_factor.shape[1] // 2

    def kernel(core_ref, source, down, mine, other, half_down, sems):
        core = core_ref[0]
        start = pl.multiple_of((1 - core) * features, features)
        copies = [
            pltpu.make_async_copy(
                down.at[:, pl.ds(start, features)], half_down, sems.at[2 * chips]
            )
        ]
        for q in range(chips):
            for i, (target, half) in enumerate(((other, 1 - core), (mine, core))):
                start = pl.multiple_of((2 * q + half) * width, width)
                copies.append(
                    pltpu.make_async_copy(
                        source.at[:, pl.ds(start, width)], target.at[q], sems.at[2 * q + i]
                    )
                )
        for copy in copies:
            copy.start()
        for copy in copies:
            copy.wait()

    block = jax.ShapeDtypeStruct((chips, rank_width, width), up_factor.dtype)
    return pl.pallas_call(
        kernel,
        in_specs=[pl.BlockSpec(memory_space=pltpu.SMEM)]
        + [pl.BlockSpec(memory_space=pltpu.HBM)] * 2,
        out_specs=[pl.BlockSpec(memory_space=pltpu.VMEM)] * 3,
        out_shape=[
            block, block, jax.ShapeDtypeStruct((rank_width, features), down_factor.dtype)
        ],
        scratch_shapes=[pltpu.SemaphoreType.DMA((2 * chips + 1,))],
        compiler_params=vmem(2 * rank_width * (hidden + features)),
        cost_estimate=pl.CostEstimate(
            flops=0, bytes_accessed=4 * rank_width * hidden, transcendentals=0
        ),
    )(core, up_factor, down_factor)


def describe(ranks, adapter_slot, segment_lengths, segment_adapter, position, total_rows, limit):
    slots, segments = ranks.shape[0], segment_lengths.shape[0]
    rank_width = limit // 2
    shift = rank_width.bit_length() - 1

    def kernel(
        ranks_in, home_in, length_in, adapter_in, position_ref,
        gain_ref, own_ref, choose_ref, live_ref, fixed_ref, code_ref, begin_ref, full_ref,
        rank_of, rows_of, used, factor, order, ranks_ref, home_ref, length_ref, adapter_ref, sems,
    ):
        pairs = zip(
            (ranks_in, home_in, length_in, adapter_in),
            (ranks_ref, home_ref, length_ref, adapter_ref),
        )
        copies = [
            pltpu.make_async_copy(source, target, sems.at[i])
            for i, (source, target) in enumerate(pairs)
        ]
        for copy in copies:
            copy.start()
        for copy in copies:
            copy.wait()
        for a in range(slots):
            rows_of[a] = 0
            rank_of[home_ref[a]] = ranks_ref[a]
        starts, start = [], jnp.int32(0)
        for i in range(segments):
            slot = home_ref[adapter_ref[i]]
            starts.append((start, start + length_ref[i], slot))
            order[i] = rows_of[slot] - start
            rows_of[slot] = rows_of[slot] + length_ref[i]
            start = start + length_ref[i]
        full = jnp.int32(0)
        for s in range(slots):
            used[s] = jnp.minimum(rows_of[s], rank_of[s])
            factor[s] = (rank_of[s] < rows_of[s]).astype(jnp.int32)
            begin_ref[s] = used[s - 1] if s % 2 else jnp.int32(0)
            if s % 2:
                full = jnp.maximum(full, used[s - 1] + used[s])
        full_ref[0] = full

        def tables(row):
            spot, code = jnp.zeros_like(row), jnp.zeros_like(row)
            for i, (low, high, slot) in enumerate(starts):
                hit = (row >= low) & (row < high)
                spot = jnp.where(hit, row + (order[i] + begin_ref[slot]), spot)
                code = jnp.where(hit, slot + 32 * factor[slot] + 64 * rank_of[slot], code)
            return spot, code & 31, (code >> 5) & 1, code >> 6

        here = position_ref[0]
        spot, slot, by_factor, _ = tables(lax.broadcasted_iota(jnp.int32, (total_rows, limit), 0))
        code_ref[...] = slot + 32 * by_factor + 64 * spot

        lane = lax.broadcasted_iota(jnp.int32, (total_rows // 2, limit), 1)
        row = lax.broadcasted_iota(jnp.int32, (total_rows // 2, limit), 0)
        _, slot, _, rank = tables(row + (lane >> shift) * (total_rows // 2))
        own_ref[...] = jnp.where(slot == here, 1.0, 0.0)
        scale = ADAPTER_ALPHA / rank.astype(jnp.float32)
        inside = ((slot >> 1) == (here >> 1)) & ((lane & (rank_width - 1)) < rank)
        gain_ref[...] = jnp.where(inside, scale, 0.0)

        spot, slot, by_factor, _ = tables(lax.broadcasted_iota(jnp.int32, (8, total_rows), 1))
        mine = ((slot >> 1) == (here >> 1)) & (by_factor == 0)
        spot = jnp.broadcast_to(jnp.where(mine, spot, -1)[:1], (limit, total_rows))
        line = lax.broadcasted_iota(jnp.int32, (limit, total_rows), 0)
        choose_ref[...] = jnp.where(line == spot, 1.0, 0.0).astype(jnp.bfloat16)

        line = lax.broadcasted_iota(jnp.int32, (limit, limit), 0)
        lane = lax.broadcasted_iota(jnp.int32, (limit, limit), 1)
        half, column = lane >> shift, lane & (rank_width - 1)
        other = here ^ 1
        begin = jnp.where(half == 0, begin_ref[here], begin_ref[other])
        many = jnp.where(half == 0, used[here], used[other])
        kind = jnp.where(half == 0, factor[here], factor[other])
        held = (line == begin + column) & (column < many) & (kind == 1)
        fixed_ref[...] = jnp.where(held, 1.0, 0.0).astype(jnp.bfloat16)
        live = (line >= begin) & (line < begin + many) & (kind == 0)
        live_ref[...] = jnp.where(live, 1.0, 0.0)

    smem, whole = pl.BlockSpec(memory_space=pltpu.SMEM), pl.BlockSpec(memory_space=pltpu.VMEM)
    return pl.pallas_call(
        kernel,
        in_specs=[pl.BlockSpec(memory_space=pltpu.HBM)] * 4 + [smem],
        out_specs=[whole] * 6 + [smem] * 2,
        out_shape=[
            jax.ShapeDtypeStruct((total_rows // 2, limit), jnp.float32),
            jax.ShapeDtypeStruct((total_rows // 2, limit), jnp.float32),
            jax.ShapeDtypeStruct((limit, total_rows), jnp.bfloat16),
            jax.ShapeDtypeStruct((limit, limit), jnp.float32),
            jax.ShapeDtypeStruct((limit, limit), jnp.bfloat16),
            jax.ShapeDtypeStruct((total_rows, limit), jnp.int32),
            jax.ShapeDtypeStruct((slots,), jnp.int32),
            jax.ShapeDtypeStruct((1,), jnp.int32),
        ],
        scratch_shapes=[pltpu.SMEM((slots,), jnp.int32)] * 4
        + [pltpu.SMEM((segments,), jnp.int32)]
        + [pltpu.SMEM((slots,), jnp.int32)] * 2
        + [pltpu.SMEM((segments,), jnp.int32)] * 2
        + [pltpu.SemaphoreType.DMA((4,))],
        compiler_params=vmem(16 * total_rows * limit),
        cost_estimate=pl.CostEstimate(
            flops=200 * total_rows * limit, bytes_accessed=16 * total_rows * limit, transcendentals=0
        ),
    )(ranks, adapter_slot, segment_lengths, segment_adapter, position)


def collect_rows(blocks, places, core, own_down, other_down, own):
    count = len(blocks)
    height, features = blocks[0].shape
    height = height // 2
    rank_width = other_down.shape[0]
    half_rows = own.shape[0]
    chunk = 1024 if features % 1024 == 0 else features
    chunks = features // chunk

    def kernel(places_ref, core_ref, own_ref, *refs):
        sources, own_down_ref, other_down_ref = refs[:count], refs[count], refs[count + 1]
        rows_ref, shrink_ref, downs, sems = refs[count + 2 :]
        groups = []
        for k in range(chunks):
            columns = pl.ds(k * chunk, chunk)
            offset = pl.multiple_of(core_ref[0] * features + k * chunk, chunk)
            copies = [
                pltpu.make_async_copy(
                    own_down_ref.at[:, pl.ds(offset, chunk)],
                    downs.at[pl.ds(0, rank_width), columns],
                    sems.at[k, 2 * count],
                ),
                pltpu.make_async_copy(
                    other_down_ref.at[:, columns],
                    downs.at[pl.ds(rank_width, rank_width), columns],
                    sems.at[k, 2 * count + 1],
                ),
            ]
            for i in range(2 * count):
                start = pl.multiple_of(places_ref[i] * height, height)
                copies.append(
                    pltpu.make_async_copy(
                        sources[i // 2].at[pl.ds(i % 2 * height, height), columns],
                        rows_ref.at[pl.ds(start, height), columns],
                        sems.at[k, i],
                    )
                )
            groups.append(copies)
            for copy in copies:
                copy.start()
        shrink = jnp.zeros((2 * half_rows, 2 * rank_width), jnp.float32)
        for k in range(chunks):
            for copy in groups[k]:
                copy.wait()
            columns = pl.ds(k * chunk, chunk)
            shrink = shrink + lax.dot_general(
                rows_ref[:, columns],
                downs[:, columns],
                (((1,), (1,)), ((), ())),
                preferred_element_type=jnp.float32,
            )
        top, bottom = shrink[:half_rows], shrink[half_rows:]
        first = jnp.concatenate([top[:, :rank_width], bottom[:, :rank_width]], axis=1)
        second = jnp.concatenate([top[:, rank_width:], bottom[:, rank_width:]], axis=1)
        shrink_ref[...] = jnp.where(own_ref[...] > 0.5, first, second)

    smem, whole = pl.BlockSpec(memory_space=pltpu.SMEM), pl.BlockSpec(memory_space=pltpu.VMEM)
    rows = 2 * count * height
    return pl.pallas_call(
        kernel,
        in_specs=[smem, smem, whole] + [pl.BlockSpec(memory_space=pl.ANY)] * (count + 2),
        out_specs=[whole] * 2,
        out_shape=[
            jax.ShapeDtypeStruct((rows, features), blocks[0].dtype),
            jax.ShapeDtypeStruct(own.shape, jnp.float32),
        ],
        scratch_shapes=[
            pltpu.VMEM((2 * rank_width, features), own_down.dtype),
            pltpu.SemaphoreType.DMA((chunks, 2 * count + 2)),
        ],
        compiler_params=vmem(4 * rows * features),
        cost_estimate=pl.CostEstimate(
            flops=4 * rows * features * rank_width,
            bytes_accessed=4 * rows * features,
            transcendentals=0,
        ),
    )(places, core, own, *blocks, own_down, other_down)


def build_payload(choose, live, fixed, coeff, mine, other, first, count):
    chips, rank_width, width = mine.shape

    half_rows = coeff.shape[0]

    def kernel(choose_ref, live_ref, fixed_ref, coeff_ref, mine_ref, other_ref, out_ref):
        lines = pl.ds(first, count)
        folded = coeff_ref[...]
        top = jnp.dot(choose_ref[lines, :half_rows], folded, preferred_element_type=jnp.float32)
        low = jnp.dot(choose_ref[lines, half_rows:], folded, preferred_element_type=jnp.float32)
        chosen = top[:, :rank_width] + low[:, rank_width:]
        select = jnp.concatenate([chosen, chosen], axis=1) * live_ref[lines]
        select = (select + fixed_ref[lines].astype(jnp.float32)).astype(jnp.bfloat16)

        @pl.loop(0, chips)
        def _(q):
            out_ref[q] = jnp.dot(
                select,
                jnp.concatenate([mine_ref[q], other_ref[q]], axis=0),
                preferred_element_type=jnp.float32,
            ).astype(out_ref.dtype)

    return pl.pallas_call(
        kernel,
        in_specs=[pl.BlockSpec(memory_space=pltpu.VMEM)] * 6,
        out_specs=pl.BlockSpec(memory_space=pltpu.VMEM),
        out_shape=jax.ShapeDtypeStruct((chips, count, width), mine.dtype),
        compiler_params=vmem(4 * chips * width * (2 * rank_width + count)),
        cost_estimate=pl.CostEstimate(
            flops=4 * chips * count * rank_width * width,
            bytes_accessed=2 * chips * width * (2 * rank_width + count),
            transcendentals=0,
        ),
    )(choose, live, fixed, coeff, mine, other)


def combine(base, code, begin, more, coeff, incoming, extra):
    total_rows, width = base.shape
    chips, first, _ = incoming.shape
    second = extra.shape[1]
    limit = first + second
    rank_width = limit // 2
    shift = rank_width.bit_length() - 1
    tile = 256 if width % 256 == 0 else 128

    def kernel(
        begin_ref, more_ref, base_ref, code_ref, coeff_ref, incoming_ref, extra_ref,
        out_ref, late, base_part, near_rows, sems,
    ):
        fetch = pltpu.make_async_copy(extra_ref, late, sems.at[0])
        get_base = pltpu.make_async_copy(base_ref, base_part, sems.at[1])
        get_near = pltpu.make_async_copy(incoming_ref, near_rows, sems.at[2])
        get_near.start()
        get_base.start()
        folded = coeff_ref[...].astype(jnp.float32)
        both = jnp.concatenate(
            [
                jnp.concatenate([part, part], axis=1)
                for part in (folded[:, :rank_width], folded[:, rank_width:])
            ],
            axis=0,
        )
        code_value = code_ref[...]
        slot, by_factor, spot = code_value & 31, (code_value >> 5) & 1, code_value >> 6
        lane = lax.broadcasted_iota(jnp.int32, (total_rows, limit), 1)
        owned = jnp.where(by_factor == 1, slot, -1) - (lane >> shift)
        finished = jnp.where(by_factor == 0, spot, -1)[:, :1]
        finished_chip = (slot >> 1)[:, :1]

        def weights(low, count):
            target = finished - low
            target = jnp.where((target >= 0) & (target < count), finished_chip * count + target, -1)
            wide = lax.broadcasted_iota(jnp.int32, (total_rows, chips * count), 1)
            total = jnp.where(wide == target, 1.0, 0.0)
            line = lax.broadcasted_iota(jnp.int32, (limit, chips * count), 0)
            place = lax.broadcasted_iota(jnp.int32, (limit, chips * count), 1)
            for q in range(chips):
                goal = jnp.where(
                    line < rank_width, line, line - rank_width + begin_ref[2 * q + 1]
                ) - low
                moved = (goal >= 0) & (goal < count) & (place == q * count + goal)
                moved = jnp.where(moved, 1.0, 0.0).astype(jnp.bfloat16)
                part = jnp.where(owned == 2 * q, both, 0.0).astype(jnp.bfloat16)
                total = total + jnp.dot(part, moved, preferred_element_type=jnp.float32)
            return total.astype(jnp.bfloat16)

        near = weights(0, first)
        get_near.wait()
        get_base.wait()

        def write(far):
            @pl.loop(0, width // tile)
            def _(i):
                columns = pl.ds(pl.multiple_of(i * tile, tile), tile)
                block = near_rows[:, :, columns].reshape(chips * first, tile)
                total = jnp.dot(near, block, preferred_element_type=jnp.float32)
                total += base_part[:, columns]
                if far is not None:
                    block = late[:, :, columns].reshape(chips * second, tile)
                    total += jnp.dot(far, block, preferred_element_type=jnp.float32)
                out_ref[:, columns] = total.astype(out_ref.dtype)

        @pl.when(more_ref[0] > first)
        def _():
            fetch.start()
            far = weights(first, second)
            fetch.wait()
            write(far)

        @pl.when(more_ref[0] <= first)
        def _():
            write(None)

    smem, whole = pl.BlockSpec(memory_space=pltpu.SMEM), pl.BlockSpec(memory_space=pltpu.VMEM)
    return pl.pallas_call(
        kernel,
        in_specs=[smem] * 2
        + [pl.BlockSpec(memory_space=pl.ANY)]
        + [whole] * 2
        + [pl.BlockSpec(memory_space=pl.ANY)] * 2,
        out_specs=whole,
        out_shape=jax.ShapeDtypeStruct((total_rows, width), jnp.bfloat16),
        scratch_shapes=[
            pltpu.VMEM(extra.shape, extra.dtype),
            pltpu.VMEM(base.shape, base.dtype),
            pltpu.VMEM(incoming.shape, incoming.dtype),
            pltpu.SemaphoreType.DMA((3,)),
        ],
        compiler_params=vmem(8 * total_rows * width + 2 * chips * limit * width),
        cost_estimate=pl.CostEstimate(
            flops=4 * total_rows * chips * limit * width,
            bytes_accessed=6 * total_rows * width + 2 * chips * limit * width,
            transcendentals=0,
        ),
    )(begin, more, base, code, coeff, incoming, extra)


def ring_gather(block, shards, halfway):
    chips = shards // 2
    depth = chips // 2
    cycle = list(range(0, chips, 2)) + list(range(chips - 1, 0, -2))
    ahead = [
        (2 * cycle[p] + c, 2 * cycle[(p + 1) % chips] + c) for p in range(chips) for c in range(2)
    ]
    back = [(b, a) for a, b in ahead]
    held = {0: block}
    for step in range(1, depth + 1):
        held[-step] = lax.ppermute(held[1 - step], "tensor", ahead)
        if step < chips - depth:
            held[step] = lax.ppermute(held[step - 1], "tensor", back)
        held[-step] = halfway(step, held[-step])
    table = np.zeros((shards, shards), np.int32)
    for t in range(shards):
        for i, offset in enumerate(held):
            chip = cycle[(cycle.index(t // 2) + offset) % chips]
            table[t, 2 * i], table[t, 2 * i + 1] = 2 * chip + t % 2, 2 * chip + 1 - t % 2
    places = lax.dynamic_index_in_dim(table, lax.axis_index("tensor"), keepdims=False)
    return list(held.values()), places


def largest_over_groups(value):
    groups = lax.axis_size("groups")
    for shift in range(1, groups):
        other = lax.ppermute(value, "groups", [(g, (g + shift) % groups) for g in range(groups)])
        value = jnp.maximum(value, other)
    return value


def pooled(
    input_rows,
    up_weight,
    adapter_down,
    adapter_up,
    ranks,
    adapter_slot,
    segment_lengths,
    segment_adapter,
):
    shards = lax.axis_size("tensor")
    position = lax.axis_index("tensor").astype(jnp.int32)
    chips = shards // 2
    total_rows = input_rows.shape[0] * shards
    rank_width = adapter_up.shape[1]
    limit = 2 * rank_width
    sibling = [(t, t ^ 1) for t in range(shards)]
    same_core = [list(range(c, shards, 2)) for c in range(2)]

    core = position & 1
    features = input_rows.shape[1] // 2

    def swap(value):
        keep = lax.dynamic_slice_in_dim(value, core * features, features, 1)
        send = lax.dynamic_slice_in_dim(value, (1 - core) * features, features, 1)
        return keep, lax.ppermute(send, "tensor", sibling)

    block = jnp.concatenate(swap(input_rows), axis=0)
    tables = describe(
        ranks, adapter_slot, segment_lengths, segment_adapter, position[None], total_rows, limit
    )
    gain, own, choose, live, fixed, code, begin, full = tables
    fullest = largest_over_groups(full)
    packed = ()

    def halfway(step, piece):
        nonlocal packed, own
        if step == 1:
            piece, own, which = lax.optimization_barrier((piece, own, core[None]))
            packed = split_for_pair(adapter_up[0], adapter_down[0], which, chips)
        if step == 2:
            piece, packed = lax.optimization_barrier((piece, packed))
        return piece

    blocks, places = ring_gather(block, shards, halfway)
    mine, other, down_half = packed
    down_half = lax.ppermute(down_half, "tensor", sibling)
    blocks, other, down_half = lax.optimization_barrier((blocks, other, down_half))
    other = lax.ppermute(other, "tensor", sibling)
    rows, shrink = collect_rows(blocks, places, core[None], adapter_down[0], down_half, own)
    shrink = shrink + lax.ppermute(shrink, "tensor", sibling)
    coeff = (shrink * gain).astype(jnp.bfloat16)
    coeff, rows, fullest = lax.optimization_barrier((coeff, rows, fullest))

    def payload(low, count):
        return build_payload(choose, live, fixed, coeff, mine, other, low, count)

    def exchange(value):
        return lax.all_to_all(
            value,
            "tensor",
            split_axis=0,
            concat_axis=0,
            axis_index_groups=same_core,
            tiled=True,
        )

    near = payload(0, FIRST_ROWS)
    rows_other = lax.ppermute(rows, "tensor", sibling)
    every = coeff + lax.ppermute(coeff, "tensor", [(t, t ^ 2) for t in range(shards)])
    every, near = lax.optimization_barrier((every, near))
    shifts = [[(t, (t + 4 * k) % shards) for t in range(shards)] for k in range(1, shards // 4)]
    others = [lax.ppermute(every, "tensor", hop) for hop in shifts]
    for value in others:
        every = every + value
    near, every, rows, rows_other = lax.optimization_barrier((near, every, rows, rows_other))
    incoming = exchange(near)
    halves = [jnp.where(core == c, rows, rows_other) for c in range(2)]
    base = jnp.dot(
        jnp.concatenate(halves, axis=1), up_weight, preferred_element_type=jnp.float32
    )
    fullest, base, incoming = lax.optimization_barrier((fullest, base, incoming))
    rest = limit - FIRST_ROWS

    def later(count):
        def run():
            value = jnp.zeros((chips, rest - count, up_weight.shape[1]), adapter_up.dtype)
            if count:
                late = exchange(payload(FIRST_ROWS, count))
                value = jnp.concatenate([late, value], axis=1)
            return value

        return run

    sizes = (0,) + tuple(size for size in MORE_ROWS if size < rest) + (rest,)
    which = sum((fullest[0] > FIRST_ROWS + size).astype(jnp.int32) for size in sizes[:-1])
    extra = lax.switch(which, [later(size) for size in sizes])
    return combine(base, code, begin, fullest, every, incoming, extra)


def gathered(input_rows, up_weight, adapter_down, adapter_up, slot_row, row_rank):
    shards = lax.axis_size("tensor")
    position = lax.axis_index("tensor")
    total_rows = input_rows.shape[0] * shards
    stored, rank_width, hidden = adapter_up.shape
    width = hidden // shards
    slots = shards * stored
    outgoing = jnp.stack(
        [adapter_up[:, :, i * width : (i + 1) * width] for i in range(shards)], axis=0
    )
    incoming = lax.all_to_all(outgoing, "tensor", split_axis=0, concat_axis=0, tiled=True)
    rows = lax.all_gather(input_rows, "tensor", axis=0, tiled=True)
    shrink = jnp.einsum("gf,ojf->ogj", rows, adapter_down, preferred_element_type=jnp.float32)
    own = position * stored + jnp.arange(stored, dtype=jnp.int32)
    inside = jnp.arange(rank_width, dtype=jnp.int32)[None, :] < row_rank[:, None]
    keep = (slot_row[None, :] == own[:, None])[:, :, None] & inside[None]
    scale = ADAPTER_ALPHA / row_rank.astype(jnp.float32)
    own_coeff = jnp.where(keep, shrink * scale[None, :, None], 0.0).astype(jnp.bfloat16)
    base = jnp.dot(rows, up_weight, preferred_element_type=jnp.float32)
    own_coeff, base = lax.optimization_barrier((own_coeff, base))
    coeff = lax.all_gather(own_coeff, "tensor", axis=0, tiled=True)
    placed = coeff.transpose(1, 0, 2).reshape(total_rows, slots * rank_width)
    factors = incoming.reshape(slots * rank_width, width)
    term = jnp.dot(placed, factors, preferred_element_type=jnp.float32)
    return (base + term).astype(jnp.bfloat16)


def on_device(
    input_rows,
    up_weight,
    adapter_down,
    adapter_up,
    ranks,
    adapter_slot,
    segment_lengths,
    segment_adapter,
):
    shards = lax.axis_size("tensor")
    stored, rank_width, _ = adapter_up.shape
    tiled = up_weight.shape[1] % 128 == 0 and input_rows.shape[0] % 16 == 0 and rank_width == 64
    tiled = tiled and input_rows.shape[1] % 256 == 0 and input_rows.shape[0] * shards <= 256
    if shards == POOLED_SHARDS and stored == 1 and tiled:
        return pooled(
            input_rows,
            up_weight,
            adapter_down,
            adapter_up,
            ranks,
            adapter_slot,
            segment_lengths,
            segment_adapter,
        )
    slot_row, row_rank = row_tables(
        input_rows.shape[0] * shards, ranks, adapter_slot, segment_lengths, segment_adapter
    )
    return gathered(input_rows, up_weight, adapter_down, adapter_up, slot_row, row_rank)


def solution(mesh):
    placed = (
        P(("groups", "tensor"), None),
        P(None, "tensor"),
        P(("groups", "tensor"), None, None),
        P(("groups", "tensor"), None, None),
        P("groups"),
        P("groups"),
        P("groups"),
        P("groups"),
    )
    return jax.shard_map(
        on_device, mesh=mesh, in_specs=placed, out_specs=P("groups", "tensor"), check_vma=False
    )
```

```python
import jax
import jax.numpy as jnp
import numpy as np
from jax import lax
from jax.experimental import pallas as pl
from jax.experimental.pallas import tpu as pltpu
from jax.sharding import PartitionSpec as P

ADAPTER_ALPHA = 32.0
POOLED_SHARDS = 16
FIRST_ROWS = 64
MORE_ROWS = (16, 32)


def row_tables(row_count, ranks, adapter_slot, segment_lengths, segment_adapter):
    seg_ends = jnp.cumsum(segment_lengths)
    positions = jnp.arange(row_count, dtype=jnp.int32)
    seg_row = jnp.sum((seg_ends[None, :] <= positions[:, None]).astype(jnp.int32), axis=1)
    seg_pick = (
        seg_row[:, None] == jnp.arange(segment_lengths.shape[0], dtype=jnp.int32)[None, :]
    ).astype(jnp.int32)
    adapter_row = jnp.sum(seg_pick * segment_adapter[None, :], axis=1)
    pool_pick = (
        adapter_row[:, None] == jnp.arange(ranks.shape[0], dtype=jnp.int32)[None, :]
    ).astype(jnp.int32)
    slot_row = jnp.sum(pool_pick * adapter_slot[None, :], axis=1)
    row_rank_values = jnp.sum(pool_pick * ranks[None, :], axis=1)
    return (slot_row, row_rank_values)


def vmem(buffers):
    return pltpu.CompilerParams(vmem_limit_bytes=buffers + (8 << 20))


def split_for_pair(up_factor, down_factor, core, chips):
    rank_width, hidden = up_factor.shape
    width = hidden // (2 * chips)
    features = down_factor.shape[1] // 2

    def kernel(core_ref, source, down, mine, other, half_down, sems):
        core = core_ref[0]
        start = pl.multiple_of((1 - core) * features, features)
        copies = [
            pltpu.make_async_copy(
                down.at[:, pl.ds(start, features)], half_down, sems.at[2 * chips]
            )
        ]
        for q in range(chips):
            for i, (target, half) in enumerate(((other, 1 - core), (mine, core))):
                start = pl.multiple_of((2 * q + half) * width, width)
                copies.append(
                    pltpu.make_async_copy(
                        source.at[:, pl.ds(start, width)], target.at[q], sems.at[2 * q + i]
                    )
                )
        for copy in copies:
            copy.start()
        for copy in copies:
            copy.wait()

    block = jax.ShapeDtypeStruct((chips, rank_width, width), up_factor.dtype)
    return pl.pallas_call(
        kernel,
        in_specs=[pl.BlockSpec(memory_space=pltpu.SMEM)]
        + [pl.BlockSpec(memory_space=pltpu.HBM)] * 2,
        out_specs=[pl.BlockSpec(memory_space=pltpu.VMEM)] * 3,
        out_shape=[
            block, block, jax.ShapeDtypeStruct((rank_width, features), down_factor.dtype)
        ],
        scratch_shapes=[pltpu.SemaphoreType.DMA((2 * chips + 1,))],
        compiler_params=vmem(2 * rank_width * (hidden + features)),
        cost_estimate=pl.CostEstimate(
            flops=0, bytes_accessed=4 * rank_width * hidden, transcendentals=0
        ),
    )(core, up_factor, down_factor)


def describe(ranks, adapter_slot, segment_lengths, segment_adapter, position, total_rows, limit):
    slots, segments = ranks.shape[0], segment_lengths.shape[0]
    rank_width = limit // 2
    shift = rank_width.bit_length() - 1

    def kernel(
        ranks_in, home_in, length_in, adapter_in, position_ref,
        gain_ref, own_ref, choose_ref, live_ref, fixed_ref, code_ref, begin_ref, full_ref,
        rank_of, rows_of, used, factor, order, ranks_ref, home_ref, length_ref, adapter_ref, sems,
    ):
        pairs = zip(
            (ranks_in, home_in, length_in, adapter_in),
            (ranks_ref, home_ref, length_ref, adapter_ref),
        )
        copies = [
            pltpu.make_async_copy(source, target, sems.at[i])
            for i, (source, target) in enumerate(pairs)
        ]
        for copy in copies:
            copy.start()
        for copy in copies:
            copy.wait()
        for a in range(slots):
            rows_of[a] = 0
            rank_of[home_ref[a]] = ranks_ref[a]
        starts, start = [], jnp.int32(0)
        for i in range(segments):
            slot = home_ref[adapter_ref[i]]
            starts.append((start, start + length_ref[i], slot))
            order[i] = rows_of[slot] - start
            rows_of[slot] = rows_of[slot] + length_ref[i]
            start = start + length_ref[i]
        full = jnp.int32(0)
        for s in range(slots):
            used[s] = jnp.minimum(rows_of[s], rank_of[s])
            factor[s] = (rank_of[s] < rows_of[s]).astype(jnp.int32)
            begin_ref[s] = used[s - 1] if s % 2 else jnp.int32(0)
            if s % 2:
                full = jnp.maximum(full, used[s - 1] + used[s])
        full_ref[0] = full

        def tables(row):
            spot, code = jnp.zeros_like(row), jnp.zeros_like(row)
            for i, (low, high, slot) in enumerate(starts):
                hit = (row >= low) & (row < high)
                spot = jnp.where(hit, row + (order[i] + begin_ref[slot]), spot)
                code = jnp.where(hit, slot + 32 * factor[slot] + 64 * rank_of[slot], code)
            return spot, code & 31, (code >> 5) & 1, code >> 6

        here = position_ref[0]
        spot, slot, by_factor, _ = tables(lax.broadcasted_iota(jnp.int32, (total_rows, limit), 0))
        code_ref[...] = slot + 32 * by_factor + 64 * spot

        lane = lax.broadcasted_iota(jnp.int32, (total_rows // 2, limit), 1)
        row = lax.broadcasted_iota(jnp.int32, (total_rows // 2, limit), 0)
        _, slot, _, rank = tables(row + (lane >> shift) * (total_rows // 2))
        own_ref[...] = jnp.where(slot == here, 1.0, 0.0)
        scale = ADAPTER_ALPHA / rank.astype(jnp.float32)
        inside = ((slot >> 1) == (here >> 1)) & ((lane & (rank_width - 1)) < rank)
        gain_ref[...] = jnp.where(inside, scale, 0.0)

        spot, slot, by_factor, _ = tables(lax.broadcasted_iota(jnp.int32, (8, total_rows), 1))
        mine = ((slot >> 1) == (here >> 1)) & (by_factor == 0)
        spot = jnp.broadcast_to(jnp.where(mine, spot, -1)[:1], (limit, total_rows))
        line = lax.broadcasted_iota(jnp.int32, (limit, total_rows), 0)
        choose_ref[...] = jnp.where(line == spot, 1.0, 0.0).astype(jnp.bfloat16)

        line = lax.broadcasted_iota(jnp.int32, (limit, limit), 0)
        lane = lax.broadcasted_iota(jnp.int32, (limit, limit), 1)
        half, column = lane >> shift, lane & (rank_width - 1)
        other = here ^ 1
        begin = jnp.where(half == 0, begin_ref[here], begin_ref[other])
        many = jnp.where(half == 0, used[here], used[other])
        kind = jnp.where(half == 0, factor[here], factor[other])
        held = (line == begin + column) & (column < many) & (kind == 1)
        fixed_ref[...] = jnp.where(held, 1.0, 0.0).astype(jnp.bfloat16)
        live = (line >= begin) & (line < begin + many) & (kind == 0)
        live_ref[...] = jnp.where(live, 1.0, 0.0)

    smem, whole = pl.BlockSpec(memory_space=pltpu.SMEM), pl.BlockSpec(memory_space=pltpu.VMEM)
    return pl.pallas_call(
        kernel,
        in_specs=[pl.BlockSpec(memory_space=pltpu.HBM)] * 4 + [smem],
        out_specs=[whole] * 6 + [smem] * 2,
        out_shape=[
            jax.ShapeDtypeStruct((total_rows // 2, limit), jnp.float32),
            jax.ShapeDtypeStruct((total_rows // 2, limit), jnp.float32),
            jax.ShapeDtypeStruct((limit, total_rows), jnp.bfloat16),
            jax.ShapeDtypeStruct((limit, limit), jnp.float32),
            jax.ShapeDtypeStruct((limit, limit), jnp.bfloat16),
            jax.ShapeDtypeStruct((total_rows, limit), jnp.int32),
            jax.ShapeDtypeStruct((slots,), jnp.int32),
            jax.ShapeDtypeStruct((1,), jnp.int32),
        ],
        scratch_shapes=[pltpu.SMEM((slots,), jnp.int32)] * 4
        + [pltpu.SMEM((segments,), jnp.int32)]
        + [pltpu.SMEM((slots,), jnp.int32)] * 2
        + [pltpu.SMEM((segments,), jnp.int32)] * 2
        + [pltpu.SemaphoreType.DMA((4,))],
        compiler_params=vmem(16 * total_rows * limit),
        cost_estimate=pl.CostEstimate(
            flops=200 * total_rows * limit, bytes_accessed=16 * total_rows * limit, transcendentals=0
        ),
    )(ranks, adapter_slot, segment_lengths, segment_adapter, position)


def collect_rows(blocks, places, core, own_down, other_down, own):
    count = len(blocks)
    height, features = blocks[0].shape
    height = height // 2
    rank_width = other_down.shape[0]
    half_rows = own.shape[0]
    chunk = 1024 if features % 1024 == 0 else features
    chunks = features // chunk

    def kernel(places_ref, core_ref, own_ref, *refs):
        sources, own_down_ref, other_down_ref = refs[:count], refs[count], refs[count + 1]
        rows_ref, shrink_ref, downs, sems = refs[count + 2 :]
        groups = []
        for k in range(chunks):
            columns = pl.ds(k * chunk, chunk)
            offset = pl.multiple_of(core_ref[0] * features + k * chunk, chunk)
            copies = [
                pltpu.make_async_copy(
                    own_down_ref.at[:, pl.ds(offset, chunk)],
                    downs.at[pl.ds(0, rank_width), columns],
                    sems.at[k, 2 * count],
                ),
                pltpu.make_async_copy(
                    other_down_ref.at[:, columns],
                    downs.at[pl.ds(rank_width, rank_width), columns],
                    sems.at[k, 2 * count + 1],
                ),
            ]
            for i in range(2 * count):
                start = pl.multiple_of(places_ref[i] * height, height)
                copies.append(
                    pltpu.make_async_copy(
                        sources[i // 2].at[pl.ds(i % 2 * height, height), columns],
                        rows_ref.at[pl.ds(start, height), columns],
                        sems.at[k, i],
                    )
                )
            groups.append(copies)
            for copy in copies:
                copy.start()
        shrink = jnp.zeros((2 * half_rows, 2 * rank_width), jnp.float32)
        for k in range(chunks):
            for copy in groups[k]:
                copy.wait()
            columns = pl.ds(k * chunk, chunk)
            shrink = shrink + lax.dot_general(
                rows_ref[:, columns],
                downs[:, columns],
                (((1,), (1,)), ((), ())),
                preferred_element_type=jnp.float32,
            )
        top, bottom = shrink[:half_rows], shrink[half_rows:]
        first = jnp.concatenate([top[:, :rank_width], bottom[:, :rank_width]], axis=1)
        second = jnp.concatenate([top[:, rank_width:], bottom[:, rank_width:]], axis=1)
        shrink_ref[...] = jnp.where(own_ref[...] > 0.5, first, second)

    smem, whole = pl.BlockSpec(memory_space=pltpu.SMEM), pl.BlockSpec(memory_space=pltpu.VMEM)
    rows = 2 * count * height
    return pl.pallas_call(
        kernel,
        in_specs=[smem, smem, whole] + [pl.BlockSpec(memory_space=pl.ANY)] * (count + 2),
        out_specs=[whole] * 2,
        out_shape=[
            jax.ShapeDtypeStruct((rows, features), blocks[0].dtype),
            jax.ShapeDtypeStruct(own.shape, jnp.float32),
        ],
        scratch_shapes=[
            pltpu.VMEM((2 * rank_width, features), own_down.dtype),
            pltpu.SemaphoreType.DMA((chunks, 2 * count + 2)),
        ],
        compiler_params=vmem(4 * rows * features),
        cost_estimate=pl.CostEstimate(
            flops=4 * rows * features * rank_width,
            bytes_accessed=4 * rows * features,
            transcendentals=0,
        ),
    )(places, core, own, *blocks, own_down, other_down)


def build_payload(choose, live, fixed, coeff, mine, other, first, count):
    chips, rank_width, width = mine.shape

    half_rows = coeff.shape[0]

    def kernel(choose_ref, live_ref, fixed_ref, coeff_ref, mine_ref, other_ref, out_ref):
        lines = pl.ds(first, count)
        folded = coeff_ref[...]
        top = jnp.dot(choose_ref[lines, :half_rows], folded, preferred_element_type=jnp.float32)
        low = jnp.dot(choose_ref[lines, half_rows:], folded, preferred_element_type=jnp.float32)
        chosen = top[:, :rank_width] + low[:, rank_width:]
        select = jnp.concatenate([chosen, chosen], axis=1) * live_ref[lines]
        select = (select + fixed_ref[lines].astype(jnp.float32)).astype(jnp.bfloat16)

        @pl.loop(0, chips)
        def _(q):
            out_ref[q] = jnp.dot(
                select,
                jnp.concatenate([mine_ref[q], other_ref[q]], axis=0),
                preferred_element_type=jnp.float32,
            ).astype(out_ref.dtype)

    return pl.pallas_call(
        kernel,
        in_specs=[pl.BlockSpec(memory_space=pltpu.VMEM)] * 6,
        out_specs=pl.BlockSpec(memory_space=pltpu.VMEM),
        out_shape=jax.ShapeDtypeStruct((chips, count, width), mine.dtype),
        compiler_params=vmem(4 * chips * width * (2 * rank_width + count)),
        cost_estimate=pl.CostEstimate(
            flops=4 * chips * count * rank_width * width,
            bytes_accessed=2 * chips * width * (2 * rank_width + count),
            transcendentals=0,
        ),
    )(choose, live, fixed, coeff, mine, other)


def combine(base, code, begin, more, coeff, incoming, extra):
    total_rows, width = base.shape
    chips, first, _ = incoming.shape
    second = extra.shape[1]
    limit = first + second
    rank_width = limit // 2
    shift = rank_width.bit_length() - 1
    tile = 256 if width % 256 == 0 else 128

    def kernel(
        begin_ref, more_ref, base_ref, code_ref, coeff_ref, incoming_ref, extra_ref,
        out_ref, late, base_part, near_rows, sems,
    ):
        fetch = pltpu.make_async_copy(extra_ref, late, sems.at[0])
        get_base = pltpu.make_async_copy(base_ref, base_part, sems.at[1])
        get_near = pltpu.make_async_copy(incoming_ref, near_rows, sems.at[2])
        get_near.start()
        get_base.start()
        folded = coeff_ref[...].astype(jnp.float32)
        both = jnp.concatenate(
            [
                jnp.concatenate([part, part], axis=1)
                for part in (folded[:, :rank_width], folded[:, rank_width:])
            ],
            axis=0,
        )
        code_value = code_ref[...]
        slot, by_factor, spot = code_value & 31, (code_value >> 5) & 1, code_value >> 6
        lane = lax.broadcasted_iota(jnp.int32, (total_rows, limit), 1)
        owned = jnp.where(by_factor == 1, slot, -1) - (lane >> shift)
        finished = jnp.where(by_factor == 0, spot, -1)[:, :1]
        finished_chip = (slot >> 1)[:, :1]

        def weights(low, count):
            target = finished - low
            target = jnp.where((target >= 0) & (target < count), finished_chip * count + target, -1)
            wide = lax.broadcasted_iota(jnp.int32, (total_rows, chips * count), 1)
            total = jnp.where(wide == target, 1.0, 0.0)
            line = lax.broadcasted_iota(jnp.int32, (limit, chips * count), 0)
            place = lax.broadcasted_iota(jnp.int32, (limit, chips * count), 1)
            for q in range(chips):
                goal = jnp.where(
                    line < rank_width, line, line - rank_width + begin_ref[2 * q + 1]
                ) - low
                moved = (goal >= 0) & (goal < count) & (place == q * count + goal)
                moved = jnp.where(moved, 1.0, 0.0).astype(jnp.bfloat16)
                part = jnp.where(owned == 2 * q, both, 0.0).astype(jnp.bfloat16)
                total = total + jnp.dot(part, moved, preferred_element_type=jnp.float32)
            return total.astype(jnp.bfloat16)

        near = weights(0, first)
        get_near.wait()
        get_base.wait()

        def write(far):
            @pl.loop(0, width // tile)
            def _(i):
                columns = pl.ds(pl.multiple_of(i * tile, tile), tile)
                block = near_rows[:, :, columns].reshape(chips * first, tile)
                total = jnp.dot(near, block, preferred_element_type=jnp.float32)
                total += base_part[:, columns]
                if far is not None:
                    block = late[:, :, columns].reshape(chips * second, tile)
                    total += jnp.dot(far, block, preferred_element_type=jnp.float32)
                out_ref[:, columns] = total.astype(out_ref.dtype)

        @pl.when(more_ref[0] > first)
        def _():
            fetch.start()
            far = weights(first, second)
            fetch.wait()
            write(far)

        @pl.when(more_ref[0] <= first)
        def _():
            write(None)

    smem, whole = pl.BlockSpec(memory_space=pltpu.SMEM), pl.BlockSpec(memory_space=pltpu.VMEM)
    return pl.pallas_call(
        kernel,
        in_specs=[smem] * 2
        + [pl.BlockSpec(memory_space=pl.ANY)]
        + [whole] * 2
        + [pl.BlockSpec(memory_space=pl.ANY)] * 2,
        out_specs=whole,
        out_shape=jax.ShapeDtypeStruct((total_rows, width), jnp.bfloat16),
        scratch_shapes=[
            pltpu.VMEM(extra.shape, extra.dtype),
            pltpu.VMEM(base.shape, base.dtype),
            pltpu.VMEM(incoming.shape, incoming.dtype),
            pltpu.SemaphoreType.DMA((3,)),
        ],
        compiler_params=vmem(8 * total_rows * width + 2 * chips * limit * width),
        cost_estimate=pl.CostEstimate(
            flops=4 * total_rows * chips * limit * width,
            bytes_accessed=6 * total_rows * width + 2 * chips * limit * width,
            transcendentals=0,
        ),
    )(begin, more, base, code, coeff, incoming, extra)


def ring_gather(block, shards, halfway):
    chips = shards // 2
    depth = chips // 2
    cycle = list(range(0, chips, 2)) + list(range(chips - 1, 0, -2))
    ahead = [
        (2 * cycle[p] + c, 2 * cycle[(p + 1) % chips] + c) for p in range(chips) for c in range(2)
    ]
    back = [(b, a) for a, b in ahead]
    held = {0: block}
    for step in range(1, depth + 1):
        held[-step] = lax.ppermute(held[1 - step], "tensor", ahead)
        if step < chips - depth:
            held[step] = lax.ppermute(held[step - 1], "tensor", back)
        held[-step] = halfway(step, held[-step])
    table = np.zeros((shards, shards), np.int32)
    for t in range(shards):
        for i, offset in enumerate(held):
            chip = cycle[(cycle.index(t // 2) + offset) % chips]
            table[t, 2 * i], table[t, 2 * i + 1] = 2 * chip + t % 2, 2 * chip + 1 - t % 2
    places = lax.dynamic_index_in_dim(table, lax.axis_index("tensor"), keepdims=False)
    return list(held.values()), places


def largest_over_groups(value):
    groups = lax.axis_size("groups")
    for shift in range(1, groups):
        other = lax.ppermute(value, "groups", [(g, (g + shift) % groups) for g in range(groups)])
        value = jnp.maximum(value, other)
    return value


def pooled(
    input_rows,
    up_weight,
    adapter_down,
    adapter_up,
    ranks,
    adapter_slot,
    segment_lengths,
    segment_adapter,
):
    shards = lax.axis_size("tensor")
    position = lax.axis_index("tensor").astype(jnp.int32)
    chips = shards // 2
    total_rows = input_rows.shape[0] * shards
    rank_width = adapter_up.shape[1]
    limit = 2 * rank_width
    sibling = [(t, t ^ 1) for t in range(shards)]
    same_core = [list(range(c, shards, 2)) for c in range(2)]

    core = position & 1
    features = input_rows.shape[1] // 2

    def swap(value):
        keep = lax.dynamic_slice_in_dim(value, core * features, features, 1)
        send = lax.dynamic_slice_in_dim(value, (1 - core) * features, features, 1)
        return keep, lax.ppermute(send, "tensor", sibling)

    block = jnp.concatenate(swap(input_rows), axis=0)
    tables = describe(
        ranks, adapter_slot, segment_lengths, segment_adapter, position[None], total_rows, limit
    )
    gain, own, choose, live, fixed, code, begin, full = tables
    fullest = largest_over_groups(full)
    packed = ()

    def halfway(step, piece):
        nonlocal packed, own
        if step == 1:
            piece, own, which = lax.optimization_barrier((piece, own, core[None]))
            mine, other, down_half = split_for_pair(
                adapter_up[0], adapter_down[0], which, chips
            )
            packed = (mine, other, down_half)
        if step == 2:
            piece, packed = lax.optimization_barrier((piece, packed))
            mine, other, down_half = packed
            other = lax.ppermute(other, "tensor", sibling)
            packed = (mine, other, lax.ppermute(down_half, "tensor", sibling))
        if step == 3:
            piece, packed = lax.optimization_barrier((piece, packed))
        return piece

    blocks, places = ring_gather(block, shards, halfway)
    mine, other, down_half = packed
    rows, shrink = collect_rows(blocks, places, core[None], adapter_down[0], down_half, own)
    shrink = shrink + lax.ppermute(shrink, "tensor", sibling)
    coeff = (shrink * gain).astype(jnp.bfloat16)
    coeff, rows, fullest = lax.optimization_barrier((coeff, rows, fullest))

    def payload(low, count):
        return build_payload(choose, live, fixed, coeff, mine, other, low, count)

    def exchange(value):
        return lax.all_to_all(
            value,
            "tensor",
            split_axis=0,
            concat_axis=0,
            axis_index_groups=same_core,
            tiled=True,
        )

    near = payload(0, FIRST_ROWS)
    rows_other = lax.ppermute(rows, "tensor", sibling)
    every, bit = coeff, 2
    while bit < shards:
        every = every + lax.ppermute(every, "tensor", [(t, t ^ bit) for t in range(shards)])
        if bit == 2:
            every, near = lax.optimization_barrier((every, near))
        bit *= 2
    near, every, rows, rows_other = lax.optimization_barrier((near, every, rows, rows_other))
    incoming = exchange(near)
    halves = [jnp.where(core == c, rows, rows_other) for c in range(2)]
    base = jnp.dot(
        jnp.concatenate(halves, axis=1), up_weight, preferred_element_type=jnp.float32
    )
    fullest, base, incoming = lax.optimization_barrier((fullest, base, incoming))
    rest = limit - FIRST_ROWS

    def later(count):
        def run():
            value = jnp.zeros((chips, rest - count, up_weight.shape[1]), adapter_up.dtype)
            if count:
                late = exchange(payload(FIRST_ROWS, count))
                value = jnp.concatenate([late, value], axis=1)
            return value

        return run

    sizes = (0,) + tuple(size for size in MORE_ROWS if size < rest) + (rest,)
    which = sum((fullest[0] > FIRST_ROWS + size).astype(jnp.int32) for size in sizes[:-1])
    extra = lax.switch(which, [later(size) for size in sizes])
    return combine(base, code, begin, fullest, every, incoming, extra)


def gathered(input_rows, up_weight, adapter_down, adapter_up, slot_row, row_rank):
    shards = lax.axis_size("tensor")
    position = lax.axis_index("tensor")
    total_rows = input_rows.shape[0] * shards
    stored, rank_width, hidden = adapter_up.shape
    width = hidden // shards
    slots = shards * stored
    outgoing = jnp.stack(
        [adapter_up[:, :, i * width : (i + 1) * width] for i in range(shards)], axis=0
    )
    incoming = lax.all_to_all(outgoing, "tensor", split_axis=0, concat_axis=0, tiled=True)
    rows = lax.all_gather(input_rows, "tensor", axis=0, tiled=True)
    shrink = jnp.einsum("gf,ojf->ogj", rows, adapter_down, preferred_element_type=jnp.float32)
    own = position * stored + jnp.arange(stored, dtype=jnp.int32)
    inside = jnp.arange(rank_width, dtype=jnp.int32)[None, :] < row_rank[:, None]
    keep = (slot_row[None, :] == own[:, None])[:, :, None] & inside[None]
    scale = ADAPTER_ALPHA / row_rank.astype(jnp.float32)
    own_coeff = jnp.where(keep, shrink * scale[None, :, None], 0.0).astype(jnp.bfloat16)
    base = jnp.dot(rows, up_weight, preferred_element_type=jnp.float32)
    own_coeff, base = lax.optimization_barrier((own_coeff, base))
    coeff = lax.all_gather(own_coeff, "tensor", axis=0, tiled=True)
    placed = coeff.transpose(1, 0, 2).reshape(total_rows, slots * rank_width)
    factors = incoming.reshape(slots * rank_width, width)
    term = jnp.dot(placed, factors, preferred_element_type=jnp.float32)
    return (base + term).astype(jnp.bfloat16)


def on_device(
    input_rows,
    up_weight,
    adapter_down,
    adapter_up,
    ranks,
    adapter_slot,
    segment_lengths,
    segment_adapter,
):
    shards = lax.axis_size("tensor")
    stored, rank_width, _ = adapter_up.shape
    tiled = up_weight.shape[1] % 128 == 0 and input_rows.shape[0] % 16 == 0 and rank_width == 64
    tiled = tiled and input_rows.shape[1] % 256 == 0 and input_rows.shape[0] * shards <= 256
    if shards == POOLED_SHARDS and stored == 1 and tiled:
        return pooled(
            input_rows,
            up_weight,
            adapter_down,
            adapter_up,
            ranks,
            adapter_slot,
            segment_lengths,
            segment_adapter,
        )
    slot_row, row_rank = row_tables(
        input_rows.shape[0] * shards, ranks, adapter_slot, segment_lengths, segment_adapter
    )
    return gathered(input_rows, up_weight, adapter_down, adapter_up, slot_row, row_rank)


def solution(mesh):
    placed = (
        P(("groups", "tensor"), None),
        P(None, "tensor"),
        P(("groups", "tensor"), None, None),
        P(("groups", "tensor"), None, None),
        P("groups"),
        P("groups"),
        P("groups"),
        P("groups"),
    )
    return jax.shard_map(
        on_device, mesh=mesh, in_specs=placed, out_specs=P("groups", "tensor"), check_vma=False
    )
```

```python
import jax
import jax.numpy as jnp
import numpy as np
from jax import lax
from jax.experimental import pallas as pl
from jax.experimental.pallas import tpu as pltpu
from jax.sharding import PartitionSpec as P

ADAPTER_ALPHA = 32.0
POOLED_SHARDS = 16
FIRST_ROWS = 64
MORE_ROWS = (16, 32)
WIDE_GRANT = 56 << 20


def row_tables(row_count, ranks, adapter_slot, segment_lengths, segment_adapter):
    seg_ends = jnp.cumsum(segment_lengths)
    positions = jnp.arange(row_count, dtype=jnp.int32)
    seg_row = jnp.sum((seg_ends[None, :] <= positions[:, None]).astype(jnp.int32), axis=1)
    seg_pick = (
        seg_row[:, None] == jnp.arange(segment_lengths.shape[0], dtype=jnp.int32)[None, :]
    ).astype(jnp.int32)
    adapter_row = jnp.sum(seg_pick * segment_adapter[None, :], axis=1)
    pool_pick = (
        adapter_row[:, None] == jnp.arange(ranks.shape[0], dtype=jnp.int32)[None, :]
    ).astype(jnp.int32)
    slot_row = jnp.sum(pool_pick * adapter_slot[None, :], axis=1)
    row_rank_values = jnp.sum(pool_pick * ranks[None, :], axis=1)
    return (slot_row, row_rank_values)


def vmem(buffers):
    return pltpu.CompilerParams(vmem_limit_bytes=buffers + (8 << 20))


def split_for_pair(up_factor, down_factor, core, chips):
    rank_width, hidden = up_factor.shape
    width = hidden // (2 * chips)
    features = down_factor.shape[1] // 2

    def kernel(core_ref, source, down, mine, other, half_down, sems):
        core = core_ref[0]
        start = pl.multiple_of((1 - core) * features, features)
        copies = [
            pltpu.make_async_copy(
                down.at[:, pl.ds(start, features)], half_down, sems.at[2 * chips]
            )
        ]
        for q in range(chips):
            for i, (target, half) in enumerate(((other, 1 - core), (mine, core))):
                start = pl.multiple_of((2 * q + half) * width, width)
                copies.append(
                    pltpu.make_async_copy(
                        source.at[:, pl.ds(start, width)], target.at[q], sems.at[2 * q + i]
                    )
                )
        for copy in copies:
            copy.start()
        for copy in copies:
            copy.wait()

    block = jax.ShapeDtypeStruct((chips, rank_width, width), up_factor.dtype)
    return pl.pallas_call(
        kernel,
        in_specs=[pl.BlockSpec(memory_space=pltpu.SMEM)]
        + [pl.BlockSpec(memory_space=pltpu.HBM)] * 2,
        out_specs=[pl.BlockSpec(memory_space=pltpu.VMEM)] * 3,
        out_shape=[
            block, block, jax.ShapeDtypeStruct((rank_width, features), down_factor.dtype)
        ],
        scratch_shapes=[pltpu.SemaphoreType.DMA((2 * chips + 1,))],
        compiler_params=pltpu.CompilerParams(vmem_limit_bytes=WIDE_GRANT),
        cost_estimate=pl.CostEstimate(
            flops=0, bytes_accessed=4 * rank_width * hidden, transcendentals=0
        ),
    )(core, up_factor, down_factor)


def describe(ranks, adapter_slot, segment_lengths, segment_adapter, position, total_rows, limit):
    slots, segments = ranks.shape[0], segment_lengths.shape[0]
    rank_width = limit // 2
    shift = rank_width.bit_length() - 1

    def kernel(
        ranks_in, home_in, length_in, adapter_in, position_ref,
        gain_ref, own_ref, choose_ref, live_ref, fixed_ref, code_ref, begin_ref, full_ref,
        rank_of, rows_of, used, factor, order, ranks_ref, home_ref, length_ref, adapter_ref, sems,
    ):
        pairs = zip(
            (ranks_in, home_in, length_in, adapter_in),
            (ranks_ref, home_ref, length_ref, adapter_ref),
        )
        copies = [
            pltpu.make_async_copy(source, target, sems.at[i])
            for i, (source, target) in enumerate(pairs)
        ]
        for copy in copies:
            copy.start()
        for copy in copies:
            copy.wait()
        for a in range(slots):
            rows_of[a] = 0
            rank_of[home_ref[a]] = ranks_ref[a]
        starts, start = [], jnp.int32(0)
        for i in range(segments):
            slot = home_ref[adapter_ref[i]]
            starts.append((start, start + length_ref[i], slot))
            order[i] = rows_of[slot] - start
            rows_of[slot] = rows_of[slot] + length_ref[i]
            start = start + length_ref[i]
        full = jnp.int32(0)
        for s in range(slots):
            used[s] = jnp.minimum(rows_of[s], rank_of[s])
            factor[s] = (rank_of[s] < rows_of[s]).astype(jnp.int32)
            begin_ref[s] = used[s - 1] if s % 2 else jnp.int32(0)
            if s % 2:
                full = jnp.maximum(full, used[s - 1] + used[s])
        full_ref[0] = full

        def tables(row):
            spot, code = jnp.zeros_like(row), jnp.zeros_like(row)
            for i, (low, high, slot) in enumerate(starts):
                hit = (row >= low) & (row < high)
                spot = jnp.where(hit, row + (order[i] + begin_ref[slot]), spot)
                code = jnp.where(hit, slot + 32 * factor[slot] + 64 * rank_of[slot], code)
            return spot, code & 31, (code >> 5) & 1, code >> 6

        here = position_ref[0]
        spot, slot, by_factor, _ = tables(lax.broadcasted_iota(jnp.int32, (total_rows, limit), 0))
        code_ref[...] = slot + 32 * by_factor + 64 * spot

        lane = lax.broadcasted_iota(jnp.int32, (total_rows // 2, limit), 1)
        row = lax.broadcasted_iota(jnp.int32, (total_rows // 2, limit), 0)
        _, slot, _, rank = tables(row + (lane >> shift) * (total_rows // 2))
        own_ref[...] = jnp.where(slot == here, 1.0, 0.0)
        scale = ADAPTER_ALPHA / rank.astype(jnp.float32)
        inside = ((slot >> 1) == (here >> 1)) & ((lane & (rank_width - 1)) < rank)
        gain_ref[...] = jnp.where(inside, scale, 0.0)

        spot, slot, by_factor, _ = tables(lax.broadcasted_iota(jnp.int32, (8, total_rows), 1))
        mine = ((slot >> 1) == (here >> 1)) & (by_factor == 0)
        spot = jnp.broadcast_to(jnp.where(mine, spot, -1)[:1], (limit, total_rows))
        line = lax.broadcasted_iota(jnp.int32, (limit, total_rows), 0)
        choose_ref[...] = jnp.where(line == spot, 1.0, 0.0).astype(jnp.bfloat16)

        line = lax.broadcasted_iota(jnp.int32, (limit, limit), 0)
        lane = lax.broadcasted_iota(jnp.int32, (limit, limit), 1)
        half, column = lane >> shift, lane & (rank_width - 1)
        other = here ^ 1
        begin = jnp.where(half == 0, begin_ref[here], begin_ref[other])
        many = jnp.where(half == 0, used[here], used[other])
        kind = jnp.where(half == 0, factor[here], factor[other])
        held = (line == begin + column) & (column < many) & (kind == 1)
        fixed_ref[...] = jnp.where(held, 1.0, 0.0).astype(jnp.bfloat16)
        live = (line >= begin) & (line < begin + many) & (kind == 0)
        live_ref[...] = jnp.where(live, 1.0, 0.0)

    smem, whole = pl.BlockSpec(memory_space=pltpu.SMEM), pl.BlockSpec(memory_space=pltpu.VMEM)
    return pl.pallas_call(
        kernel,
        in_specs=[pl.BlockSpec(memory_space=pltpu.HBM)] * 4 + [smem],
        out_specs=[whole] * 6 + [smem] * 2,
        out_shape=[
            jax.ShapeDtypeStruct((total_rows // 2, limit), jnp.float32),
            jax.ShapeDtypeStruct((total_rows // 2, limit), jnp.float32),
            jax.ShapeDtypeStruct((limit, total_rows), jnp.bfloat16),
            jax.ShapeDtypeStruct((limit, limit), jnp.float32),
            jax.ShapeDtypeStruct((limit, limit), jnp.bfloat16),
            jax.ShapeDtypeStruct((total_rows, limit), jnp.int32),
            jax.ShapeDtypeStruct((slots,), jnp.int32),
            jax.ShapeDtypeStruct((1,), jnp.int32),
        ],
        scratch_shapes=[pltpu.SMEM((slots,), jnp.int32)] * 4
        + [pltpu.SMEM((segments,), jnp.int32)]
        + [pltpu.SMEM((slots,), jnp.int32)] * 2
        + [pltpu.SMEM((segments,), jnp.int32)] * 2
        + [pltpu.SemaphoreType.DMA((4,))],
        compiler_params=vmem(16 * total_rows * limit),
        cost_estimate=pl.CostEstimate(
            flops=200 * total_rows * limit, bytes_accessed=16 * total_rows * limit, transcendentals=0
        ),
    )(ranks, adapter_slot, segment_lengths, segment_adapter, position)


def collect_rows(blocks, places, core, own_down, other_down, own):
    count = len(blocks)
    height, features = blocks[0].shape
    height = height // 2
    rank_width = other_down.shape[0]
    half_rows = own.shape[0]
    chunk = 1024 if features % 1024 == 0 else features
    chunks = features // chunk

    def kernel(places_ref, core_ref, own_ref, *refs):
        sources, own_down_ref, other_down_ref = refs[:count], refs[count], refs[count + 1]
        rows_ref, shrink_ref, downs, sems = refs[count + 2 :]
        groups = []
        for k in range(chunks):
            columns = pl.ds(k * chunk, chunk)
            offset = pl.multiple_of(core_ref[0] * features + k * chunk, chunk)
            copies = [
                pltpu.make_async_copy(
                    own_down_ref.at[:, pl.ds(offset, chunk)],
                    downs.at[pl.ds(0, rank_width), columns],
                    sems.at[k, 2 * count],
                ),
                pltpu.make_async_copy(
                    other_down_ref.at[:, columns],
                    downs.at[pl.ds(rank_width, rank_width), columns],
                    sems.at[k, 2 * count + 1],
                ),
            ]
            for i in range(2 * count):
                start = pl.multiple_of(places_ref[i] * height, height)
                copies.append(
                    pltpu.make_async_copy(
                        sources[i // 2].at[pl.ds(i % 2 * height, height), columns],
                        rows_ref.at[pl.ds(start, height), columns],
                        sems.at[k, i],
                    )
                )
            groups.append(copies)
            for copy in copies:
                copy.start()
        shrink = jnp.zeros((2 * half_rows, 2 * rank_width), jnp.float32)
        for k in range(chunks):
            for copy in groups[k]:
                copy.wait()
            columns = pl.ds(k * chunk, chunk)
            shrink = shrink + lax.dot_general(
                rows_ref[:, columns],
                downs[:, columns],
                (((1,), (1,)), ((), ())),
                preferred_element_type=jnp.float32,
            )
        top, bottom = shrink[:half_rows], shrink[half_rows:]
        first = jnp.concatenate([top[:, :rank_width], bottom[:, :rank_width]], axis=1)
        second = jnp.concatenate([top[:, rank_width:], bottom[:, rank_width:]], axis=1)
        shrink_ref[...] = jnp.where(own_ref[...] > 0.5, first, second)

    smem, whole = pl.BlockSpec(memory_space=pltpu.SMEM), pl.BlockSpec(memory_space=pltpu.VMEM)
    rows = 2 * count * height
    return pl.pallas_call(
        kernel,
        in_specs=[smem, smem, whole] + [pl.BlockSpec(memory_space=pl.ANY)] * (count + 2),
        out_specs=[whole] * 2,
        out_shape=[
            jax.ShapeDtypeStruct((rows, features), blocks[0].dtype),
            jax.ShapeDtypeStruct(own.shape, jnp.float32),
        ],
        scratch_shapes=[
            pltpu.VMEM((2 * rank_width, features), own_down.dtype),
            pltpu.SemaphoreType.DMA((chunks, 2 * count + 2)),
        ],
        compiler_params=vmem(4 * rows * features),
        cost_estimate=pl.CostEstimate(
            flops=4 * rows * features * rank_width,
            bytes_accessed=4 * rows * features,
            transcendentals=0,
        ),
    )(places, core, own, *blocks, own_down, other_down)


def build_payload(choose, live, fixed, coeff, mine, other, first, count):
    chips, rank_width, width = mine.shape

    half_rows = coeff.shape[0]

    def kernel(choose_ref, live_ref, fixed_ref, coeff_ref, mine_ref, other_ref, out_ref):
        lines = pl.ds(first, count)
        folded = coeff_ref[...]
        top = jnp.dot(choose_ref[lines, :half_rows], folded, preferred_element_type=jnp.float32)
        low = jnp.dot(choose_ref[lines, half_rows:], folded, preferred_element_type=jnp.float32)
        chosen = top[:, :rank_width] + low[:, rank_width:]
        select = jnp.concatenate([chosen, chosen], axis=1) * live_ref[lines]
        select = (select + fixed_ref[lines].astype(jnp.float32)).astype(jnp.bfloat16)

        @pl.loop(0, chips)
        def _(q):
            out_ref[q] = jnp.dot(
                select,
                jnp.concatenate([mine_ref[q], other_ref[q]], axis=0),
                preferred_element_type=jnp.float32,
            ).astype(out_ref.dtype)

    return pl.pallas_call(
        kernel,
        in_specs=[pl.BlockSpec(memory_space=pltpu.VMEM)] * 6,
        out_specs=pl.BlockSpec(memory_space=pltpu.VMEM),
        out_shape=jax.ShapeDtypeStruct((chips, count, width), mine.dtype),
        compiler_params=vmem(4 * chips * width * (2 * rank_width + count)),
        cost_estimate=pl.CostEstimate(
            flops=4 * chips * count * rank_width * width,
            bytes_accessed=2 * chips * width * (2 * rank_width + count),
            transcendentals=0,
        ),
    )(choose, live, fixed, coeff, mine, other)


def combine(base, code, begin, more, coeff, incoming, extra):
    total_rows, width = base.shape
    chips, first, _ = incoming.shape
    second = extra.shape[1]
    limit = first + second
    rank_width = limit // 2
    shift = rank_width.bit_length() - 1
    tile = 256 if width % 256 == 0 else 128

    def kernel(
        begin_ref, more_ref, base_ref, code_ref, coeff_ref, incoming_ref, extra_ref,
        out_ref, late, base_part, near_rows, sems,
    ):
        fetch = pltpu.make_async_copy(extra_ref, late, sems.at[0])
        get_base = pltpu.make_async_copy(base_ref, base_part, sems.at[1])
        get_near = pltpu.make_async_copy(incoming_ref, near_rows, sems.at[2])
        get_near.start()
        get_base.start()
        folded = coeff_ref[...].astype(jnp.float32)
        both = jnp.concatenate(
            [
                jnp.concatenate([part, part], axis=1)
                for part in (folded[:, :rank_width], folded[:, rank_width:])
            ],
            axis=0,
        )
        code_value = code_ref[...]
        slot, by_factor, spot = code_value & 31, (code_value >> 5) & 1, code_value >> 6
        lane = lax.broadcasted_iota(jnp.int32, (total_rows, limit), 1)
        owned = jnp.where(by_factor == 1, slot, -1) - (lane >> shift)
        finished = jnp.where(by_factor == 0, spot, -1)[:, :1]
        finished_chip = (slot >> 1)[:, :1]

        def weights(low, count):
            target = finished - low
            target = jnp.where((target >= 0) & (target < count), finished_chip * count + target, -1)
            wide = lax.broadcasted_iota(jnp.int32, (total_rows, chips * count), 1)
            total = jnp.where(wide == target, 1.0, 0.0)
            line = lax.broadcasted_iota(jnp.int32, (limit, chips * count), 0)
            place = lax.broadcasted_iota(jnp.int32, (limit, chips * count), 1)
            for q in range(chips):
                goal = jnp.where(
                    line < rank_width, line, line - rank_width + begin_ref[2 * q + 1]
                ) - low
                moved = (goal >= 0) & (goal < count) & (place == q * count + goal)
                moved = jnp.where(moved, 1.0, 0.0).astype(jnp.bfloat16)
                part = jnp.where(owned == 2 * q, both, 0.0).astype(jnp.bfloat16)
                total = total + jnp.dot(part, moved, preferred_element_type=jnp.float32)
            return total.astype(jnp.bfloat16)

        near = weights(0, first)
        get_near.wait()
        get_base.wait()

        def write(far):
            @pl.loop(0, width // tile)
            def _(i):
                columns = pl.ds(pl.multiple_of(i * tile, tile), tile)
                block = near_rows[:, :, columns].reshape(chips * first, tile)
                total = jnp.dot(near, block, preferred_element_type=jnp.float32)
                total += base_part[:, columns]
                if far is not None:
                    block = late[:, :, columns].reshape(chips * second, tile)
                    total += jnp.dot(far, block, preferred_element_type=jnp.float32)
                out_ref[:, columns] = total.astype(out_ref.dtype)

        @pl.when(more_ref[0] > first)
        def _():
            fetch.start()
            far = weights(first, second)
            fetch.wait()
            write(far)

        @pl.when(more_ref[0] <= first)
        def _():
            write(None)

    smem, whole = pl.BlockSpec(memory_space=pltpu.SMEM), pl.BlockSpec(memory_space=pltpu.VMEM)
    return pl.pallas_call(
        kernel,
        in_specs=[smem] * 2
        + [pl.BlockSpec(memory_space=pl.ANY)]
        + [whole] * 2
        + [pl.BlockSpec(memory_space=pl.ANY)] * 2,
        out_specs=whole,
        out_shape=jax.ShapeDtypeStruct((total_rows, width), jnp.bfloat16),
        scratch_shapes=[
            pltpu.VMEM(extra.shape, extra.dtype),
            pltpu.VMEM(base.shape, base.dtype),
            pltpu.VMEM(incoming.shape, incoming.dtype),
            pltpu.SemaphoreType.DMA((3,)),
        ],
        compiler_params=vmem(8 * total_rows * width + 2 * chips * limit * width),
        cost_estimate=pl.CostEstimate(
            flops=4 * total_rows * chips * limit * width,
            bytes_accessed=6 * total_rows * width + 2 * chips * limit * width,
            transcendentals=0,
        ),
    )(begin, more, base, code, coeff, incoming, extra)


def ring_gather(block, shards, halfway):
    chips = shards // 2
    depth = chips // 2
    cycle = list(range(0, chips, 2)) + list(range(chips - 1, 0, -2))
    ahead = [
        (2 * cycle[p] + c, 2 * cycle[(p + 1) % chips] + c) for p in range(chips) for c in range(2)
    ]
    back = [(b, a) for a, b in ahead]
    held = {0: block}
    for step in range(1, depth + 1):
        held[-step] = lax.ppermute(held[1 - step], "tensor", ahead)
        if step < chips - depth:
            held[step] = lax.ppermute(held[step - 1], "tensor", back)
        held[-step] = halfway(step, held[-step])
    table = np.zeros((shards, shards), np.int32)
    for t in range(shards):
        for i, offset in enumerate(held):
            chip = cycle[(cycle.index(t // 2) + offset) % chips]
            table[t, 2 * i], table[t, 2 * i + 1] = 2 * chip + t % 2, 2 * chip + 1 - t % 2
    places = lax.dynamic_index_in_dim(table, lax.axis_index("tensor"), keepdims=False)
    return list(held.values()), places


def largest_over_groups(value):
    groups = lax.axis_size("groups")
    for shift in range(1, groups):
        other = lax.ppermute(value, "groups", [(g, (g + shift) % groups) for g in range(groups)])
        value = jnp.maximum(value, other)
    return value


def pooled(
    input_rows,
    up_weight,
    adapter_down,
    adapter_up,
    ranks,
    adapter_slot,
    segment_lengths,
    segment_adapter,
):
    shards = lax.axis_size("tensor")
    position = lax.axis_index("tensor").astype(jnp.int32)
    chips = shards // 2
    total_rows = input_rows.shape[0] * shards
    rank_width = adapter_up.shape[1]
    limit = 2 * rank_width
    sibling = [(t, t ^ 1) for t in range(shards)]
    same_core = [list(range(c, shards, 2)) for c in range(2)]

    core = position & 1
    features = input_rows.shape[1] // 2

    def swap(value):
        keep = lax.dynamic_slice_in_dim(value, core * features, features, 1)
        send = lax.dynamic_slice_in_dim(value, (1 - core) * features, features, 1)
        return keep, lax.ppermute(send, "tensor", sibling)

    mine, other, down_half = split_for_pair(adapter_up[0], adapter_down[0], core[None], chips)
    block = jnp.concatenate(swap(input_rows), axis=0)
    block, mine, other, down_half = lax.optimization_barrier((block, mine, other, down_half))
    other = lax.ppermute(other, "tensor", sibling)
    down_half = lax.ppermute(down_half, "tensor", sibling)
    gain, own, choose, live, fixed, code, begin, full = describe(
        ranks, adapter_slot, segment_lengths, segment_adapter, position[None], total_rows, limit
    )
    fullest = largest_over_groups(full)
    pending = [(own, choose), (other, down_half)]

    def halfway(step, piece):
        nonlocal pending
        if step <= len(pending):
            piece, pending[step - 1] = lax.optimization_barrier((piece, pending[step - 1]))
        return piece

    blocks, places = ring_gather(block, shards, halfway)
    (own, choose), (other, down_half) = pending
    rows, shrink = collect_rows(blocks, places, core[None], adapter_down[0], down_half, own)
    shrink = shrink + lax.ppermute(shrink, "tensor", sibling)
    coeff = (shrink * gain).astype(jnp.bfloat16)
    coeff, rows, fullest = lax.optimization_barrier((coeff, rows, fullest))

    def payload(low, count):
        return build_payload(choose, live, fixed, coeff, mine, other, low, count)

    def exchange(value):
        return lax.all_to_all(
            value,
            "tensor",
            split_axis=0,
            concat_axis=0,
            axis_index_groups=same_core,
            tiled=True,
        )

    near = payload(0, FIRST_ROWS)
    rows_other = lax.ppermute(rows, "tensor", sibling)
    every, bit = coeff, 2
    while bit < shards:
        every = every + lax.ppermute(every, "tensor", [(t, t ^ bit) for t in range(shards)])
        if bit == 2:
            every, near = lax.optimization_barrier((every, near))
        bit *= 2
    near, every, rows, rows_other = lax.optimization_barrier((near, every, rows, rows_other))
    incoming = exchange(near)
    halves = [jnp.where(core == c, rows, rows_other) for c in range(2)]
    base = jnp.dot(
        jnp.concatenate(halves, axis=1), up_weight, preferred_element_type=jnp.float32
    )
    fullest, base, incoming = lax.optimization_barrier((fullest, base, incoming))
    rest = limit - FIRST_ROWS

    def later(count):
        def run():
            value = jnp.zeros((chips, rest - count, up_weight.shape[1]), adapter_up.dtype)
            if count:
                late = exchange(payload(FIRST_ROWS, count))
                value = jnp.concatenate([late, value], axis=1)
            return value

        return run

    sizes = (0,) + tuple(size for size in MORE_ROWS if size < rest) + (rest,)
    which = sum((fullest[0] > FIRST_ROWS + size).astype(jnp.int32) for size in sizes[:-1])
    extra = lax.switch(which, [later(size) for size in sizes])
    return combine(base, code, begin, fullest, every, incoming, extra)


def gathered(input_rows, up_weight, adapter_down, adapter_up, slot_row, row_rank):
    shards = lax.axis_size("tensor")
    position = lax.axis_index("tensor")
    total_rows = input_rows.shape[0] * shards
    stored, rank_width, hidden = adapter_up.shape
    width = hidden // shards
    slots = shards * stored
    outgoing = jnp.stack(
        [adapter_up[:, :, i * width : (i + 1) * width] for i in range(shards)], axis=0
    )
    incoming = lax.all_to_all(outgoing, "tensor", split_axis=0, concat_axis=0, tiled=True)
    rows = lax.all_gather(input_rows, "tensor", axis=0, tiled=True)
    shrink = jnp.einsum("gf,ojf->ogj", rows, adapter_down, preferred_element_type=jnp.float32)
    own = position * stored + jnp.arange(stored, dtype=jnp.int32)
    inside = jnp.arange(rank_width, dtype=jnp.int32)[None, :] < row_rank[:, None]
    keep = (slot_row[None, :] == own[:, None])[:, :, None] & inside[None]
    scale = ADAPTER_ALPHA / row_rank.astype(jnp.float32)
    own_coeff = jnp.where(keep, shrink * scale[None, :, None], 0.0).astype(jnp.bfloat16)
    base = jnp.dot(rows, up_weight, preferred_element_type=jnp.float32)
    own_coeff, base = lax.optimization_barrier((own_coeff, base))
    coeff = lax.all_gather(own_coeff, "tensor", axis=0, tiled=True)
    placed = coeff.transpose(1, 0, 2).reshape(total_rows, slots * rank_width)
    factors = incoming.reshape(slots * rank_width, width)
    term = jnp.dot(placed, factors, preferred_element_type=jnp.float32)
    return (base + term).astype(jnp.bfloat16)


def on_device(
    input_rows,
    up_weight,
    adapter_down,
    adapter_up,
    ranks,
    adapter_slot,
    segment_lengths,
    segment_adapter,
):
    shards = lax.axis_size("tensor")
    stored, rank_width, _ = adapter_up.shape
    tiled = up_weight.shape[1] % 128 == 0 and input_rows.shape[0] % 16 == 0 and rank_width == 64
    tiled = tiled and input_rows.shape[1] % 256 == 0 and input_rows.shape[0] * shards <= 256
    if shards == POOLED_SHARDS and stored == 1 and tiled:
        return pooled(
            input_rows,
            up_weight,
            adapter_down,
            adapter_up,
            ranks,
            adapter_slot,
            segment_lengths,
            segment_adapter,
        )
    slot_row, row_rank = row_tables(
        input_rows.shape[0] * shards, ranks, adapter_slot, segment_lengths, segment_adapter
    )
    return gathered(input_rows, up_weight, adapter_down, adapter_up, slot_row, row_rank)


def solution(mesh):
    placed = (
        P(("groups", "tensor"), None),
        P(None, "tensor"),
        P(("groups", "tensor"), None, None),
        P(("groups", "tensor"), None, None),
        P("groups"),
        P("groups"),
        P("groups"),
        P("groups"),
    )
    return jax.shard_map(
        on_device, mesh=mesh, in_specs=placed, out_specs=P("groups", "tensor"), check_vma=False
    )
```

```python
import jax
import jax.numpy as jnp
import numpy as np
from jax import lax
from jax.experimental import pallas as pl
from jax.experimental.pallas import tpu as pltpu
from jax.sharding import PartitionSpec as P

ADAPTER_ALPHA = 32.0
POOLED_SHARDS = 16
FIRST_ROWS = 64
MORE_ROWS = (16, 32)
WIDE_GRANT = 56 << 20


def row_tables(row_count, ranks, adapter_slot, segment_lengths, segment_adapter):
    seg_ends = jnp.cumsum(segment_lengths)
    positions = jnp.arange(row_count, dtype=jnp.int32)
    seg_row = jnp.sum((seg_ends[None, :] <= positions[:, None]).astype(jnp.int32), axis=1)
    seg_pick = (
        seg_row[:, None] == jnp.arange(segment_lengths.shape[0], dtype=jnp.int32)[None, :]
    ).astype(jnp.int32)
    adapter_row = jnp.sum(seg_pick * segment_adapter[None, :], axis=1)
    pool_pick = (
        adapter_row[:, None] == jnp.arange(ranks.shape[0], dtype=jnp.int32)[None, :]
    ).astype(jnp.int32)
    slot_row = jnp.sum(pool_pick * adapter_slot[None, :], axis=1)
    row_rank_values = jnp.sum(pool_pick * ranks[None, :], axis=1)
    return (slot_row, row_rank_values)


def vmem(buffers):
    return pltpu.CompilerParams(vmem_limit_bytes=buffers + (8 << 20))


def split_for_pair(up_factor, down_factor, core, chips):
    rank_width, hidden = up_factor.shape
    width = hidden // (2 * chips)
    features = down_factor.shape[1] // 2

    def kernel(core_ref, source, down, mine, other, half_down, sems):
        core = core_ref[0]
        start = pl.multiple_of((1 - core) * features, features)
        copies = [
            pltpu.make_async_copy(
                down.at[:, pl.ds(start, features)], half_down, sems.at[2 * chips]
            )
        ]
        for q in range(chips):
            for i, (target, half) in enumerate(((other, 1 - core), (mine, core))):
                start = pl.multiple_of((2 * q + half) * width, width)
                copies.append(
                    pltpu.make_async_copy(
                        source.at[:, pl.ds(start, width)], target.at[q], sems.at[2 * q + i]
                    )
                )
        for copy in copies:
            copy.start()
        for copy in copies:
            copy.wait()

    block = jax.ShapeDtypeStruct((chips, rank_width, width), up_factor.dtype)
    return pl.pallas_call(
        kernel,
        in_specs=[pl.BlockSpec(memory_space=pltpu.SMEM)]
        + [pl.BlockSpec(memory_space=pltpu.HBM)] * 2,
        out_specs=[pl.BlockSpec(memory_space=pltpu.VMEM)] * 3,
        out_shape=[
            block, block, jax.ShapeDtypeStruct((rank_width, features), down_factor.dtype)
        ],
        scratch_shapes=[pltpu.SemaphoreType.DMA((2 * chips + 1,))],
        compiler_params=pltpu.CompilerParams(vmem_limit_bytes=WIDE_GRANT),
        cost_estimate=pl.CostEstimate(
            flops=0, bytes_accessed=4 * rank_width * hidden, transcendentals=0
        ),
    )(core, up_factor, down_factor)


def describe(ranks, adapter_slot, segment_lengths, segment_adapter, position, total_rows, limit):
    slots, segments = ranks.shape[0], segment_lengths.shape[0]
    rank_width = limit // 2
    shift = rank_width.bit_length() - 1

    def kernel(
        ranks_in, home_in, length_in, adapter_in, position_ref,
        gain_ref, own_ref, choose_ref, live_ref, fixed_ref, code_ref, begin_ref, full_ref,
        rank_of, rows_of, used, factor, order, ranks_ref, home_ref, length_ref, adapter_ref, sems,
    ):
        pairs = zip(
            (ranks_in, home_in, length_in, adapter_in),
            (ranks_ref, home_ref, length_ref, adapter_ref),
        )
        copies = [
            pltpu.make_async_copy(source, target, sems.at[i])
            for i, (source, target) in enumerate(pairs)
        ]
        for copy in copies:
            copy.start()
        for copy in copies:
            copy.wait()
        for a in range(slots):
            rows_of[a] = 0
            rank_of[home_ref[a]] = ranks_ref[a]
        starts, start = [], jnp.int32(0)
        for i in range(segments):
            slot = home_ref[adapter_ref[i]]
            starts.append((start, start + length_ref[i], slot))
            order[i] = rows_of[slot] - start
            rows_of[slot] = rows_of[slot] + length_ref[i]
            start = start + length_ref[i]
        full = jnp.int32(0)
        for s in range(slots):
            used[s] = jnp.minimum(rows_of[s], rank_of[s])
            factor[s] = (rank_of[s] < rows_of[s]).astype(jnp.int32)
            begin_ref[s] = used[s - 1] if s % 2 else jnp.int32(0)
            if s % 2:
                full = jnp.maximum(full, used[s - 1] + used[s])
        full_ref[0] = full

        def tables(row):
            spot, code = jnp.zeros_like(row), jnp.zeros_like(row)
            for i, (low, high, slot) in enumerate(starts):
                hit = (row >= low) & (row < high)
                spot = jnp.where(hit, row + (order[i] + begin_ref[slot]), spot)
                code = jnp.where(hit, slot + 32 * factor[slot] + 64 * rank_of[slot], code)
            return spot, code & 31, (code >> 5) & 1, code >> 6

        here = position_ref[0]
        spot, slot, by_factor, _ = tables(lax.broadcasted_iota(jnp.int32, (total_rows, limit), 0))
        code_ref[...] = slot + 32 * by_factor + 64 * spot

        lane = lax.broadcasted_iota(jnp.int32, (total_rows // 2, limit), 1)
        row = lax.broadcasted_iota(jnp.int32, (total_rows // 2, limit), 0)
        _, slot, _, rank = tables(row + (lane >> shift) * (total_rows // 2))
        own_ref[...] = jnp.where(slot == here, 1.0, 0.0)
        scale = ADAPTER_ALPHA / rank.astype(jnp.float32)
        inside = ((slot >> 1) == (here >> 1)) & ((lane & (rank_width - 1)) < rank)
        gain_ref[...] = jnp.where(inside, scale, 0.0)

        spot, slot, by_factor, _ = tables(lax.broadcasted_iota(jnp.int32, (8, total_rows), 1))
        mine = ((slot >> 1) == (here >> 1)) & (by_factor == 0)
        spot = jnp.broadcast_to(jnp.where(mine, spot, -1)[:1], (limit, total_rows))
        line = lax.broadcasted_iota(jnp.int32, (limit, total_rows), 0)
        choose_ref[...] = jnp.where(line == spot, 1.0, 0.0).astype(jnp.bfloat16)

        line = lax.broadcasted_iota(jnp.int32, (limit, limit), 0)
        lane = lax.broadcasted_iota(jnp.int32, (limit, limit), 1)
        half, column = lane >> shift, lane & (rank_width - 1)
        other = here ^ 1
        begin = jnp.where(half == 0, begin_ref[here], begin_ref[other])
        many = jnp.where(half == 0, used[here], used[other])
        kind = jnp.where(half == 0, factor[here], factor[other])
        held = (line == begin + column) & (column < many) & (kind == 1)
        fixed_ref[...] = jnp.where(held, 1.0, 0.0).astype(jnp.bfloat16)
        live = (line >= begin) & (line < begin + many) & (kind == 0)
        live_ref[...] = jnp.where(live, 1.0, 0.0)

    smem, whole = pl.BlockSpec(memory_space=pltpu.SMEM), pl.BlockSpec(memory_space=pltpu.VMEM)
    return pl.pallas_call(
        kernel,
        in_specs=[pl.BlockSpec(memory_space=pltpu.HBM)] * 4 + [smem],
        out_specs=[whole] * 6 + [smem] * 2,
        out_shape=[
            jax.ShapeDtypeStruct((total_rows // 2, limit), jnp.float32),
            jax.ShapeDtypeStruct((total_rows // 2, limit), jnp.float32),
            jax.ShapeDtypeStruct((limit, total_rows), jnp.bfloat16),
            jax.ShapeDtypeStruct((limit, limit), jnp.float32),
            jax.ShapeDtypeStruct((limit, limit), jnp.bfloat16),
            jax.ShapeDtypeStruct((total_rows, limit), jnp.int32),
            jax.ShapeDtypeStruct((slots,), jnp.int32),
            jax.ShapeDtypeStruct((1,), jnp.int32),
        ],
        scratch_shapes=[pltpu.SMEM((slots,), jnp.int32)] * 4
        + [pltpu.SMEM((segments,), jnp.int32)]
        + [pltpu.SMEM((slots,), jnp.int32)] * 2
        + [pltpu.SMEM((segments,), jnp.int32)] * 2
        + [pltpu.SemaphoreType.DMA((4,))],
        compiler_params=vmem(16 * total_rows * limit),
        cost_estimate=pl.CostEstimate(
            flops=200 * total_rows * limit, bytes_accessed=16 * total_rows * limit, transcendentals=0
        ),
    )(ranks, adapter_slot, segment_lengths, segment_adapter, position)


def collect_rows(blocks, places, core, own_down, other_down, own):
    count = len(blocks)
    height, features = blocks[0].shape
    height = height // 2
    rank_width = other_down.shape[0]
    half_rows = own.shape[0]
    chunk = 1024 if features % 1024 == 0 else features
    chunks = features // chunk

    def kernel(places_ref, core_ref, own_ref, *refs):
        sources, own_down_ref, other_down_ref = refs[:count], refs[count], refs[count + 1]
        rows_ref, shrink_ref, downs, sems = refs[count + 2 :]
        groups = []
        for k in range(chunks):
            columns = pl.ds(k * chunk, chunk)
            offset = pl.multiple_of(core_ref[0] * features + k * chunk, chunk)
            copies = [
                pltpu.make_async_copy(
                    own_down_ref.at[:, pl.ds(offset, chunk)],
                    downs.at[pl.ds(0, rank_width), columns],
                    sems.at[k, 2 * count],
                ),
                pltpu.make_async_copy(
                    other_down_ref.at[:, columns],
                    downs.at[pl.ds(rank_width, rank_width), columns],
                    sems.at[k, 2 * count + 1],
                ),
            ]
            for i in range(2 * count):
                start = pl.multiple_of(places_ref[i] * height, height)
                copies.append(
                    pltpu.make_async_copy(
                        sources[i // 2].at[pl.ds(i % 2 * height, height), columns],
                        rows_ref.at[pl.ds(start, height), columns],
                        sems.at[k, i],
                    )
                )
            groups.append(copies)
            for copy in copies:
                copy.start()
        shrink = jnp.zeros((2 * half_rows, 2 * rank_width), jnp.float32)
        for k in range(chunks):
            for copy in groups[k]:
                copy.wait()
            columns = pl.ds(k * chunk, chunk)
            shrink = shrink + lax.dot_general(
                rows_ref[:, columns],
                downs[:, columns],
                (((1,), (1,)), ((), ())),
                preferred_element_type=jnp.float32,
            )
        top, bottom = shrink[:half_rows], shrink[half_rows:]
        first = jnp.concatenate([top[:, :rank_width], bottom[:, :rank_width]], axis=1)
        second = jnp.concatenate([top[:, rank_width:], bottom[:, rank_width:]], axis=1)
        shrink_ref[...] = jnp.where(own_ref[...] > 0.5, first, second)

    smem, whole = pl.BlockSpec(memory_space=pltpu.SMEM), pl.BlockSpec(memory_space=pltpu.VMEM)
    rows = 2 * count * height
    return pl.pallas_call(
        kernel,
        in_specs=[smem, smem, whole] + [pl.BlockSpec(memory_space=pl.ANY)] * (count + 2),
        out_specs=[whole] * 2,
        out_shape=[
            jax.ShapeDtypeStruct((rows, features), blocks[0].dtype),
            jax.ShapeDtypeStruct(own.shape, jnp.float32),
        ],
        scratch_shapes=[
            pltpu.VMEM((2 * rank_width, features), own_down.dtype),
            pltpu.SemaphoreType.DMA((chunks, 2 * count + 2)),
        ],
        compiler_params=pltpu.CompilerParams(vmem_limit_bytes=WIDE_GRANT),
        cost_estimate=pl.CostEstimate(
            flops=4 * rows * features * rank_width,
            bytes_accessed=4 * rows * features,
            transcendentals=0,
        ),
    )(places, core, own, *blocks, own_down, other_down)


def build_payload(choose, live, fixed, coeff, mine, other, first, count):
    chips, rank_width, width = mine.shape

    half_rows = coeff.shape[0]

    def kernel(choose_ref, live_ref, fixed_ref, coeff_ref, mine_ref, other_ref, out_ref):
        lines = pl.ds(first, count)
        folded = coeff_ref[...]
        top = jnp.dot(choose_ref[lines, :half_rows], folded, preferred_element_type=jnp.float32)
        low = jnp.dot(choose_ref[lines, half_rows:], folded, preferred_element_type=jnp.float32)
        chosen = top[:, :rank_width] + low[:, rank_width:]
        select = jnp.concatenate([chosen, chosen], axis=1) * live_ref[lines]
        select = (select + fixed_ref[lines].astype(jnp.float32)).astype(jnp.bfloat16)

        @pl.loop(0, chips)
        def _(q):
            out_ref[q] = jnp.dot(
                select,
                jnp.concatenate([mine_ref[q], other_ref[q]], axis=0),
                preferred_element_type=jnp.float32,
            ).astype(out_ref.dtype)

    return pl.pallas_call(
        kernel,
        in_specs=[pl.BlockSpec(memory_space=pltpu.VMEM)] * 6,
        out_specs=pl.BlockSpec(memory_space=pltpu.VMEM),
        out_shape=jax.ShapeDtypeStruct((chips, count, width), mine.dtype),
        compiler_params=vmem(4 * chips * width * (2 * rank_width + count)),
        cost_estimate=pl.CostEstimate(
            flops=4 * chips * count * rank_width * width,
            bytes_accessed=2 * chips * width * (2 * rank_width + count),
            transcendentals=0,
        ),
    )(choose, live, fixed, coeff, mine, other)


def combine(base, code, begin, more, coeff, incoming, extra):
    total_rows, width = base.shape
    chips, first, _ = incoming.shape
    second = extra.shape[1]
    limit = first + second
    rank_width = limit // 2
    shift = rank_width.bit_length() - 1
    tile = 256 if width % 256 == 0 else 128

    def kernel(
        begin_ref, more_ref, base_ref, code_ref, coeff_ref, incoming_ref, extra_ref,
        out_ref, late, base_part, near_rows, sems,
    ):
        fetch = pltpu.make_async_copy(extra_ref, late, sems.at[0])
        get_base = pltpu.make_async_copy(base_ref, base_part, sems.at[1])
        get_near = pltpu.make_async_copy(incoming_ref, near_rows, sems.at[2])
        get_near.start()
        get_base.start()
        folded = coeff_ref[...].astype(jnp.float32)
        both = jnp.concatenate(
            [
                jnp.concatenate([part, part], axis=1)
                for part in (folded[:, :rank_width], folded[:, rank_width:])
            ],
            axis=0,
        )
        code_value = code_ref[...]
        slot, by_factor, spot = code_value & 31, (code_value >> 5) & 1, code_value >> 6
        lane = lax.broadcasted_iota(jnp.int32, (total_rows, limit), 1)
        owned = jnp.where(by_factor == 1, slot, -1) - (lane >> shift)
        finished = jnp.where(by_factor == 0, spot, -1)[:, :1]
        finished_chip = (slot >> 1)[:, :1]

        def weights(low, count):
            target = finished - low
            target = jnp.where((target >= 0) & (target < count), finished_chip * count + target, -1)
            wide = lax.broadcasted_iota(jnp.int32, (total_rows, chips * count), 1)
            total = jnp.where(wide == target, 1.0, 0.0)
            line = lax.broadcasted_iota(jnp.int32, (limit, chips * count), 0)
            place = lax.broadcasted_iota(jnp.int32, (limit, chips * count), 1)
            for q in range(chips):
                goal = jnp.where(
                    line < rank_width, line, line - rank_width + begin_ref[2 * q + 1]
                ) - low
                moved = (goal >= 0) & (goal < count) & (place == q * count + goal)
                moved = jnp.where(moved, 1.0, 0.0).astype(jnp.bfloat16)
                part = jnp.where(owned == 2 * q, both, 0.0).astype(jnp.bfloat16)
                total = total + jnp.dot(part, moved, preferred_element_type=jnp.float32)
            return total.astype(jnp.bfloat16)

        near = weights(0, first)
        get_near.wait()
        get_base.wait()

        def write(far):
            @pl.loop(0, width // tile)
            def _(i):
                columns = pl.ds(pl.multiple_of(i * tile, tile), tile)
                block = near_rows[:, :, columns].reshape(chips * first, tile)
                total = jnp.dot(near, block, preferred_element_type=jnp.float32)
                total += base_part[:, columns]
                if far is not None:
                    block = late[:, :, columns].reshape(chips * second, tile)
                    total += jnp.dot(far, block, preferred_element_type=jnp.float32)
                out_ref[:, columns] = total.astype(out_ref.dtype)

        @pl.when(more_ref[0] > first)
        def _():
            fetch.start()
            far = weights(first, second)
            fetch.wait()
            write(far)

        @pl.when(more_ref[0] <= first)
        def _():
            write(None)

    smem, whole = pl.BlockSpec(memory_space=pltpu.SMEM), pl.BlockSpec(memory_space=pltpu.VMEM)
    return pl.pallas_call(
        kernel,
        in_specs=[smem] * 2
        + [pl.BlockSpec(memory_space=pl.ANY)]
        + [whole] * 2
        + [pl.BlockSpec(memory_space=pl.ANY)] * 2,
        out_specs=whole,
        out_shape=jax.ShapeDtypeStruct((total_rows, width), jnp.bfloat16),
        scratch_shapes=[
            pltpu.VMEM(extra.shape, extra.dtype),
            pltpu.VMEM(base.shape, base.dtype),
            pltpu.VMEM(incoming.shape, incoming.dtype),
            pltpu.SemaphoreType.DMA((3,)),
        ],
        compiler_params=vmem(8 * total_rows * width + 2 * chips * limit * width),
        cost_estimate=pl.CostEstimate(
            flops=4 * total_rows * chips * limit * width,
            bytes_accessed=6 * total_rows * width + 2 * chips * limit * width,
            transcendentals=0,
        ),
    )(begin, more, base, code, coeff, incoming, extra)


def ring_gather(block, shards, halfway):
    chips = shards // 2
    depth = chips // 2
    cycle = list(range(0, chips, 2)) + list(range(chips - 1, 0, -2))
    ahead = [
        (2 * cycle[p] + c, 2 * cycle[(p + 1) % chips] + c) for p in range(chips) for c in range(2)
    ]
    back = [(b, a) for a, b in ahead]
    held = {0: block}
    for step in range(1, depth + 1):
        held[-step] = lax.ppermute(held[1 - step], "tensor", ahead)
        if step < chips - depth:
            held[step] = lax.ppermute(held[step - 1], "tensor", back)
        held[-step] = halfway(step, held[-step])
    table = np.zeros((shards, shards), np.int32)
    for t in range(shards):
        for i, offset in enumerate(held):
            chip = cycle[(cycle.index(t // 2) + offset) % chips]
            table[t, 2 * i], table[t, 2 * i + 1] = 2 * chip + t % 2, 2 * chip + 1 - t % 2
    places = lax.dynamic_index_in_dim(table, lax.axis_index("tensor"), keepdims=False)
    return list(held.values()), places


def largest_over_groups(value):
    groups = lax.axis_size("groups")
    for shift in range(1, groups):
        other = lax.ppermute(value, "groups", [(g, (g + shift) % groups) for g in range(groups)])
        value = jnp.maximum(value, other)
    return value


def pooled(
    input_rows,
    up_weight,
    adapter_down,
    adapter_up,
    ranks,
    adapter_slot,
    segment_lengths,
    segment_adapter,
):
    shards = lax.axis_size("tensor")
    position = lax.axis_index("tensor").astype(jnp.int32)
    chips = shards // 2
    total_rows = input_rows.shape[0] * shards
    rank_width = adapter_up.shape[1]
    limit = 2 * rank_width
    sibling = [(t, t ^ 1) for t in range(shards)]
    same_core = [list(range(c, shards, 2)) for c in range(2)]

    core = position & 1
    features = input_rows.shape[1] // 2

    def swap(value):
        keep = lax.dynamic_slice_in_dim(value, core * features, features, 1)
        send = lax.dynamic_slice_in_dim(value, (1 - core) * features, features, 1)
        return keep, lax.ppermute(send, "tensor", sibling)

    mine, other, down_half = split_for_pair(adapter_up[0], adapter_down[0], core[None], chips)
    block = jnp.concatenate(swap(input_rows), axis=0)
    block, mine, other, down_half = lax.optimization_barrier((block, mine, other, down_half))
    other = lax.ppermute(other, "tensor", sibling)
    down_half = lax.ppermute(down_half, "tensor", sibling)
    gain, own, choose, live, fixed, code, begin, full = describe(
        ranks, adapter_slot, segment_lengths, segment_adapter, position[None], total_rows, limit
    )
    fullest = largest_over_groups(full)
    pending = [(own, choose), (other, down_half)]

    def halfway(step, piece):
        nonlocal pending
        if step <= len(pending):
            piece, pending[step - 1] = lax.optimization_barrier((piece, pending[step - 1]))
        return piece

    blocks, places = ring_gather(block, shards, halfway)
    (own, choose), (other, down_half) = pending
    rows, shrink = collect_rows(blocks, places, core[None], adapter_down[0], down_half, own)
    shrink = shrink + lax.ppermute(shrink, "tensor", sibling)
    coeff = (shrink * gain).astype(jnp.bfloat16)
    coeff, rows, fullest = lax.optimization_barrier((coeff, rows, fullest))

    def payload(low, count):
        return build_payload(choose, live, fixed, coeff, mine, other, low, count)

    def exchange(value):
        return lax.all_to_all(
            value,
            "tensor",
            split_axis=0,
            concat_axis=0,
            axis_index_groups=same_core,
            tiled=True,
        )

    near = payload(0, FIRST_ROWS)
    rows_other = lax.ppermute(rows, "tensor", sibling)
    every, bit = coeff, 2
    while bit < shards:
        every = every + lax.ppermute(every, "tensor", [(t, t ^ bit) for t in range(shards)])
        if bit == 2:
            every, near = lax.optimization_barrier((every, near))
        bit *= 2
    near, every, rows, rows_other = lax.optimization_barrier((near, every, rows, rows_other))
    incoming = exchange(near)
    halves = [jnp.where(core == c, rows, rows_other) for c in range(2)]
    base = jnp.dot(
        jnp.concatenate(halves, axis=1), up_weight, preferred_element_type=jnp.float32
    )
    fullest, base, incoming = lax.optimization_barrier((fullest, base, incoming))
    rest = limit - FIRST_ROWS

    def later(count):
        def run():
            value = jnp.zeros((chips, rest - count, up_weight.shape[1]), adapter_up.dtype)
            if count:
                late = exchange(payload(FIRST_ROWS, count))
                value = jnp.concatenate([late, value], axis=1)
            return value

        return run

    sizes = (0,) + tuple(size for size in MORE_ROWS if size < rest) + (rest,)
    which = sum((fullest[0] > FIRST_ROWS + size).astype(jnp.int32) for size in sizes[:-1])
    extra = lax.switch(which, [later(size) for size in sizes])
    return combine(base, code, begin, fullest, every, incoming, extra)


def gathered(input_rows, up_weight, adapter_down, adapter_up, slot_row, row_rank):
    shards = lax.axis_size("tensor")
    position = lax.axis_index("tensor")
    total_rows = input_rows.shape[0] * shards
    stored, rank_width, hidden = adapter_up.shape
    width = hidden // shards
    slots = shards * stored
    outgoing = jnp.stack(
        [adapter_up[:, :, i * width : (i + 1) * width] for i in range(shards)], axis=0
    )
    incoming = lax.all_to_all(outgoing, "tensor", split_axis=0, concat_axis=0, tiled=True)
    rows = lax.all_gather(input_rows, "tensor", axis=0, tiled=True)
    shrink = jnp.einsum("gf,ojf->ogj", rows, adapter_down, preferred_element_type=jnp.float32)
    own = position * stored + jnp.arange(stored, dtype=jnp.int32)
    inside = jnp.arange(rank_width, dtype=jnp.int32)[None, :] < row_rank[:, None]
    keep = (slot_row[None, :] == own[:, None])[:, :, None] & inside[None]
    scale = ADAPTER_ALPHA / row_rank.astype(jnp.float32)
    own_coeff = jnp.where(keep, shrink * scale[None, :, None], 0.0).astype(jnp.bfloat16)
    base = jnp.dot(rows, up_weight, preferred_element_type=jnp.float32)
    own_coeff, base = lax.optimization_barrier((own_coeff, base))
    coeff = lax.all_gather(own_coeff, "tensor", axis=0, tiled=True)
    placed = coeff.transpose(1, 0, 2).reshape(total_rows, slots * rank_width)
    factors = incoming.reshape(slots * rank_width, width)
    term = jnp.dot(placed, factors, preferred_element_type=jnp.float32)
    return (base + term).astype(jnp.bfloat16)


def on_device(
    input_rows,
    up_weight,
    adapter_down,
    adapter_up,
    ranks,
    adapter_slot,
    segment_lengths,
    segment_adapter,
):
    shards = lax.axis_size("tensor")
    stored, rank_width, _ = adapter_up.shape
    tiled = up_weight.shape[1] % 128 == 0 and input_rows.shape[0] % 16 == 0 and rank_width == 64
    tiled = tiled and input_rows.shape[1] % 256 == 0 and input_rows.shape[0] * shards <= 256
    if shards == POOLED_SHARDS and stored == 1 and tiled:
        return pooled(
            input_rows,
            up_weight,
            adapter_down,
            adapter_up,
            ranks,
            adapter_slot,
            segment_lengths,
            segment_adapter,
        )
    slot_row, row_rank = row_tables(
        input_rows.shape[0] * shards, ranks, adapter_slot, segment_lengths, segment_adapter
    )
    return gathered(input_rows, up_weight, adapter_down, adapter_up, slot_row, row_rank)


def solution(mesh):
    placed = (
        P(("groups", "tensor"), None),
        P(None, "tensor"),
        P(("groups", "tensor"), None, None),
        P(("groups", "tensor"), None, None),
        P("groups"),
        P("groups"),
        P("groups"),
        P("groups"),
    )
    return jax.shard_map(
        on_device, mesh=mesh, in_specs=placed, out_specs=P("groups", "tensor"), check_vma=False
    )
```

```python
import jax
import jax.numpy as jnp
import numpy as np
from jax import lax
from jax.experimental import pallas as pl
from jax.experimental.pallas import tpu as pltpu
from jax.sharding import PartitionSpec as P

ADAPTER_ALPHA = 32.0
POOLED_SHARDS = 16
FIRST_ROWS = 64
MORE_ROWS = (16, 32)
WIDE_GRANT = 56 << 20


def row_tables(row_count, ranks, adapter_slot, segment_lengths, segment_adapter):
    seg_ends = jnp.cumsum(segment_lengths)
    positions = jnp.arange(row_count, dtype=jnp.int32)
    seg_row = jnp.sum((seg_ends[None, :] <= positions[:, None]).astype(jnp.int32), axis=1)
    seg_pick = (
        seg_row[:, None] == jnp.arange(segment_lengths.shape[0], dtype=jnp.int32)[None, :]
    ).astype(jnp.int32)
    adapter_row = jnp.sum(seg_pick * segment_adapter[None, :], axis=1)
    pool_pick = (
        adapter_row[:, None] == jnp.arange(ranks.shape[0], dtype=jnp.int32)[None, :]
    ).astype(jnp.int32)
    slot_row = jnp.sum(pool_pick * adapter_slot[None, :], axis=1)
    row_rank_values = jnp.sum(pool_pick * ranks[None, :], axis=1)
    return (slot_row, row_rank_values)


def vmem(buffers):
    return pltpu.CompilerParams(vmem_limit_bytes=buffers + (8 << 20))


def split_for_pair(up_factor, down_factor, core, chips):
    rank_width, hidden = up_factor.shape
    width = hidden // (2 * chips)
    features = down_factor.shape[1] // 2

    def kernel(core_ref, source, down, mine, other, half_down, sems):
        core = core_ref[0]
        start = pl.multiple_of((1 - core) * features, features)
        copies = [
            pltpu.make_async_copy(
                down.at[:, pl.ds(start, features)], half_down, sems.at[2 * chips]
            )
        ]
        for q in range(chips):
            for i, (target, half) in enumerate(((other, 1 - core), (mine, core))):
                start = pl.multiple_of((2 * q + half) * width, width)
                copies.append(
                    pltpu.make_async_copy(
                        source.at[:, pl.ds(start, width)], target.at[q], sems.at[2 * q + i]
                    )
                )
        for copy in copies:
            copy.start()
        for copy in copies:
            copy.wait()

    block = jax.ShapeDtypeStruct((chips, rank_width, width), up_factor.dtype)
    return pl.pallas_call(
        kernel,
        in_specs=[pl.BlockSpec(memory_space=pltpu.SMEM)]
        + [pl.BlockSpec(memory_space=pltpu.HBM)] * 2,
        out_specs=[pl.BlockSpec(memory_space=pltpu.VMEM)] * 3,
        out_shape=[
            block, block, jax.ShapeDtypeStruct((rank_width, features), down_factor.dtype)
        ],
        scratch_shapes=[pltpu.SemaphoreType.DMA((2 * chips + 1,))],
        compiler_params=pltpu.CompilerParams(vmem_limit_bytes=WIDE_GRANT),
        cost_estimate=pl.CostEstimate(
            flops=0, bytes_accessed=4 * rank_width * hidden, transcendentals=0
        ),
    )(core, up_factor, down_factor)


def describe(ranks, adapter_slot, segment_lengths, segment_adapter, position, total_rows, limit):
    slots, segments = ranks.shape[0], segment_lengths.shape[0]
    rank_width = limit // 2
    shift = rank_width.bit_length() - 1

    def kernel(
        ranks_in, home_in, length_in, adapter_in, position_ref,
        gain_ref, own_ref, choose_ref, live_ref, fixed_ref, code_ref, begin_ref, full_ref,
        rank_of, rows_of, used, factor, order, ranks_ref, home_ref, length_ref, adapter_ref, sems,
    ):
        pairs = zip(
            (ranks_in, home_in, length_in, adapter_in),
            (ranks_ref, home_ref, length_ref, adapter_ref),
        )
        copies = [
            pltpu.make_async_copy(source, target, sems.at[i])
            for i, (source, target) in enumerate(pairs)
        ]
        for copy in copies:
            copy.start()
        for copy in copies:
            copy.wait()
        for a in range(slots):
            rows_of[a] = 0
            rank_of[home_ref[a]] = ranks_ref[a]
        starts, start = [], jnp.int32(0)
        for i in range(segments):
            slot = home_ref[adapter_ref[i]]
            starts.append((start, start + length_ref[i], slot))
            order[i] = rows_of[slot] - start
            rows_of[slot] = rows_of[slot] + length_ref[i]
            start = start + length_ref[i]
        full = jnp.int32(0)
        for s in range(slots):
            used[s] = jnp.minimum(rows_of[s], rank_of[s])
            factor[s] = (rank_of[s] < rows_of[s]).astype(jnp.int32)
            begin_ref[s] = used[s - 1] if s % 2 else jnp.int32(0)
            if s % 2:
                full = jnp.maximum(full, used[s - 1] + used[s])
        full_ref[0] = full

        def tables(row):
            spot, code = jnp.zeros_like(row), jnp.zeros_like(row)
            for i, (low, high, slot) in enumerate(starts):
                hit = (row >= low) & (row < high)
                spot = jnp.where(hit, row + (order[i] + begin_ref[slot]), spot)
                code = jnp.where(hit, slot + 32 * factor[slot] + 64 * rank_of[slot], code)
            return spot, code & 31, (code >> 5) & 1, code >> 6

        here = position_ref[0]
        spot, slot, by_factor, _ = tables(lax.broadcasted_iota(jnp.int32, (total_rows, limit), 0))
        code_ref[...] = slot + 32 * by_factor + 64 * spot

        lane = lax.broadcasted_iota(jnp.int32, (total_rows // 2, limit), 1)
        row = lax.broadcasted_iota(jnp.int32, (total_rows // 2, limit), 0)
        _, slot, _, rank = tables(row + (lane >> shift) * (total_rows // 2))
        own_ref[...] = jnp.where(slot == here, 1.0, 0.0)
        scale = ADAPTER_ALPHA / rank.astype(jnp.float32)
        inside = ((slot >> 1) == (here >> 1)) & ((lane & (rank_width - 1)) < rank)
        gain_ref[...] = jnp.where(inside, scale, 0.0)

        spot, slot, by_factor, _ = tables(lax.broadcasted_iota(jnp.int32, (8, total_rows), 1))
        mine = ((slot >> 1) == (here >> 1)) & (by_factor == 0)
        spot = jnp.broadcast_to(jnp.where(mine, spot, -1)[:1], (limit, total_rows))
        line = lax.broadcasted_iota(jnp.int32, (limit, total_rows), 0)
        choose_ref[...] = jnp.where(line == spot, 1.0, 0.0).astype(jnp.bfloat16)

        line = lax.broadcasted_iota(jnp.int32, (limit, limit), 0)
        lane = lax.broadcasted_iota(jnp.int32, (limit, limit), 1)
        half, column = lane >> shift, lane & (rank_width - 1)
        other = here ^ 1
        begin = jnp.where(half == 0, begin_ref[here], begin_ref[other])
        many = jnp.where(half == 0, used[here], used[other])
        kind = jnp.where(half == 0, factor[here], factor[other])
        held = (line == begin + column) & (column < many) & (kind == 1)
        fixed_ref[...] = jnp.where(held, 1.0, 0.0).astype(jnp.bfloat16)
        live = (line >= begin) & (line < begin + many) & (kind == 0)
        live_ref[...] = jnp.where(live, 1.0, 0.0)

    smem, whole = pl.BlockSpec(memory_space=pltpu.SMEM), pl.BlockSpec(memory_space=pltpu.VMEM)
    return pl.pallas_call(
        kernel,
        in_specs=[pl.BlockSpec(memory_space=pltpu.HBM)] * 4 + [smem],
        out_specs=[whole] * 6 + [smem] * 2,
        out_shape=[
            jax.ShapeDtypeStruct((total_rows // 2, limit), jnp.float32),
            jax.ShapeDtypeStruct((total_rows // 2, limit), jnp.float32),
            jax.ShapeDtypeStruct((limit, total_rows), jnp.bfloat16),
            jax.ShapeDtypeStruct((limit, limit), jnp.float32),
            jax.ShapeDtypeStruct((limit, limit), jnp.bfloat16),
            jax.ShapeDtypeStruct((total_rows, limit), jnp.int32),
            jax.ShapeDtypeStruct((slots,), jnp.int32),
            jax.ShapeDtypeStruct((1,), jnp.int32),
        ],
        scratch_shapes=[pltpu.SMEM((slots,), jnp.int32)] * 4
        + [pltpu.SMEM((segments,), jnp.int32)]
        + [pltpu.SMEM((slots,), jnp.int32)] * 2
        + [pltpu.SMEM((segments,), jnp.int32)] * 2
        + [pltpu.SemaphoreType.DMA((4,))],
        compiler_params=vmem(16 * total_rows * limit),
        cost_estimate=pl.CostEstimate(
            flops=200 * total_rows * limit, bytes_accessed=16 * total_rows * limit, transcendentals=0
        ),
    )(ranks, adapter_slot, segment_lengths, segment_adapter, position)


def collect_rows(blocks, places, core, own_down, other_down, own):
    count = len(blocks)
    height, features = blocks[0].shape
    height = height // 2
    rank_width = other_down.shape[0]
    half_rows = own.shape[0]
    chunk = 1024 if features % 1024 == 0 else features
    chunks = features // chunk

    def kernel(places_ref, core_ref, own_ref, *refs):
        sources, own_down_ref, other_down_ref = refs[:count], refs[count], refs[count + 1]
        rows_ref, shrink_ref, downs, sems = refs[count + 2 :]
        groups = []
        for k in range(chunks):
            columns = pl.ds(k * chunk, chunk)
            offset = pl.multiple_of(core_ref[0] * features + k * chunk, chunk)
            copies = [
                pltpu.make_async_copy(
                    own_down_ref.at[:, pl.ds(offset, chunk)],
                    downs.at[pl.ds(0, rank_width), columns],
                    sems.at[k, 2 * count],
                ),
                pltpu.make_async_copy(
                    other_down_ref.at[:, columns],
                    downs.at[pl.ds(rank_width, rank_width), columns],
                    sems.at[k, 2 * count + 1],
                ),
            ]
            for i in range(2 * count):
                start = pl.multiple_of(places_ref[i] * height, height)
                copies.append(
                    pltpu.make_async_copy(
                        sources[i // 2].at[pl.ds(i % 2 * height, height), columns],
                        rows_ref.at[pl.ds(start, height), columns],
                        sems.at[k, i],
                    )
                )
            groups.append(copies)
            for copy in copies:
                copy.start()
        shrink = jnp.zeros((2 * half_rows, 2 * rank_width), jnp.float32)
        for k in range(chunks):
            for copy in groups[k]:
                copy.wait()
            columns = pl.ds(k * chunk, chunk)
            shrink = shrink + lax.dot_general(
                rows_ref[:, columns],
                downs[:, columns],
                (((1,), (1,)), ((), ())),
                preferred_element_type=jnp.float32,
            )
        top, bottom = shrink[:half_rows], shrink[half_rows:]
        first = jnp.concatenate([top[:, :rank_width], bottom[:, :rank_width]], axis=1)
        second = jnp.concatenate([top[:, rank_width:], bottom[:, rank_width:]], axis=1)
        shrink_ref[...] = jnp.where(own_ref[...] > 0.5, first, second)

    smem, whole = pl.BlockSpec(memory_space=pltpu.SMEM), pl.BlockSpec(memory_space=pltpu.VMEM)
    rows = 2 * count * height
    return pl.pallas_call(
        kernel,
        in_specs=[smem, smem, whole] + [pl.BlockSpec(memory_space=pl.ANY)] * (count + 2),
        out_specs=[whole] * 2,
        out_shape=[
            jax.ShapeDtypeStruct((rows, features), blocks[0].dtype),
            jax.ShapeDtypeStruct(own.shape, jnp.float32),
        ],
        scratch_shapes=[
            pltpu.VMEM((2 * rank_width, features), own_down.dtype),
            pltpu.SemaphoreType.DMA((chunks, 2 * count + 2)),
        ],
        compiler_params=pltpu.CompilerParams(vmem_limit_bytes=WIDE_GRANT),
        cost_estimate=pl.CostEstimate(
            flops=4 * rows * features * rank_width,
            bytes_accessed=4 * rows * features,
            transcendentals=0,
        ),
    )(places, core, own, *blocks, own_down, other_down)


def build_payload(choose, live, fixed, coeff, mine, other, first, count):
    chips, rank_width, width = mine.shape

    half_rows = coeff.shape[0]

    def kernel(choose_ref, live_ref, fixed_ref, coeff_ref, mine_ref, other_ref, out_ref):
        lines = pl.ds(first, count)
        folded = coeff_ref[...]
        top = jnp.dot(choose_ref[lines, :half_rows], folded, preferred_element_type=jnp.float32)
        low = jnp.dot(choose_ref[lines, half_rows:], folded, preferred_element_type=jnp.float32)
        chosen = top[:, :rank_width] + low[:, rank_width:]
        select = jnp.concatenate([chosen, chosen], axis=1) * live_ref[lines]
        select = (select + fixed_ref[lines].astype(jnp.float32)).astype(jnp.bfloat16)

        @pl.loop(0, chips)
        def _(q):
            out_ref[q] = jnp.dot(
                select,
                jnp.concatenate([mine_ref[q], other_ref[q]], axis=0),
                preferred_element_type=jnp.float32,
            ).astype(out_ref.dtype)

    return pl.pallas_call(
        kernel,
        in_specs=[pl.BlockSpec(memory_space=pltpu.VMEM)] * 6,
        out_specs=pl.BlockSpec(memory_space=pltpu.VMEM),
        out_shape=jax.ShapeDtypeStruct((chips, count, width), mine.dtype),
        compiler_params=vmem(4 * chips * width * (2 * rank_width + count)),
        cost_estimate=pl.CostEstimate(
            flops=4 * chips * count * rank_width * width,
            bytes_accessed=2 * chips * width * (2 * rank_width + count),
            transcendentals=0,
        ),
    )(choose, live, fixed, coeff, mine, other)


def combine(base, code, begin, more, coeff, incoming, extra):
    total_rows, width = base.shape
    chips, first, _ = incoming.shape
    second = extra.shape[1]
    limit = first + second
    rank_width = limit // 2
    shift = rank_width.bit_length() - 1
    tile = 256 if width % 256 == 0 else 128

    def kernel(
        begin_ref, more_ref, base_ref, code_ref, coeff_ref, incoming_ref, extra_ref,
        out_ref, late, base_part, near_rows, sems,
    ):
        fetch = pltpu.make_async_copy(extra_ref, late, sems.at[0])
        get_base = pltpu.make_async_copy(base_ref, base_part, sems.at[1])
        get_near = pltpu.make_async_copy(incoming_ref, near_rows, sems.at[2])
        get_near.start()
        get_base.start()
        folded = coeff_ref[...].astype(jnp.float32)
        both = jnp.concatenate(
            [
                jnp.concatenate([part, part], axis=1)
                for part in (folded[:, :rank_width], folded[:, rank_width:])
            ],
            axis=0,
        )
        code_value = code_ref[...]
        slot, by_factor, spot = code_value & 31, (code_value >> 5) & 1, code_value >> 6
        lane = lax.broadcasted_iota(jnp.int32, (total_rows, limit), 1)
        owned = jnp.where(by_factor == 1, slot, -1) - (lane >> shift)
        finished = jnp.where(by_factor == 0, spot, -1)[:, :1]
        finished_chip = (slot >> 1)[:, :1]

        def weights(low, count):
            target = finished - low
            target = jnp.where((target >= 0) & (target < count), finished_chip * count + target, -1)
            wide = lax.broadcasted_iota(jnp.int32, (total_rows, chips * count), 1)
            total = jnp.where(wide == target, 1.0, 0.0)
            line = lax.broadcasted_iota(jnp.int32, (limit, chips * count), 0)
            place = lax.broadcasted_iota(jnp.int32, (limit, chips * count), 1)
            for q in range(chips):
                goal = jnp.where(
                    line < rank_width, line, line - rank_width + begin_ref[2 * q + 1]
                ) - low
                moved = (goal >= 0) & (goal < count) & (place == q * count + goal)
                moved = jnp.where(moved, 1.0, 0.0).astype(jnp.bfloat16)
                part = jnp.where(owned == 2 * q, both, 0.0).astype(jnp.bfloat16)
                total = total + jnp.dot(part, moved, preferred_element_type=jnp.float32)
            return total.astype(jnp.bfloat16)

        near = weights(0, first)
        get_near.wait()
        get_base.wait()

        def write(far):
            @pl.loop(0, width // tile)
            def _(i):
                columns = pl.ds(pl.multiple_of(i * tile, tile), tile)
                block = near_rows[:, :, columns].reshape(chips * first, tile)
                total = jnp.dot(near, block, preferred_element_type=jnp.float32)
                total += base_part[:, columns]
                if far is not None:
                    block = late[:, :, columns].reshape(chips * second, tile)
                    total += jnp.dot(far, block, preferred_element_type=jnp.float32)
                out_ref[:, columns] = total.astype(out_ref.dtype)

        @pl.when(more_ref[0] > first)
        def _():
            fetch.start()
            far = weights(first, second)
            fetch.wait()
            write(far)

        @pl.when(more_ref[0] <= first)
        def _():
            write(None)

    smem, whole = pl.BlockSpec(memory_space=pltpu.SMEM), pl.BlockSpec(memory_space=pltpu.VMEM)
    return pl.pallas_call(
        kernel,
        in_specs=[smem] * 2
        + [pl.BlockSpec(memory_space=pl.ANY)]
        + [whole] * 2
        + [pl.BlockSpec(memory_space=pl.ANY)] * 2,
        out_specs=whole,
        out_shape=jax.ShapeDtypeStruct((total_rows, width), jnp.bfloat16),
        scratch_shapes=[
            pltpu.VMEM(extra.shape, extra.dtype),
            pltpu.VMEM(base.shape, base.dtype),
            pltpu.VMEM(incoming.shape, incoming.dtype),
            pltpu.SemaphoreType.DMA((3,)),
        ],
        compiler_params=pltpu.CompilerParams(vmem_limit_bytes=WIDE_GRANT),
        cost_estimate=pl.CostEstimate(
            flops=4 * total_rows * chips * limit * width,
            bytes_accessed=6 * total_rows * width + 2 * chips * limit * width,
            transcendentals=0,
        ),
    )(begin, more, base, code, coeff, incoming, extra)


def ring_gather(block, shards, halfway):
    chips = shards // 2
    depth = chips // 2
    cycle = list(range(0, chips, 2)) + list(range(chips - 1, 0, -2))
    ahead = [
        (2 * cycle[p] + c, 2 * cycle[(p + 1) % chips] + c) for p in range(chips) for c in range(2)
    ]
    back = [(b, a) for a, b in ahead]
    held = {0: block}
    for step in range(1, depth + 1):
        held[-step] = lax.ppermute(held[1 - step], "tensor", ahead)
        if step < chips - depth:
            held[step] = lax.ppermute(held[step - 1], "tensor", back)
        held[-step] = halfway(step, held[-step])
    table = np.zeros((shards, shards), np.int32)
    for t in range(shards):
        for i, offset in enumerate(held):
            chip = cycle[(cycle.index(t // 2) + offset) % chips]
            table[t, 2 * i], table[t, 2 * i + 1] = 2 * chip + t % 2, 2 * chip + 1 - t % 2
    places = lax.dynamic_index_in_dim(table, lax.axis_index("tensor"), keepdims=False)
    return list(held.values()), places


def largest_over_groups(value):
    groups = lax.axis_size("groups")
    for shift in range(1, groups):
        other = lax.ppermute(value, "groups", [(g, (g + shift) % groups) for g in range(groups)])
        value = jnp.maximum(value, other)
    return value


def pooled(
    input_rows,
    up_weight,
    adapter_down,
    adapter_up,
    ranks,
    adapter_slot,
    segment_lengths,
    segment_adapter,
):
    shards = lax.axis_size("tensor")
    position = lax.axis_index("tensor").astype(jnp.int32)
    chips = shards // 2
    total_rows = input_rows.shape[0] * shards
    rank_width = adapter_up.shape[1]
    limit = 2 * rank_width
    sibling = [(t, t ^ 1) for t in range(shards)]
    same_core = [list(range(c, shards, 2)) for c in range(2)]

    core = position & 1
    features = input_rows.shape[1] // 2

    def swap(value):
        keep = lax.dynamic_slice_in_dim(value, core * features, features, 1)
        send = lax.dynamic_slice_in_dim(value, (1 - core) * features, features, 1)
        return keep, lax.ppermute(send, "tensor", sibling)

    mine, other, down_half = split_for_pair(adapter_up[0], adapter_down[0], core[None], chips)
    block = jnp.concatenate(swap(input_rows), axis=0)
    block, mine, other, down_half = lax.optimization_barrier((block, mine, other, down_half))
    other = lax.ppermute(other, "tensor", sibling)
    down_half = lax.ppermute(down_half, "tensor", sibling)
    gain, own, choose, live, fixed, code, begin, full = describe(
        ranks, adapter_slot, segment_lengths, segment_adapter, position[None], total_rows, limit
    )
    fullest = largest_over_groups(full)
    pending = [(own, choose), (other, down_half)]

    def halfway(step, piece):
        nonlocal pending
        if step <= len(pending):
            piece, pending[step - 1] = lax.optimization_barrier((piece, pending[step - 1]))
        return piece

    blocks, places = ring_gather(block, shards, halfway)
    (own, choose), (other, down_half) = pending
    rows, shrink = collect_rows(blocks, places, core[None], adapter_down[0], down_half, own)
    shrink = shrink + lax.ppermute(shrink, "tensor", sibling)
    coeff = (shrink * gain).astype(jnp.bfloat16)
    coeff, rows, fullest = lax.optimization_barrier((coeff, rows, fullest))

    def payload(low, count):
        return build_payload(choose, live, fixed, coeff, mine, other, low, count)

    def exchange(value):
        return lax.all_to_all(
            value,
            "tensor",
            split_axis=0,
            concat_axis=0,
            axis_index_groups=same_core,
            tiled=True,
        )

    near = payload(0, FIRST_ROWS)
    rows_other = lax.ppermute(rows, "tensor", sibling)
    every, bit = coeff, 2
    while bit < shards:
        every = every + lax.ppermute(every, "tensor", [(t, t ^ bit) for t in range(shards)])
        if bit == 2:
            every, near = lax.optimization_barrier((every, near))
        bit *= 2
    near, every, rows, rows_other = lax.optimization_barrier((near, every, rows, rows_other))
    incoming = exchange(near)
    halves = [jnp.where(core == c, rows, rows_other) for c in range(2)]
    base = jnp.dot(
        jnp.concatenate(halves, axis=1), up_weight, preferred_element_type=jnp.float32
    )
    choose, base = lax.optimization_barrier((choose, base))
    rest = limit - FIRST_ROWS
    far = payload(FIRST_ROWS, rest)
    fullest, base, incoming, far = lax.optimization_barrier((fullest, base, incoming, far))

    def later(count):
        def run():
            value = jnp.zeros((chips, rest - count, up_weight.shape[1]), adapter_up.dtype)
            if count:
                late = exchange(far[:, :count])
                value = jnp.concatenate([late, value], axis=1)
            return value

        return run

    sizes = (0,) + tuple(size for size in MORE_ROWS if size < rest) + (rest,)
    which = sum((fullest[0] > FIRST_ROWS + size).astype(jnp.int32) for size in sizes[:-1])
    extra = lax.switch(which, [later(size) for size in sizes])
    return combine(base, code, begin, fullest, every, incoming, extra)


def gathered(input_rows, up_weight, adapter_down, adapter_up, slot_row, row_rank):
    shards = lax.axis_size("tensor")
    position = lax.axis_index("tensor")
    total_rows = input_rows.shape[0] * shards
    stored, rank_width, hidden = adapter_up.shape
    width = hidden // shards
    slots = shards * stored
    outgoing = jnp.stack(
        [adapter_up[:, :, i * width : (i + 1) * width] for i in range(shards)], axis=0
    )
    incoming = lax.all_to_all(outgoing, "tensor", split_axis=0, concat_axis=0, tiled=True)
    rows = lax.all_gather(input_rows, "tensor", axis=0, tiled=True)
    shrink = jnp.einsum("gf,ojf->ogj", rows, adapter_down, preferred_element_type=jnp.float32)
    own = position * stored + jnp.arange(stored, dtype=jnp.int32)
    inside = jnp.arange(rank_width, dtype=jnp.int32)[None, :] < row_rank[:, None]
    keep = (slot_row[None, :] == own[:, None])[:, :, None] & inside[None]
    scale = ADAPTER_ALPHA / row_rank.astype(jnp.float32)
    own_coeff = jnp.where(keep, shrink * scale[None, :, None], 0.0).astype(jnp.bfloat16)
    base = jnp.dot(rows, up_weight, preferred_element_type=jnp.float32)
    own_coeff, base = lax.optimization_barrier((own_coeff, base))
    coeff = lax.all_gather(own_coeff, "tensor", axis=0, tiled=True)
    placed = coeff.transpose(1, 0, 2).reshape(total_rows, slots * rank_width)
    factors = incoming.reshape(slots * rank_width, width)
    term = jnp.dot(placed, factors, preferred_element_type=jnp.float32)
    return (base + term).astype(jnp.bfloat16)


def on_device(
    input_rows,
    up_weight,
    adapter_down,
    adapter_up,
    ranks,
    adapter_slot,
    segment_lengths,
    segment_adapter,
):
    shards = lax.axis_size("tensor")
    stored, rank_width, _ = adapter_up.shape
    tiled = up_weight.shape[1] % 128 == 0 and input_rows.shape[0] % 16 == 0 and rank_width == 64
    tiled = tiled and input_rows.shape[1] % 256 == 0 and input_rows.shape[0] * shards <= 256
    if shards == POOLED_SHARDS and stored == 1 and tiled:
        return pooled(
            input_rows,
            up_weight,
            adapter_down,
            adapter_up,
            ranks,
            adapter_slot,
            segment_lengths,
            segment_adapter,
        )
    slot_row, row_rank = row_tables(
        input_rows.shape[0] * shards, ranks, adapter_slot, segment_lengths, segment_adapter
    )
    return gathered(input_rows, up_weight, adapter_down, adapter_up, slot_row, row_rank)


def solution(mesh):
    placed = (
        P(("groups", "tensor"), None),
        P(None, "tensor"),
        P(("groups", "tensor"), None, None),
        P(("groups", "tensor"), None, None),
        P("groups"),
        P("groups"),
        P("groups"),
        P("groups"),
    )
    return jax.shard_map(
        on_device, mesh=mesh, in_specs=placed, out_specs=P("groups", "tensor"), check_vma=False
    )
```

```python
import jax
import jax.numpy as jnp
import numpy as np
from jax import lax
from jax.experimental import pallas as pl
from jax.experimental.pallas import tpu as pltpu
from jax.sharding import PartitionSpec as P

ADAPTER_ALPHA = 32.0
POOLED_SHARDS = 16
FIRST_ROWS = 64
MORE_ROWS = (16, 32)
WIDE_GRANT = 56 << 20


def row_tables(row_count, ranks, adapter_slot, segment_lengths, segment_adapter):
    seg_ends = jnp.cumsum(segment_lengths)
    positions = jnp.arange(row_count, dtype=jnp.int32)
    seg_row = jnp.sum((seg_ends[None, :] <= positions[:, None]).astype(jnp.int32), axis=1)
    seg_pick = (
        seg_row[:, None] == jnp.arange(segment_lengths.shape[0], dtype=jnp.int32)[None, :]
    ).astype(jnp.int32)
    adapter_row = jnp.sum(seg_pick * segment_adapter[None, :], axis=1)
    pool_pick = (
        adapter_row[:, None] == jnp.arange(ranks.shape[0], dtype=jnp.int32)[None, :]
    ).astype(jnp.int32)
    slot_row = jnp.sum(pool_pick * adapter_slot[None, :], axis=1)
    row_rank_values = jnp.sum(pool_pick * ranks[None, :], axis=1)
    return (slot_row, row_rank_values)


def vmem(buffers):
    return pltpu.CompilerParams(vmem_limit_bytes=buffers + (8 << 20))


def split_for_pair(up_factor, down_factor, core, chips):
    rank_width, hidden = up_factor.shape
    width = hidden // (2 * chips)
    features = down_factor.shape[1] // 2

    def kernel(core_ref, source, down, mine, other, half_down, sems):
        core = core_ref[0]
        start = pl.multiple_of((1 - core) * features, features)
        copies = [
            pltpu.make_async_copy(
                down.at[:, pl.ds(start, features)], half_down, sems.at[2 * chips]
            )
        ]
        for q in range(chips):
            for i, (target, half) in enumerate(((other, 1 - core), (mine, core))):
                start = pl.multiple_of((2 * q + half) * width, width)
                copies.append(
                    pltpu.make_async_copy(
                        source.at[:, pl.ds(start, width)], target.at[q], sems.at[2 * q + i]
                    )
                )
        for copy in copies:
            copy.start()
        for copy in copies:
            copy.wait()

    block = jax.ShapeDtypeStruct((chips, rank_width, width), up_factor.dtype)
    return pl.pallas_call(
        kernel,
        in_specs=[pl.BlockSpec(memory_space=pltpu.SMEM)]
        + [pl.BlockSpec(memory_space=pltpu.HBM)] * 2,
        out_specs=[pl.BlockSpec(memory_space=pltpu.VMEM)] * 3,
        out_shape=[
            block, block, jax.ShapeDtypeStruct((rank_width, features), down_factor.dtype)
        ],
        scratch_shapes=[pltpu.SemaphoreType.DMA((2 * chips + 1,))],
        compiler_params=pltpu.CompilerParams(vmem_limit_bytes=WIDE_GRANT),
        cost_estimate=pl.CostEstimate(
            flops=0, bytes_accessed=4 * rank_width * hidden, transcendentals=0
        ),
    )(core, up_factor, down_factor)


def describe(ranks, adapter_slot, segment_lengths, segment_adapter, position, total_rows, limit):
    slots, segments = ranks.shape[0], segment_lengths.shape[0]
    rank_width = limit // 2
    shift = rank_width.bit_length() - 1

    def kernel(
        ranks_in, home_in, length_in, adapter_in, position_ref,
        gain_ref, own_ref, choose_ref, live_ref, fixed_ref, code_ref, begin_ref, full_ref,
        rank_of, rows_of, used, factor, order, ranks_ref, home_ref, length_ref, adapter_ref, sems,
    ):
        pairs = zip(
            (ranks_in, home_in, length_in, adapter_in),
            (ranks_ref, home_ref, length_ref, adapter_ref),
        )
        copies = [
            pltpu.make_async_copy(source, target, sems.at[i])
            for i, (source, target) in enumerate(pairs)
        ]
        for copy in copies:
            copy.start()
        for copy in copies:
            copy.wait()
        for a in range(slots):
            rows_of[a] = 0
            rank_of[home_ref[a]] = ranks_ref[a]
        starts, start = [], jnp.int32(0)
        for i in range(segments):
            slot = home_ref[adapter_ref[i]]
            starts.append((start, start + length_ref[i], slot))
            order[i] = rows_of[slot] - start
            rows_of[slot] = rows_of[slot] + length_ref[i]
            start = start + length_ref[i]
        full = jnp.int32(0)
        for s in range(slots):
            used[s] = jnp.minimum(rows_of[s], rank_of[s])
            factor[s] = (rank_of[s] < rows_of[s]).astype(jnp.int32)
            begin_ref[s] = used[s - 1] if s % 2 else jnp.int32(0)
            if s % 2:
                full = jnp.maximum(full, used[s - 1] + used[s])
        full_ref[0] = full

        def tables(row):
            spot, code = jnp.zeros_like(row), jnp.zeros_like(row)
            for i, (low, high, slot) in enumerate(starts):
                hit = (row >= low) & (row < high)
                spot = jnp.where(hit, row + (order[i] + begin_ref[slot]), spot)
                code = jnp.where(hit, slot + 32 * factor[slot] + 64 * rank_of[slot], code)
            return spot, code & 31, (code >> 5) & 1, code >> 6

        here = position_ref[0]
        spot, slot, by_factor, _ = tables(lax.broadcasted_iota(jnp.int32, (total_rows, limit), 0))
        code_ref[...] = slot + 32 * by_factor + 64 * spot

        lane = lax.broadcasted_iota(jnp.int32, (total_rows // 2, limit), 1)
        row = lax.broadcasted_iota(jnp.int32, (total_rows // 2, limit), 0)
        _, slot, _, rank = tables(row + (lane >> shift) * (total_rows // 2))
        own_ref[...] = jnp.where(slot == here, 1.0, 0.0)
        scale = ADAPTER_ALPHA / rank.astype(jnp.float32)
        inside = ((slot >> 1) == (here >> 1)) & ((lane & (rank_width - 1)) < rank)
        gain_ref[...] = jnp.where(inside, scale, 0.0)

        spot, slot, by_factor, _ = tables(lax.broadcasted_iota(jnp.int32, (8, total_rows), 1))
        mine = ((slot >> 1) == (here >> 1)) & (by_factor == 0)
        spot = jnp.broadcast_to(jnp.where(mine, spot, -1)[:1], (limit, total_rows))
        line = lax.broadcasted_iota(jnp.int32, (limit, total_rows), 0)
        choose_ref[...] = jnp.where(line == spot, 1.0, 0.0).astype(jnp.bfloat16)

        line = lax.broadcasted_iota(jnp.int32, (limit, limit), 0)
        lane = lax.broadcasted_iota(jnp.int32, (limit, limit), 1)
        half, column = lane >> shift, lane & (rank_width - 1)
        other = here ^ 1
        begin = jnp.where(half == 0, begin_ref[here], begin_ref[other])
        many = jnp.where(half == 0, used[here], used[other])
        kind = jnp.where(half == 0, factor[here], factor[other])
        held = (line == begin + column) & (column < many) & (kind == 1)
        fixed_ref[...] = jnp.where(held, 1.0, 0.0).astype(jnp.bfloat16)
        live = (line >= begin) & (line < begin + many) & (kind == 0)
        live_ref[...] = jnp.where(live, 1.0, 0.0)

    smem, whole = pl.BlockSpec(memory_space=pltpu.SMEM), pl.BlockSpec(memory_space=pltpu.VMEM)
    return pl.pallas_call(
        kernel,
        in_specs=[pl.BlockSpec(memory_space=pltpu.HBM)] * 4 + [smem],
        out_specs=[whole] * 6 + [smem] * 2,
        out_shape=[
            jax.ShapeDtypeStruct((total_rows // 2, limit), jnp.float32),
            jax.ShapeDtypeStruct((total_rows // 2, limit), jnp.float32),
            jax.ShapeDtypeStruct((limit, total_rows), jnp.bfloat16),
            jax.ShapeDtypeStruct((limit, limit), jnp.float32),
            jax.ShapeDtypeStruct((limit, limit), jnp.bfloat16),
            jax.ShapeDtypeStruct((total_rows, limit), jnp.int32),
            jax.ShapeDtypeStruct((slots,), jnp.int32),
            jax.ShapeDtypeStruct((1,), jnp.int32),
        ],
        scratch_shapes=[pltpu.SMEM((slots,), jnp.int32)] * 4
        + [pltpu.SMEM((segments,), jnp.int32)]
        + [pltpu.SMEM((slots,), jnp.int32)] * 2
        + [pltpu.SMEM((segments,), jnp.int32)] * 2
        + [pltpu.SemaphoreType.DMA((4,))],
        compiler_params=vmem(16 * total_rows * limit),
        cost_estimate=pl.CostEstimate(
            flops=200 * total_rows * limit, bytes_accessed=16 * total_rows * limit, transcendentals=0
        ),
    )(ranks, adapter_slot, segment_lengths, segment_adapter, position)


def collect_rows(blocks, places, core, own_down, other_down, own):
    count = len(blocks)
    height, features = blocks[0].shape
    height = height // 2
    rank_width = other_down.shape[0]
    half_rows = own.shape[0]
    chunk = 1024 if features % 1024 == 0 else features
    chunks = features // chunk

    def kernel(places_ref, core_ref, own_ref, *refs):
        sources, own_down_ref, other_down_ref = refs[:count], refs[count], refs[count + 1]
        rows_ref, shrink_ref, downs, sems = refs[count + 2 :]
        groups = []
        for k in range(chunks):
            columns = pl.ds(k * chunk, chunk)
            offset = pl.multiple_of(core_ref[0] * features + k * chunk, chunk)
            copies = [
                pltpu.make_async_copy(
                    own_down_ref.at[:, pl.ds(offset, chunk)],
                    downs.at[pl.ds(0, rank_width), columns],
                    sems.at[k, 2 * count],
                ),
                pltpu.make_async_copy(
                    other_down_ref.at[:, columns],
                    downs.at[pl.ds(rank_width, rank_width), columns],
                    sems.at[k, 2 * count + 1],
                ),
            ]
            for i in range(2 * count):
                start = pl.multiple_of(places_ref[i] * height, height)
                copies.append(
                    pltpu.make_async_copy(
                        sources[i // 2].at[pl.ds(i % 2 * height, height), columns],
                        rows_ref.at[pl.ds(start, height), columns],
                        sems.at[k, i],
                    )
                )
            groups.append(copies)
            for copy in copies:
                copy.start()
        shrink = jnp.zeros((2 * half_rows, 2 * rank_width), jnp.float32)
        for k in range(chunks):
            for copy in groups[k]:
                copy.wait()
            columns = pl.ds(k * chunk, chunk)
            shrink = shrink + lax.dot_general(
                rows_ref[:, columns],
                downs[:, columns],
                (((1,), (1,)), ((), ())),
                preferred_element_type=jnp.float32,
            )
        top, bottom = shrink[:half_rows], shrink[half_rows:]
        first = jnp.concatenate([top[:, :rank_width], bottom[:, :rank_width]], axis=1)
        second = jnp.concatenate([top[:, rank_width:], bottom[:, rank_width:]], axis=1)
        shrink_ref[...] = jnp.where(own_ref[...] > 0.5, first, second)

    smem, whole = pl.BlockSpec(memory_space=pltpu.SMEM), pl.BlockSpec(memory_space=pltpu.VMEM)
    rows = 2 * count * height
    return pl.pallas_call(
        kernel,
        in_specs=[smem, smem, whole] + [pl.BlockSpec(memory_space=pl.ANY)] * (count + 2),
        out_specs=[whole] * 2,
        out_shape=[
            jax.ShapeDtypeStruct((rows, features), blocks[0].dtype),
            jax.ShapeDtypeStruct(own.shape, jnp.float32),
        ],
        scratch_shapes=[
            pltpu.VMEM((2 * rank_width, features), own_down.dtype),
            pltpu.SemaphoreType.DMA((chunks, 2 * count + 2)),
        ],
        compiler_params=pltpu.CompilerParams(vmem_limit_bytes=WIDE_GRANT),
        cost_estimate=pl.CostEstimate(
            flops=4 * rows * features * rank_width,
            bytes_accessed=4 * rows * features,
            transcendentals=0,
        ),
    )(places, core, own, *blocks, own_down, other_down)


def build_payload(choose, live, fixed, coeff, mine, other, first, count):
    chips, rank_width, width = mine.shape

    half_rows = coeff.shape[0]

    def kernel(choose_ref, live_ref, fixed_ref, coeff_ref, mine_ref, other_ref, out_ref):
        lines = pl.ds(first, count)
        folded = coeff_ref[...]
        top = jnp.dot(choose_ref[lines, :half_rows], folded, preferred_element_type=jnp.float32)
        low = jnp.dot(choose_ref[lines, half_rows:], folded, preferred_element_type=jnp.float32)
        chosen = top[:, :rank_width] + low[:, rank_width:]
        select = jnp.concatenate([chosen, chosen], axis=1) * live_ref[lines]
        select = (select + fixed_ref[lines].astype(jnp.float32)).astype(jnp.bfloat16)

        @pl.loop(0, chips)
        def _(q):
            out_ref[q] = jnp.dot(
                select,
                jnp.concatenate([mine_ref[q], other_ref[q]], axis=0),
                preferred_element_type=jnp.float32,
            ).astype(out_ref.dtype)

    return pl.pallas_call(
        kernel,
        in_specs=[pl.BlockSpec(memory_space=pltpu.VMEM)] * 6,
        out_specs=pl.BlockSpec(memory_space=pltpu.VMEM),
        out_shape=jax.ShapeDtypeStruct((chips, count, width), mine.dtype),
        compiler_params=vmem(4 * chips * width * (2 * rank_width + count)),
        cost_estimate=pl.CostEstimate(
            flops=4 * chips * count * rank_width * width,
            bytes_accessed=2 * chips * width * (2 * rank_width + count),
            transcendentals=0,
        ),
    )(choose, live, fixed, coeff, mine, other)


def combine(base, code, begin, more, coeff, incoming, extra):
    total_rows, width = base.shape
    chips, first, _ = incoming.shape
    second = extra.shape[1]
    limit = first + second
    rank_width = limit // 2
    shift = rank_width.bit_length() - 1
    tile = 256 if width % 256 == 0 else 128

    def kernel(
        begin_ref, more_ref, base_ref, code_ref, coeff_ref, incoming_ref, extra_ref,
        out_ref, late, base_part, near_rows, sems,
    ):
        fetch = pltpu.make_async_copy(extra_ref, late, sems.at[0])
        get_base = pltpu.make_async_copy(base_ref, base_part, sems.at[1])
        get_near = pltpu.make_async_copy(incoming_ref, near_rows, sems.at[2])
        get_near.start()
        get_base.start()
        folded = coeff_ref[...].astype(jnp.float32)
        both = jnp.concatenate(
            [
                jnp.concatenate([part, part], axis=1)
                for part in (folded[:, :rank_width], folded[:, rank_width:])
            ],
            axis=0,
        )
        code_value = code_ref[...]
        slot, by_factor, spot = code_value & 31, (code_value >> 5) & 1, code_value >> 6
        lane = lax.broadcasted_iota(jnp.int32, (total_rows, limit), 1)
        owned = jnp.where(by_factor == 1, slot, -1) - (lane >> shift)
        finished = jnp.where(by_factor == 0, spot, -1)[:, :1]
        finished_chip = (slot >> 1)[:, :1]

        def weights(low, count):
            target = finished - low
            target = jnp.where((target >= 0) & (target < count), finished_chip * count + target, -1)
            wide = lax.broadcasted_iota(jnp.int32, (total_rows, chips * count), 1)
            total = jnp.where(wide == target, 1.0, 0.0)
            line = lax.broadcasted_iota(jnp.int32, (limit, chips * count), 0)
            place = lax.broadcasted_iota(jnp.int32, (limit, chips * count), 1)
            for q in range(chips):
                goal = jnp.where(
                    line < rank_width, line, line - rank_width + begin_ref[2 * q + 1]
                ) - low
                moved = (goal >= 0) & (goal < count) & (place == q * count + goal)
                moved = jnp.where(moved, 1.0, 0.0).astype(jnp.bfloat16)
                part = jnp.where(owned == 2 * q, both, 0.0).astype(jnp.bfloat16)
                total = total + jnp.dot(part, moved, preferred_element_type=jnp.float32)
            return total.astype(jnp.bfloat16)

        near = weights(0, first)
        get_near.wait()
        get_base.wait()

        def write(far):
            @pl.loop(0, width // tile)
            def _(i):
                columns = pl.ds(pl.multiple_of(i * tile, tile), tile)
                block = near_rows[:, :, columns].reshape(chips * first, tile)
                total = jnp.dot(near, block, preferred_element_type=jnp.float32)
                total += base_part[:, columns]
                if far is not None:
                    block = late[:, :, columns].reshape(chips * second, tile)
                    total += jnp.dot(far, block, preferred_element_type=jnp.float32)
                out_ref[:, columns] = total.astype(out_ref.dtype)

        @pl.when(more_ref[0] > first)
        def _():
            fetch.start()
            far = weights(first, second)
            fetch.wait()
            write(far)

        @pl.when(more_ref[0] <= first)
        def _():
            write(None)

    smem, whole = pl.BlockSpec(memory_space=pltpu.SMEM), pl.BlockSpec(memory_space=pltpu.VMEM)
    return pl.pallas_call(
        kernel,
        in_specs=[smem] * 2
        + [pl.BlockSpec(memory_space=pl.ANY)]
        + [whole] * 2
        + [pl.BlockSpec(memory_space=pl.ANY)] * 2,
        out_specs=whole,
        out_shape=jax.ShapeDtypeStruct((total_rows, width), jnp.bfloat16),
        scratch_shapes=[
            pltpu.VMEM(extra.shape, extra.dtype),
            pltpu.VMEM(base.shape, base.dtype),
            pltpu.VMEM(incoming.shape, incoming.dtype),
            pltpu.SemaphoreType.DMA((3,)),
        ],
        compiler_params=pltpu.CompilerParams(vmem_limit_bytes=WIDE_GRANT),
        cost_estimate=pl.CostEstimate(
            flops=4 * total_rows * chips * limit * width,
            bytes_accessed=6 * total_rows * width + 2 * chips * limit * width,
            transcendentals=0,
        ),
    )(begin, more, base, code, coeff, incoming, extra)


def ring_gather(block, shards, halfway):
    chips = shards // 2
    depth = chips // 2
    cycle = list(range(0, chips, 2)) + list(range(chips - 1, 0, -2))
    ahead = [
        (2 * cycle[p] + c, 2 * cycle[(p + 1) % chips] + c) for p in range(chips) for c in range(2)
    ]
    back = [(b, a) for a, b in ahead]
    held = {0: block}
    for step in range(1, depth + 1):
        held[-step] = lax.ppermute(held[1 - step], "tensor", ahead)
        if step < chips - depth:
            held[step] = lax.ppermute(held[step - 1], "tensor", back)
        held[-step] = halfway(step, held[-step])
    table = np.zeros((shards, shards), np.int32)
    for t in range(shards):
        for i, offset in enumerate(held):
            chip = cycle[(cycle.index(t // 2) + offset) % chips]
            table[t, 2 * i], table[t, 2 * i + 1] = 2 * chip + t % 2, 2 * chip + 1 - t % 2
    places = lax.dynamic_index_in_dim(table, lax.axis_index("tensor"), keepdims=False)
    return list(held.values()), places


def largest_over_groups(value):
    groups = lax.axis_size("groups")
    for shift in range(1, groups):
        other = lax.ppermute(value, "groups", [(g, (g + shift) % groups) for g in range(groups)])
        value = jnp.maximum(value, other)
    return value


def pooled(
    input_rows,
    up_weight,
    adapter_down,
    adapter_up,
    ranks,
    adapter_slot,
    segment_lengths,
    segment_adapter,
):
    shards = lax.axis_size("tensor")
    position = lax.axis_index("tensor").astype(jnp.int32)
    chips = shards // 2
    total_rows = input_rows.shape[0] * shards
    rank_width = adapter_up.shape[1]
    limit = 2 * rank_width
    sibling = [(t, t ^ 1) for t in range(shards)]
    same_core = [list(range(c, shards, 2)) for c in range(2)]

    core = position & 1
    features = input_rows.shape[1] // 2

    def swap(value):
        keep = lax.dynamic_slice_in_dim(value, core * features, features, 1)
        send = lax.dynamic_slice_in_dim(value, (1 - core) * features, features, 1)
        return keep, lax.ppermute(send, "tensor", sibling)

    mine, other, down_half = split_for_pair(adapter_up[0], adapter_down[0], core[None], chips)
    block = jnp.concatenate(swap(input_rows), axis=0)
    block, mine, other, down_half = lax.optimization_barrier((block, mine, other, down_half))
    other = lax.ppermute(other, "tensor", sibling)
    down_half = lax.ppermute(down_half, "tensor", sibling)
    gain, own, choose, live, fixed, code, begin, full = describe(
        ranks, adapter_slot, segment_lengths, segment_adapter, position[None], total_rows, limit
    )
    fullest = largest_over_groups(full)
    pending = [(own, choose), (other, down_half)]

    def halfway(step, piece):
        nonlocal pending
        if step <= len(pending):
            piece, pending[step - 1] = lax.optimization_barrier((piece, pending[step - 1]))
        return piece

    blocks, places = ring_gather(block, shards, halfway)
    (own, choose), (other, down_half) = pending
    rows, shrink = collect_rows(blocks, places, core[None], adapter_down[0], down_half, own)
    shrink = shrink + lax.ppermute(shrink, "tensor", sibling)
    coeff = (shrink * gain).astype(jnp.bfloat16)
    coeff, rows, fullest = lax.optimization_barrier((coeff, rows, fullest))

    def payload(low, count):
        return build_payload(choose, live, fixed, coeff, mine, other, low, count)

    def exchange(value):
        return lax.all_to_all(
            value,
            "tensor",
            split_axis=0,
            concat_axis=0,
            axis_index_groups=same_core,
            tiled=True,
        )

    near = payload(0, FIRST_ROWS)
    rows_other = lax.ppermute(rows, "tensor", sibling)
    every, bit = coeff, 2
    while bit < shards:
        every = every + lax.ppermute(every, "tensor", [(t, t ^ bit) for t in range(shards)])
        if bit == 2:
            every, near = lax.optimization_barrier((every, near))
        bit *= 2
    near, every, rows, rows_other = lax.optimization_barrier((near, every, rows, rows_other))
    incoming = exchange(near)
    halves = [jnp.where(core == c, rows, rows_other) for c in range(2)]
    base = jnp.dot(
        jnp.concatenate(halves, axis=1), up_weight, preferred_element_type=jnp.float32
    )
    choose, base = lax.optimization_barrier((choose, base))
    rest = limit - FIRST_ROWS
    far = payload(FIRST_ROWS, rest)
    fullest, base, incoming, far = lax.optimization_barrier((fullest, base, incoming, far))

    def later(count):
        def run():
            value = far
            if count:
                late = exchange(far[:, :count])
                value = jnp.concatenate([late, far[:, count:]], axis=1)
            return value

        return run

    sizes = (0,) + tuple(size for size in MORE_ROWS if size < rest) + (rest,)
    which = sum((fullest[0] > FIRST_ROWS + size).astype(jnp.int32) for size in sizes[:-1])
    extra = lax.switch(which, [later(size) for size in sizes])
    return combine(base, code, begin, fullest, every, incoming, extra)


def gathered(input_rows, up_weight, adapter_down, adapter_up, slot_row, row_rank):
    shards = lax.axis_size("tensor")
    position = lax.axis_index("tensor")
    total_rows = input_rows.shape[0] * shards
    stored, rank_width, hidden = adapter_up.shape
    width = hidden // shards
    slots = shards * stored
    outgoing = jnp.stack(
        [adapter_up[:, :, i * width : (i + 1) * width] for i in range(shards)], axis=0
    )
    incoming = lax.all_to_all(outgoing, "tensor", split_axis=0, concat_axis=0, tiled=True)
    rows = lax.all_gather(input_rows, "tensor", axis=0, tiled=True)
    shrink = jnp.einsum("gf,ojf->ogj", rows, adapter_down, preferred_element_type=jnp.float32)
    own = position * stored + jnp.arange(stored, dtype=jnp.int32)
    inside = jnp.arange(rank_width, dtype=jnp.int32)[None, :] < row_rank[:, None]
    keep = (slot_row[None, :] == own[:, None])[:, :, None] & inside[None]
    scale = ADAPTER_ALPHA / row_rank.astype(jnp.float32)
    own_coeff = jnp.where(keep, shrink * scale[None, :, None], 0.0).astype(jnp.bfloat16)
    base = jnp.dot(rows, up_weight, preferred_element_type=jnp.float32)
    own_coeff, base = lax.optimization_barrier((own_coeff, base))
    coeff = lax.all_gather(own_coeff, "tensor", axis=0, tiled=True)
    placed = coeff.transpose(1, 0, 2).reshape(total_rows, slots * rank_width)
    factors = incoming.reshape(slots * rank_width, width)
    term = jnp.dot(placed, factors, preferred_element_type=jnp.float32)
    return (base + term).astype(jnp.bfloat16)


def on_device(
    input_rows,
    up_weight,
    adapter_down,
    adapter_up,
    ranks,
    adapter_slot,
    segment_lengths,
    segment_adapter,
):
    shards = lax.axis_size("tensor")
    stored, rank_width, _ = adapter_up.shape
    tiled = up_weight.shape[1] % 128 == 0 and input_rows.shape[0] % 16 == 0 and rank_width == 64
    tiled = tiled and input_rows.shape[1] % 256 == 0 and input_rows.shape[0] * shards <= 256
    if shards == POOLED_SHARDS and stored == 1 and tiled:
        return pooled(
            input_rows,
            up_weight,
            adapter_down,
            adapter_up,
            ranks,
            adapter_slot,
            segment_lengths,
            segment_adapter,
        )
    slot_row, row_rank = row_tables(
        input_rows.shape[0] * shards, ranks, adapter_slot, segment_lengths, segment_adapter
    )
    return gathered(input_rows, up_weight, adapter_down, adapter_up, slot_row, row_rank)


def solution(mesh):
    placed = (
        P(("groups", "tensor"), None),
        P(None, "tensor"),
        P(("groups", "tensor"), None, None),
        P(("groups", "tensor"), None, None),
        P("groups"),
        P("groups"),
        P("groups"),
        P("groups"),
    )
    return jax.shard_map(
        on_device, mesh=mesh, in_specs=placed, out_specs=P("groups", "tensor"), check_vma=False
    )
```

```python
import jax
import jax.numpy as jnp
import numpy as np
from jax import lax
from jax.experimental import pallas as pl
from jax.experimental.pallas import tpu as pltpu
from jax.sharding import PartitionSpec as P

ADAPTER_ALPHA = 32.0
POOLED_SHARDS = 16
FIRST_ROWS = 64
MORE_ROWS = (16, 32)
WIDE_GRANT = 56 << 20


def row_tables(row_count, ranks, adapter_slot, segment_lengths, segment_adapter):
    seg_ends = jnp.cumsum(segment_lengths)
    positions = jnp.arange(row_count, dtype=jnp.int32)
    seg_row = jnp.sum((seg_ends[None, :] <= positions[:, None]).astype(jnp.int32), axis=1)
    seg_pick = (
        seg_row[:, None] == jnp.arange(segment_lengths.shape[0], dtype=jnp.int32)[None, :]
    ).astype(jnp.int32)
    adapter_row = jnp.sum(seg_pick * segment_adapter[None, :], axis=1)
    pool_pick = (
        adapter_row[:, None] == jnp.arange(ranks.shape[0], dtype=jnp.int32)[None, :]
    ).astype(jnp.int32)
    slot_row = jnp.sum(pool_pick * adapter_slot[None, :], axis=1)
    row_rank_values = jnp.sum(pool_pick * ranks[None, :], axis=1)
    return (slot_row, row_rank_values)


def vmem(buffers):
    return pltpu.CompilerParams(vmem_limit_bytes=buffers + (8 << 20))


def split_for_pair(up_factor, down_factor, core, chips):
    rank_width, hidden = up_factor.shape
    width = hidden // (2 * chips)
    features = down_factor.shape[1] // 2

    def kernel(core_ref, source, down, mine, other, half_down, sems):
        core = core_ref[0]
        start = pl.multiple_of((1 - core) * features, features)
        copies = [
            pltpu.make_async_copy(
                down.at[:, pl.ds(start, features)], half_down, sems.at[2 * chips]
            )
        ]
        for q in range(chips):
            for i, (target, half) in enumerate(((other, 1 - core), (mine, core))):
                start = pl.multiple_of((2 * q + half) * width, width)
                copies.append(
                    pltpu.make_async_copy(
                        source.at[:, pl.ds(start, width)], target.at[q], sems.at[2 * q + i]
                    )
                )
        for copy in copies:
            copy.start()
        for copy in copies:
            copy.wait()

    block = jax.ShapeDtypeStruct((chips, rank_width, width), up_factor.dtype)
    return pl.pallas_call(
        kernel,
        in_specs=[pl.BlockSpec(memory_space=pltpu.SMEM)]
        + [pl.BlockSpec(memory_space=pltpu.HBM)] * 2,
        out_specs=[pl.BlockSpec(memory_space=pltpu.VMEM)] * 3,
        out_shape=[
            block, block, jax.ShapeDtypeStruct((rank_width, features), down_factor.dtype)
        ],
        scratch_shapes=[pltpu.SemaphoreType.DMA((2 * chips + 1,))],
        compiler_params=pltpu.CompilerParams(vmem_limit_bytes=WIDE_GRANT),
        cost_estimate=pl.CostEstimate(
            flops=0, bytes_accessed=4 * rank_width * hidden, transcendentals=0
        ),
    )(core, up_factor, down_factor)


def describe(ranks, adapter_slot, segment_lengths, segment_adapter, position, total_rows, limit):
    slots, segments = ranks.shape[0], segment_lengths.shape[0]
    rank_width = limit // 2
    shift = rank_width.bit_length() - 1

    def kernel(
        ranks_in, home_in, length_in, adapter_in, position_ref,
        gain_ref, own_ref, choose_ref, live_ref, fixed_ref, code_ref, begin_ref, full_ref,
        rank_of, rows_of, used, factor, order, ranks_ref, home_ref, length_ref, adapter_ref, sems,
    ):
        pairs = zip(
            (ranks_in, home_in, length_in, adapter_in),
            (ranks_ref, home_ref, length_ref, adapter_ref),
        )
        copies = [
            pltpu.make_async_copy(source, target, sems.at[i])
            for i, (source, target) in enumerate(pairs)
        ]
        for copy in copies:
            copy.start()
        for copy in copies:
            copy.wait()
        for a in range(slots):
            rows_of[a] = 0
            rank_of[home_ref[a]] = ranks_ref[a]
        starts, start = [], jnp.int32(0)
        for i in range(segments):
            slot = home_ref[adapter_ref[i]]
            starts.append((start, start + length_ref[i], slot))
            order[i] = rows_of[slot] - start
            rows_of[slot] = rows_of[slot] + length_ref[i]
            start = start + length_ref[i]
        full = jnp.int32(0)
        for s in range(slots):
            used[s] = jnp.minimum(rows_of[s], rank_of[s])
            factor[s] = (rank_of[s] < rows_of[s]).astype(jnp.int32)
            begin_ref[s] = used[s - 1] if s % 2 else jnp.int32(0)
            if s % 2:
                full = jnp.maximum(full, used[s - 1] + used[s])
        full_ref[0] = full

        def tables(row):
            spot, code = jnp.zeros_like(row), jnp.zeros_like(row)
            for i, (low, high, slot) in enumerate(starts):
                hit = (row >= low) & (row < high)
                spot = jnp.where(hit, row + (order[i] + begin_ref[slot]), spot)
                code = jnp.where(hit, slot + 32 * factor[slot] + 64 * rank_of[slot], code)
            return spot, code & 31, (code >> 5) & 1, code >> 6

        here = position_ref[0]
        spot, slot, by_factor, _ = tables(lax.broadcasted_iota(jnp.int32, (total_rows, limit), 0))
        code_ref[...] = slot + 32 * by_factor + 64 * spot

        lane = lax.broadcasted_iota(jnp.int32, (total_rows // 2, limit), 1)
        row = lax.broadcasted_iota(jnp.int32, (total_rows // 2, limit), 0)
        _, slot, _, rank = tables(row + (lane >> shift) * (total_rows // 2))
        own_ref[...] = jnp.where(slot == here, 1.0, 0.0)
        scale = ADAPTER_ALPHA / rank.astype(jnp.float32)
        inside = ((slot >> 1) == (here >> 1)) & ((lane & (rank_width - 1)) < rank)
        gain_ref[...] = jnp.where(inside, scale, 0.0)

        spot, slot, by_factor, _ = tables(lax.broadcasted_iota(jnp.int32, (8, total_rows), 1))
        mine = ((slot >> 1) == (here >> 1)) & (by_factor == 0)
        spot = jnp.broadcast_to(jnp.where(mine, spot, -1)[:1], (limit, total_rows))
        line = lax.broadcasted_iota(jnp.int32, (limit, total_rows), 0)
        choose_ref[...] = jnp.where(line == spot, 1.0, 0.0).astype(jnp.bfloat16)

        line = lax.broadcasted_iota(jnp.int32, (limit, limit), 0)
        lane = lax.broadcasted_iota(jnp.int32, (limit, limit), 1)
        half, column = lane >> shift, lane & (rank_width - 1)
        other = here ^ 1
        begin = jnp.where(half == 0, begin_ref[here], begin_ref[other])
        many = jnp.where(half == 0, used[here], used[other])
        kind = jnp.where(half == 0, factor[here], factor[other])
        held = (line == begin + column) & (column < many) & (kind == 1)
        fixed_ref[...] = jnp.where(held, 1.0, 0.0).astype(jnp.bfloat16)
        live = (line >= begin) & (line < begin + many) & (kind == 0)
        live_ref[...] = jnp.where(live, 1.0, 0.0)

    smem, whole = pl.BlockSpec(memory_space=pltpu.SMEM), pl.BlockSpec(memory_space=pltpu.VMEM)
    return pl.pallas_call(
        kernel,
        in_specs=[pl.BlockSpec(memory_space=pltpu.HBM)] * 4 + [smem],
        out_specs=[whole] * 6 + [smem] * 2,
        out_shape=[
            jax.ShapeDtypeStruct((total_rows // 2, limit), jnp.float32),
            jax.ShapeDtypeStruct((total_rows // 2, limit), jnp.float32),
            jax.ShapeDtypeStruct((limit, total_rows), jnp.bfloat16),
            jax.ShapeDtypeStruct((limit, limit), jnp.float32),
            jax.ShapeDtypeStruct((limit, limit), jnp.bfloat16),
            jax.ShapeDtypeStruct((total_rows, limit), jnp.int32),
            jax.ShapeDtypeStruct((slots,), jnp.int32),
            jax.ShapeDtypeStruct((1,), jnp.int32),
        ],
        scratch_shapes=[pltpu.SMEM((slots,), jnp.int32)] * 4
        + [pltpu.SMEM((segments,), jnp.int32)]
        + [pltpu.SMEM((slots,), jnp.int32)] * 2
        + [pltpu.SMEM((segments,), jnp.int32)] * 2
        + [pltpu.SemaphoreType.DMA((4,))],
        compiler_params=vmem(16 * total_rows * limit),
        cost_estimate=pl.CostEstimate(
            flops=200 * total_rows * limit, bytes_accessed=16 * total_rows * limit, transcendentals=0
        ),
    )(ranks, adapter_slot, segment_lengths, segment_adapter, position)


def collect_rows(blocks, places, core, own_down, other_down, own):
    count = len(blocks)
    height, features = blocks[0].shape
    height = height // 2
    rank_width = other_down.shape[0]
    half_rows = own.shape[0]
    chunk = 2048 if features % 2048 == 0 else features
    chunks = features // chunk

    def kernel(places_ref, core_ref, own_ref, *refs):
        sources, own_down_ref, other_down_ref = refs[:count], refs[count], refs[count + 1]
        rows_ref, shrink_ref, downs, sems = refs[count + 2 :]
        groups = []
        for k in range(chunks):
            columns = pl.ds(k * chunk, chunk)
            offset = pl.multiple_of(core_ref[0] * features + k * chunk, chunk)
            copies = [
                pltpu.make_async_copy(
                    own_down_ref.at[:, pl.ds(offset, chunk)],
                    downs.at[pl.ds(0, rank_width), columns],
                    sems.at[k, 2 * count],
                ),
                pltpu.make_async_copy(
                    other_down_ref.at[:, columns],
                    downs.at[pl.ds(rank_width, rank_width), columns],
                    sems.at[k, 2 * count + 1],
                ),
            ]
            for i in range(2 * count):
                start = pl.multiple_of(places_ref[i] * height, height)
                copies.append(
                    pltpu.make_async_copy(
                        sources[i // 2].at[pl.ds(i % 2 * height, height), columns],
                        rows_ref.at[pl.ds(start, height), columns],
                        sems.at[k, i],
                    )
                )
            groups.append(copies)
            for copy in copies:
                copy.start()
        shrink = jnp.zeros((2 * half_rows, 2 * rank_width), jnp.float32)
        for k in range(chunks):
            for copy in groups[k]:
                copy.wait()
            columns = pl.ds(k * chunk, chunk)
            shrink = shrink + lax.dot_general(
                rows_ref[:, columns],
                downs[:, columns],
                (((1,), (1,)), ((), ())),
                preferred_element_type=jnp.float32,
            )
        top, bottom = shrink[:half_rows], shrink[half_rows:]
        first = jnp.concatenate([top[:, :rank_width], bottom[:, :rank_width]], axis=1)
        second = jnp.concatenate([top[:, rank_width:], bottom[:, rank_width:]], axis=1)
        shrink_ref[...] = jnp.where(own_ref[...] > 0.5, first, second)

    smem, whole = pl.BlockSpec(memory_space=pltpu.SMEM), pl.BlockSpec(memory_space=pltpu.VMEM)
    rows = 2 * count * height
    return pl.pallas_call(
        kernel,
        in_specs=[smem, smem, whole] + [pl.BlockSpec(memory_space=pl.ANY)] * (count + 2),
        out_specs=[whole] * 2,
        out_shape=[
            jax.ShapeDtypeStruct((rows, features), blocks[0].dtype),
            jax.ShapeDtypeStruct(own.shape, jnp.float32),
        ],
        scratch_shapes=[
            pltpu.VMEM((2 * rank_width, features), own_down.dtype),
            pltpu.SemaphoreType.DMA((chunks, 2 * count + 2)),
        ],
        compiler_params=pltpu.CompilerParams(vmem_limit_bytes=WIDE_GRANT),
        cost_estimate=pl.CostEstimate(
            flops=4 * rows * features * rank_width,
            bytes_accessed=4 * rows * features,
            transcendentals=0,
        ),
    )(places, core, own, *blocks, own_down, other_down)


def build_payload(choose, live, fixed, coeff, mine, other, first, count):
    chips, rank_width, width = mine.shape

    half_rows = coeff.shape[0]

    def kernel(choose_ref, live_ref, fixed_ref, coeff_ref, mine_ref, other_ref, out_ref):
        lines = pl.ds(first, count)
        folded = coeff_ref[...]
        top = jnp.dot(choose_ref[lines, :half_rows], folded, preferred_element_type=jnp.float32)
        low = jnp.dot(choose_ref[lines, half_rows:], folded, preferred_element_type=jnp.float32)
        chosen = top[:, :rank_width] + low[:, rank_width:]
        select = jnp.concatenate([chosen, chosen], axis=1) * live_ref[lines]
        select = (select + fixed_ref[lines].astype(jnp.float32)).astype(jnp.bfloat16)

        @pl.loop(0, chips)
        def _(q):
            out_ref[q] = jnp.dot(
                select,
                jnp.concatenate([mine_ref[q], other_ref[q]], axis=0),
                preferred_element_type=jnp.float32,
            ).astype(out_ref.dtype)

    return pl.pallas_call(
        kernel,
        in_specs=[pl.BlockSpec(memory_space=pltpu.VMEM)] * 6,
        out_specs=pl.BlockSpec(memory_space=pltpu.VMEM),
        out_shape=jax.ShapeDtypeStruct((chips, count, width), mine.dtype),
        compiler_params=vmem(4 * chips * width * (2 * rank_width + count)),
        cost_estimate=pl.CostEstimate(
            flops=4 * chips * count * rank_width * width,
            bytes_accessed=2 * chips * width * (2 * rank_width + count),
            transcendentals=0,
        ),
    )(choose, live, fixed, coeff, mine, other)


def combine(base, code, begin, more, coeff, incoming, extra):
    total_rows, width = base.shape
    chips, first, _ = incoming.shape
    second = extra.shape[1]
    limit = first + second
    rank_width = limit // 2
    shift = rank_width.bit_length() - 1
    tile = 256 if width % 256 == 0 else 128

    def kernel(
        begin_ref, more_ref, base_ref, code_ref, coeff_ref, incoming_ref, extra_ref,
        out_ref, late, base_part, near_rows, sems,
    ):
        fetch = pltpu.make_async_copy(extra_ref, late, sems.at[0])
        get_base = pltpu.make_async_copy(base_ref, base_part, sems.at[1])
        get_near = pltpu.make_async_copy(incoming_ref, near_rows, sems.at[2])
        get_near.start()
        get_base.start()
        folded = coeff_ref[...].astype(jnp.float32)
        both = jnp.concatenate(
            [
                jnp.concatenate([part, part], axis=1)
                for part in (folded[:, :rank_width], folded[:, rank_width:])
            ],
            axis=0,
        )
        code_value = code_ref[...]
        slot, by_factor, spot = code_value & 31, (code_value >> 5) & 1, code_value >> 6
        lane = lax.broadcasted_iota(jnp.int32, (total_rows, limit), 1)
        owned = jnp.where(by_factor == 1, slot, -1) - (lane >> shift)
        finished = jnp.where(by_factor == 0, spot, -1)[:, :1]
        finished_chip = (slot >> 1)[:, :1]

        def weights(low, count):
            target = finished - low
            target = jnp.where((target >= 0) & (target < count), finished_chip * count + target, -1)
            wide = lax.broadcasted_iota(jnp.int32, (total_rows, chips * count), 1)
            total = jnp.where(wide == target, 1.0, 0.0)
            line = lax.broadcasted_iota(jnp.int32, (limit, chips * count), 0)
            place = lax.broadcasted_iota(jnp.int32, (limit, chips * count), 1)
            for q in range(chips):
                goal = jnp.where(
                    line < rank_width, line, line - rank_width + begin_ref[2 * q + 1]
                ) - low
                moved = (goal >= 0) & (goal < count) & (place == q * count + goal)
                moved = jnp.where(moved, 1.0, 0.0).astype(jnp.bfloat16)
                part = jnp.where(owned == 2 * q, both, 0.0).astype(jnp.bfloat16)
                total = total + jnp.dot(part, moved, preferred_element_type=jnp.float32)
            return total.astype(jnp.bfloat16)

        near = weights(0, first)
        get_near.wait()
        get_base.wait()

        def write(far):
            @pl.loop(0, width // tile)
            def _(i):
                columns = pl.ds(pl.multiple_of(i * tile, tile), tile)
                block = near_rows[:, :, columns].reshape(chips * first, tile)
                total = jnp.dot(near, block, preferred_element_type=jnp.float32)
                total += base_part[:, columns]
                if far is not None:
                    block = late[:, :, columns].reshape(chips * second, tile)
                    total += jnp.dot(far, block, preferred_element_type=jnp.float32)
                out_ref[:, columns] = total.astype(out_ref.dtype)

        @pl.when(more_ref[0] > first)
        def _():
            fetch.start()
            far = weights(first, second)
            fetch.wait()
            write(far)

        @pl.when(more_ref[0] <= first)
        def _():
            write(None)

    smem, whole = pl.BlockSpec(memory_space=pltpu.SMEM), pl.BlockSpec(memory_space=pltpu.VMEM)
    return pl.pallas_call(
        kernel,
        in_specs=[smem] * 2
        + [pl.BlockSpec(memory_space=pl.ANY)]
        + [whole] * 2
        + [pl.BlockSpec(memory_space=pl.ANY)] * 2,
        out_specs=whole,
        out_shape=jax.ShapeDtypeStruct((total_rows, width), jnp.bfloat16),
        scratch_shapes=[
            pltpu.VMEM(extra.shape, extra.dtype),
            pltpu.VMEM(base.shape, base.dtype),
            pltpu.VMEM(incoming.shape, incoming.dtype),
            pltpu.SemaphoreType.DMA((3,)),
        ],
        compiler_params=pltpu.CompilerParams(vmem_limit_bytes=WIDE_GRANT),
        cost_estimate=pl.CostEstimate(
            flops=4 * total_rows * chips * limit * width,
            bytes_accessed=6 * total_rows * width + 2 * chips * limit * width,
            transcendentals=0,
        ),
    )(begin, more, base, code, coeff, incoming, extra)


def ring_gather(block, shards, halfway):
    chips = shards // 2
    depth = chips // 2
    cycle = list(range(0, chips, 2)) + list(range(chips - 1, 0, -2))
    ahead = [
        (2 * cycle[p] + c, 2 * cycle[(p + 1) % chips] + c) for p in range(chips) for c in range(2)
    ]
    back = [(b, a) for a, b in ahead]
    held = {0: block}
    for step in range(1, depth + 1):
        held[-step] = lax.ppermute(held[1 - step], "tensor", ahead)
        if step < chips - depth:
            held[step] = lax.ppermute(held[step - 1], "tensor", back)
        held[-step] = halfway(step, held[-step])
    table = np.zeros((shards, shards), np.int32)
    for t in range(shards):
        for i, offset in enumerate(held):
            chip = cycle[(cycle.index(t // 2) + offset) % chips]
            table[t, 2 * i], table[t, 2 * i + 1] = 2 * chip + t % 2, 2 * chip + 1 - t % 2
    places = lax.dynamic_index_in_dim(table, lax.axis_index("tensor"), keepdims=False)
    return list(held.values()), places


def largest_over_groups(value):
    groups = lax.axis_size("groups")
    for shift in range(1, groups):
        other = lax.ppermute(value, "groups", [(g, (g + shift) % groups) for g in range(groups)])
        value = jnp.maximum(value, other)
    return value


def pooled(
    input_rows,
    up_weight,
    adapter_down,
    adapter_up,
    ranks,
    adapter_slot,
    segment_lengths,
    segment_adapter,
):
    shards = lax.axis_size("tensor")
    position = lax.axis_index("tensor").astype(jnp.int32)
    chips = shards // 2
    total_rows = input_rows.shape[0] * shards
    rank_width = adapter_up.shape[1]
    limit = 2 * rank_width
    sibling = [(t, t ^ 1) for t in range(shards)]
    same_core = [list(range(c, shards, 2)) for c in range(2)]

    core = position & 1
    features = input_rows.shape[1] // 2

    def swap(value):
        keep = lax.dynamic_slice_in_dim(value, core * features, features, 1)
        send = lax.dynamic_slice_in_dim(value, (1 - core) * features, features, 1)
        return keep, lax.ppermute(send, "tensor", sibling)

    mine, other, down_half = split_for_pair(adapter_up[0], adapter_down[0], core[None], chips)
    block = jnp.concatenate(swap(input_rows), axis=0)
    block, mine, other, down_half = lax.optimization_barrier((block, mine, other, down_half))
    other = lax.ppermute(other, "tensor", sibling)
    down_half = lax.ppermute(down_half, "tensor", sibling)
    gain, own, choose, live, fixed, code, begin, full = describe(
        ranks, adapter_slot, segment_lengths, segment_adapter, position[None], total_rows, limit
    )
    fullest = largest_over_groups(full)
    pending = [(own, choose), (other, down_half)]

    def halfway(step, piece):
        nonlocal pending
        if step <= len(pending):
            piece, pending[step - 1] = lax.optimization_barrier((piece, pending[step - 1]))
        return piece

    blocks, places = ring_gather(block, shards, halfway)
    (own, choose), (other, down_half) = pending
    rows, shrink = collect_rows(blocks, places, core[None], adapter_down[0], down_half, own)
    shrink = shrink + lax.ppermute(shrink, "tensor", sibling)
    coeff = (shrink * gain).astype(jnp.bfloat16)
    coeff, rows, fullest = lax.optimization_barrier((coeff, rows, fullest))

    def payload(low, count):
        return build_payload(choose, live, fixed, coeff, mine, other, low, count)

    def exchange(value):
        return lax.all_to_all(
            value,
            "tensor",
            split_axis=0,
            concat_axis=0,
            axis_index_groups=same_core,
            tiled=True,
        )

    near = payload(0, FIRST_ROWS)
    rows_other = lax.ppermute(rows, "tensor", sibling)
    every, bit = coeff, 2
    while bit < shards:
        every = every + lax.ppermute(every, "tensor", [(t, t ^ bit) for t in range(shards)])
        if bit == 2:
            every, near = lax.optimization_barrier((every, near))
        bit *= 2
    near, every, rows, rows_other = lax.optimization_barrier((near, every, rows, rows_other))
    incoming = exchange(near)
    halves = [jnp.where(core == c, rows, rows_other) for c in range(2)]
    base = jnp.dot(
        jnp.concatenate(halves, axis=1), up_weight, preferred_element_type=jnp.float32
    )
    choose, base = lax.optimization_barrier((choose, base))
    rest = limit - FIRST_ROWS
    far = payload(FIRST_ROWS, rest)
    fullest, base, incoming, far = lax.optimization_barrier((fullest, base, incoming, far))

    def later(count):
        def run():
            value = jnp.zeros((chips, rest - count, up_weight.shape[1]), adapter_up.dtype)
            if count:
                late = exchange(far[:, :count])
                value = jnp.concatenate([late, value], axis=1)
            return value

        return run

    sizes = (0,) + tuple(size for size in MORE_ROWS if size < rest) + (rest,)
    which = sum((fullest[0] > FIRST_ROWS + size).astype(jnp.int32) for size in sizes[:-1])
    extra = lax.switch(which, [later(size) for size in sizes])
    return combine(base, code, begin, fullest, every, incoming, extra)


def gathered(input_rows, up_weight, adapter_down, adapter_up, slot_row, row_rank):
    shards = lax.axis_size("tensor")
    position = lax.axis_index("tensor")
    total_rows = input_rows.shape[0] * shards
    stored, rank_width, hidden = adapter_up.shape
    width = hidden // shards
    slots = shards * stored
    outgoing = jnp.stack(
        [adapter_up[:, :, i * width : (i + 1) * width] for i in range(shards)], axis=0
    )
    incoming = lax.all_to_all(outgoing, "tensor", split_axis=0, concat_axis=0, tiled=True)
    rows = lax.all_gather(input_rows, "tensor", axis=0, tiled=True)
    shrink = jnp.einsum("gf,ojf->ogj", rows, adapter_down, preferred_element_type=jnp.float32)
    own = position * stored + jnp.arange(stored, dtype=jnp.int32)
    inside = jnp.arange(rank_width, dtype=jnp.int32)[None, :] < row_rank[:, None]
    keep = (slot_row[None, :] == own[:, None])[:, :, None] & inside[None]
    scale = ADAPTER_ALPHA / row_rank.astype(jnp.float32)
    own_coeff = jnp.where(keep, shrink * scale[None, :, None], 0.0).astype(jnp.bfloat16)
    base = jnp.dot(rows, up_weight, preferred_element_type=jnp.float32)
    own_coeff, base = lax.optimization_barrier((own_coeff, base))
    coeff = lax.all_gather(own_coeff, "tensor", axis=0, tiled=True)
    placed = coeff.transpose(1, 0, 2).reshape(total_rows, slots * rank_width)
    factors = incoming.reshape(slots * rank_width, width)
    term = jnp.dot(placed, factors, preferred_element_type=jnp.float32)
    return (base + term).astype(jnp.bfloat16)


def on_device(
    input_rows,
    up_weight,
    adapter_down,
    adapter_up,
    ranks,
    adapter_slot,
    segment_lengths,
    segment_adapter,
):
    shards = lax.axis_size("tensor")
    stored, rank_width, _ = adapter_up.shape
    tiled = up_weight.shape[1] % 128 == 0 and input_rows.shape[0] % 16 == 0 and rank_width == 64
    tiled = tiled and input_rows.shape[1] % 256 == 0 and input_rows.shape[0] * shards <= 256
    if shards == POOLED_SHARDS and stored == 1 and tiled:
        return pooled(
            input_rows,
            up_weight,
            adapter_down,
            adapter_up,
            ranks,
            adapter_slot,
            segment_lengths,
            segment_adapter,
        )
    slot_row, row_rank = row_tables(
        input_rows.shape[0] * shards, ranks, adapter_slot, segment_lengths, segment_adapter
    )
    return gathered(input_rows, up_weight, adapter_down, adapter_up, slot_row, row_rank)


def solution(mesh):
    placed = (
        P(("groups", "tensor"), None),
        P(None, "tensor"),
        P(("groups", "tensor"), None, None),
        P(("groups", "tensor"), None, None),
        P("groups"),
        P("groups"),
        P("groups"),
        P("groups"),
    )
    return jax.shard_map(
        on_device, mesh=mesh, in_specs=placed, out_specs=P("groups", "tensor"), check_vma=False
    )
```
